32 devices in a mesh: gx: 8 (over z, y), gz: 4 (over x, core).
Axes of the slice: x: 2, y: 2, z: 4, core: 2. Of those that a mesh axis runs over, the one named last changes fastest.
Arguments:
- populations: float32 [19, 32, 64, 128], P(None, 'gx', 'gz'), may hold values from 0.019 to 0.44, as said below
- fluid_mask: int32 [32, 64, 128], P('gx', 'gz'), may hold values 0 or 1
Outputs:
- spectrum: float32 [2, 128, 32, 64], P(None, 'gx', 'gz')
The draws below stay inside these ranges and needn't reach their ends.
Inputs may be any that keep to these rules, and one draw needn't show every extreme that they name: `populations`: each entry lies between 0.7 and 1.3 times the weight of its velocity.
All inputs are finite; a program needn't handle non-finite values. No bound on the sum of `fluid_mask` on one device may be relied on, other than what follows from the above.
Results may differ from the reference program's by a relative error of at most 0.0003.
Values sent between devices are 32-bit elements; how exact they have to be, the bound alone decides.
A program may use at most 64 MiB of HBM per device.

```python
import math
import jax
import jax.numpy as jnp
from jax import lax

NY = 128
NX = 32
NZ = 64


LATTICE_WEIGHTS = (1.0 / 3.0,) + (1.0 / 18.0,) * 6 + (1.0 / 36.0,) * 12


def draw_populations(key, part):
    weights = jnp.asarray(LATTICE_WEIGHTS, jnp.float32).reshape(19, 1, 1, 1)
    shape = (19, NX, NZ, NY)
    noise = jnp.clip(jax.random.normal(key, shape, jnp.float32), -3.0, 3.0)
    factor = 1.0 + 0.1 * noise
    return weights * factor


def plant(entries, stream_key, least, top_value):
    place = [jax.random.randint(jax.random.fold_in(stream_key, axis), (), 0, length) for axis, length in enumerate(entries.shape)]
    widest = entries.shape.index(max(entries.shape))
    neighbour = place[:widest] + [(place[widest] + 1) % entries.shape[widest]] + place[widest + 1:]
    return entries.at[tuple(place)].set(least).at[tuple(neighbour)].set(top_value)


def setup_inputs(seed: int = 0) -> dict:
    splits = jax.random.split(jax.random.key(seed), 3)
    populations = draw_populations(jax.random.fold_in(splits[2], 71), 0)
    fluid_mask = plant((jax.random.randint(splits[1], (NX, NZ, NY), 0, 5) < 4).astype(jnp.int32), jax.random.fold_in(splits[1], 1), 0, 1)
    return dict(populations=populations, fluid_mask=fluid_mask)


VELOCITIES = ((0, 0, 0), (1, 0, 0), (-1, 0, 0), (0, 1, 0), (0, -1, 0), (0, 0, 1), (0, 0, -1), (1, 1, 0), (-1, -1, 0), (1, -1, 0), (-1, 1, 0), (1, 0, 1), (-1, 0, -1), (1, 0, -1), (-1, 0, 1), (0, 1, 1), (0, -1, -1), (0, 1, -1), (0, -1, 1))
LATTICE_WEIGHTS = (1.0 / 3.0,) + (1.0 / 18.0,) * 6 + (1.0 / 36.0,) * 12
OPPOSITES = (0, 2, 1, 4, 3, 6, 5, 8, 7, 10, 9, 12, 11, 14, 13, 16, 15, 18, 17)
RELAX_TIME = 0.6
BODY_FORCE = 0.0001
SPEED_UNIT = 0.05

def component(which, float_type):
    return jnp.asarray([velocity[which] for velocity in VELOCITIES], float_type).reshape(19, 1, 1, 1)

def collide(current, fluid_cells):
    float_type = current.dtype
    along_x = component(0, float_type)
    along_y = component(1, float_type)
    along_z = component(2, float_type)
    weights = jnp.asarray(LATTICE_WEIGHTS, float_type).reshape(19, 1, 1, 1)
    density = lax.optimization_barrier(jnp.sum(current, axis=0))
    speed_x = lax.optimization_barrier(jnp.sum(along_x * current, axis=0)) / density
    speed_y = lax.optimization_barrier(jnp.sum(along_y * current, axis=0)) / density
    speed_z = lax.optimization_barrier(jnp.sum(along_z * current, axis=0)) / density
    project = along_x * speed_x + along_y * speed_y + along_z * speed_z
    square = speed_x * speed_x + speed_y * speed_y + speed_z * speed_z
    balance = weights * density * (1.0 + 3.0 * project + 4.5 * project * project - 1.5 * square)
    relaxed = current - (current - balance) / RELAX_TIME + 3.0 * BODY_FORCE * weights * along_x * density
    return jnp.where(fluid_cells > 0, relaxed, current)

def stream(padded):
    extent_x = padded.shape[1] - 2
    extent_z = padded.shape[2] - 2
    height = padded.shape[3]
    walled = jnp.pad(padded, ((0, 0), (0, 0), (0, 0), (1, 1)))
    fluid_self = padded[19, 1:1 + extent_x, 1:1 + extent_z, :]
    results = []
    for number in range(19):
        step_x, step_y, step_z = VELOCITIES[number]
        start_x = 1 - step_x
        start_z = 1 - step_z
        start_y = 1 - step_y
        source_value = walled[number, start_x:start_x + extent_x, start_z:start_z + extent_z, start_y:start_y + height]
        source_fluid = walled[19, start_x:start_x + extent_x, start_z:start_z + extent_z, start_y:start_y + height]
        bounce = padded[OPPOSITES[number], 1:1 + extent_x, 1:1 + extent_z, :]
        own_value = padded[number, 1:1 + extent_x, 1:1 + extent_z, :]
        arrived = jnp.where(source_fluid > 0, source_value, bounce)
        results.append(jnp.where(fluid_self > 0, arrived, own_value))
    return jnp.stack(results, axis=0)

def reference(populations, fluid_mask):
    fluid_cells = fluid_mask.astype(populations.dtype)
    current = populations
    for repeat in range(2):
        relaxed = collide(current, fluid_cells)
        stacked = jnp.concatenate([relaxed, fluid_cells[None]], axis=0)
        padded = jnp.pad(stacked, ((0, 0), (1, 1), (1, 1), (0, 0)), mode='wrap')
        current = stream(padded)
    along_x = component(0, populations.dtype)
    density = lax.optimization_barrier(jnp.sum(current, axis=0))
    speed_x = fluid_cells * lax.optimization_barrier(jnp.sum(along_x * current, axis=0)) / density
    transformed = jnp.fft.fftn(speed_x, axes=(0, 1))
    norm_scale = 1.0 / (math.sqrt(NX * NZ) * SPEED_UNIT)
    stacked_parts = jnp.stack([jnp.real(transformed), jnp.imag(transformed)], axis=0) * norm_scale
    return jnp.transpose(stacked_parts, (0, 3, 1, 2)).astype(populations.dtype)
```

```python
import functools
import math

import jax
import jax.numpy as jnp
import numpy as np
from jax import lax
from jax.experimental import pallas as pl
from jax.experimental.pallas import tpu as pltpu
from jax.sharding import PartitionSpec as P

VELOCITIES = (
    (0, 0, 0),
    (1, 0, 0),
    (-1, 0, 0),
    (0, 1, 0),
    (0, -1, 0),
    (0, 0, 1),
    (0, 0, -1),
    (1, 1, 0),
    (-1, -1, 0),
    (1, -1, 0),
    (-1, 1, 0),
    (1, 0, 1),
    (-1, 0, -1),
    (1, 0, -1),
    (-1, 0, 1),
    (0, 1, 1),
    (0, -1, -1),
    (0, 1, -1),
    (0, -1, 1),
)
LATTICE_WEIGHTS = (1.0 / 3.0,) + (1.0 / 18.0,) * 6 + (1.0 / 36.0,) * 12
OPPOSITES = (0, 2, 1, 4, 3, 6, 5, 8, 7, 10, 9, 12, 11, 14, 13, 16, 15, 18, 17)
RELAX_TIME = 0.6
BODY_FORCE = 0.0001
SPEED_UNIT = 0.05

CHAIN = (13, 1, 7, 9, 11, 5, 15, 18, 14, 2, 8, 10, 12, 6, 16, 17, 0, 3, 4)
SLOT = {number: CHAIN.index(number) for number in CHAIN}
X_FIRST = {1: 0, -1: 8}
Z_FIRST = {1: 4, -1: 12}
SIDES = ((1, 0), (-1, 0), (0, 1), (0, -1))
DIAGONALS = ((1, 1), (1, -1), (-1, 1), (-1, -1))
DIAGONAL_SLOT = (4, 0, 8, 12)
TOP = 8
MESH = pl.DeviceIdType.MESH


def collide(f, fluid):
    omega = 1.0 / RELAX_TIME
    keep = 1.0 - omega
    plus = {}
    minus = {}
    for i in range(1, 19, 2):
        plus[i] = f[i] + f[i + 1]
        minus[i] = f[i] - f[i + 1]
    density = f[0]
    momentum = [None, None, None]
    for i in range(1, 19, 2):
        density = density + plus[i]
        for axis in range(3):
            c = VELOCITIES[i][axis]
            if c:
                term = minus[i] if c > 0 else -minus[i]
                momentum[axis] = term if momentum[axis] is None else momentum[axis] + term
    inverse = 1.0 / density
    jx, jy, jz = momentum
    square = (jx * jx + jy * jy + jz * jz) * inverse
    base = density - 1.5 * square
    force = density * BODY_FORCE
    out = [None] * 19
    w0 = LATTICE_WEIGHTS[0] * omega
    out[0] = jnp.where(fluid, keep * f[0] + w0 * base, f[0])
    for i in range(1, 19, 2):
        w = LATTICE_WEIGHTS[i]
        cj = None
        for axis in range(3):
            c = VELOCITIES[i][axis]
            if c:
                j = momentum[axis]
                if cj is None:
                    cj = j if c > 0 else -j
                else:
                    cj = cj + j if c > 0 else cj - j
        even = (w * omega) * (base + 4.5 * (cj * cj * inverse))
        odd = (3.0 * w * omega) * cj
        if VELOCITIES[i][0]:
            odd = odd + (3.0 * w * VELOCITIES[i][0]) * force
        out[i] = jnp.where(fluid, keep * f[i] + (even + odd), f[i])
        out[i + 1] = jnp.where(fluid, keep * f[i + 1] + (even - odd), f[i + 1])
    return out


def tables(count_x, count_z, extent_x, extent_z, norm):
    lane = np.arange(128)
    step = (lane // extent_z) % extent_x
    k0 = np.arange(8)[:, None]
    angle = 2.0 * np.pi * k0 * step[None, :] / (count_x * extent_x)
    twiddle = np.concatenate([np.cos(angle), np.sin(angle)], axis=0)
    quarter_cos = np.array([1.0, 0.0, -1.0, 0.0])
    quarter_sin = np.array([0.0, 1.0, 0.0, -1.0])
    k1 = np.arange(4)[:, None]
    xl = np.arange(4)[None, :]
    c = quarter_cos[(k1 * xl) % 4]
    s = quarter_sin[(k1 * xl) % 4]
    block = np.zeros((4, 2, 2, 4))
    block[:, 0, 0] = c
    block[:, 0, 1] = s
    block[:, 1, 1] = c
    block[:, 1, 0] = -s
    first = np.einsum("kpqx,zw->kpzqxw", block, np.eye(extent_z)).reshape(128, 128)
    full_z = count_z * extent_z
    z = np.arange(full_z)
    angle = 2.0 * np.pi * ((z[:, None] * z[None, :]) % full_z) / full_z
    c = np.cos(angle) * norm
    s = np.sin(angle) * norm
    second = np.zeros((2, full_z, 2, full_z))
    second[0, :, 0] = c
    second[1, :, 0] = s
    second[1, :, 1] = c
    second[0, :, 1] = -s
    second = second.reshape(2, count_z, extent_z, 2, full_z).transpose(1, 0, 2, 3, 4)
    second = second.reshape(128, 128)
    return np.concatenate([twiddle, first, second], axis=0).astype(np.float32)


def halves(value):
    high = value.astype(jnp.bfloat16)
    low = (value - high.astype(jnp.float32)).astype(jnp.bfloat16)
    return high, low


def eight_point(v):
    r = math.sqrt(0.5)
    a0, a1, a2, a3 = v[0] + v[4], v[1] + v[5], v[2] + v[6], v[3] + v[7]
    b0, b1, b2, b3 = v[0] - v[4], v[1] - v[5], v[2] - v[6], v[3] - v[7]
    e0, e1 = a0 + a2, a1 + a3
    d, t = r * (b1 - b3), r * (b1 + b3)
    re = [e0 + e1, b0 + d, a0 - a2, b0 - d, e0 - e1]
    im = [None, -b2 - t, a3 - a1, b2 - t, None]
    re = re + [re[3], re[2], re[1]]
    im = im + [-im[3], -im[2], -im[1]]
    return re, im


def kernel(spectral, populations, fluid_mask, table, *rest):
    if spectral:
        (out_ref, held, mask_i, rolled, plain, walls, edges_out, edges_in, corners_out, corners_in,
         in_sem, halo_send, halo_recv, mask_send, mask_recv,
         ux, sent_x, got_x, left, sent_z, got_z, weights, table_sem, x_send, x_recv, z_send, z_recv) = rest
    else:
        (out_ref, held, mask_i, rolled, plain, walls, edges_out, edges_in, corners_out, corners_in,
         in_sem, halo_send, halo_recv, mask_send, mask_recv) = rest
    extent_x, extent_z, height = fluid_mask.shape
    count_x, count_z = lax.axis_size("gx"), lax.axis_size("gz")
    mx, mz = lax.axis_index("gx"), lax.axis_index("gz")

    def shifted_x(step):
        return lax.rem(mx + step + count_x, count_x)

    def shifted_z(step):
        return lax.rem(mz + step + count_z, count_z)

    inner = pl.ds(TOP, extent_z)

    mask_copy = pltpu.make_async_copy(fluid_mask, mask_i, in_sem.at[extent_x])
    mask_copy.start()
    fetches = []
    for x in range(extent_x):
        fetch = pltpu.make_async_copy(populations.at[:, x], held.at[x], in_sem.at[x])
        fetch.start()
        fetches.append(fetch)
    if spectral:
        table_copy = pltpu.make_async_copy(table, weights, table_sem.at[0])
        table_copy.start()

    barrier = pltpu.get_barrier_semaphore()
    partners = [(shifted_x(dx), shifted_z(dz)) for dx, dz in SIDES + DIAGONALS]
    if spectral:
        partners += [(shifted_x(p), mz) for p in range(2, count_x - 1)]
        partners += [(mx, shifted_z(p)) for p in range(2, count_z - 1)]
    for partner in partners:
        pl.semaphore_signal(barrier, inc=1, device_id=partner, device_id_type=MESH)

    lanes = lax.broadcasted_iota(jnp.int32, (extent_z, height), 1)

    def store(step, x, g):
        for number in range(19):
            cy = VELOCITIES[number][1]
            value = g[number]
            if cy:
                plain[number, x] = value
                value = pltpu.roll(value, cy % height, 1)
            slot = SLOT[number]
            rolled[step, slot, 1 + x, inner, :] = value
            cz = VELOCITIES[number][2]
            if cz:
                order = (slot - Z_FIRST[cz]) % 16
                row = extent_z - 1 if cz > 0 else 0
                edge = value[row : row + 1, :]
                side = 0 if cz > 0 else 1
                edges_out[step, side, pl.ds(order * extent_x + x, 1), :] = edge
                cx = VELOCITIES[number][0]
                if cx and x == (extent_x - 1 if cx > 0 else 0):
                    diagonal = DIAGONALS.index((cx, cz))
                    corners_out[step, diagonal, pl.ds(0, 1), :] = edge

    mask_copy.wait()
    fluids = []
    for x in range(extent_x):
        fetches[x].wait()
        solid = mask_i[x].astype(jnp.float32)
        walls[0, 1 + x, inner, :] = solid
        for step in range(2):
            for side in range(2):
                row = extent_z - 1 if side == 0 else 0
                edges_out[step, side, pl.ds(5 * extent_x + x, 1), :] = solid[row : row + 1, :]
            for diagonal, (cx, cz) in enumerate(DIAGONALS):
                if x == (extent_x - 1 if cx > 0 else 0):
                    row = extent_z - 1 if cz > 0 else 0
                    corners_out[step, diagonal, pl.ds(1, 1), :] = solid[row : row + 1, :]
        g = collide([held[x, number] for number in range(19)], solid > 0)
        store(0, x, g)

    pl.semaphore_wait(barrier, len(partners))

    def send(step):
        copies = []
        for side, (dx, dz) in enumerate(SIDES):
            if dx:
                here, there = (extent_x, 0) if dx > 0 else (1, extent_x + 1)
                group = pl.ds(X_FIRST[dx], 5)
                source = rolled.at[step, group, here, inner]
                target = rolled.at[step, group, there, inner]
            else:
                which = 0 if dz > 0 else 1
                source = edges_out.at[step, which]
                target = edges_in.at[step, which]
            copies.append((source, target, dx, dz, side))
        for diagonal, (dx, dz) in enumerate(DIAGONALS):
            copies.append((corners_out.at[step, diagonal], corners_in.at[step, diagonal], dx, dz, 4 + diagonal))
        started = []
        if step == 0:
            for side in range(2):
                dx = SIDES[side][0]
                here, there = (extent_x, 0) if dx > 0 else (1, extent_x + 1)
                copy = pltpu.make_async_remote_copy(
                    src_ref=walls.at[0, here, inner],
                    dst_ref=walls.at[0, there, inner],
                    send_sem=mask_send.at[side],
                    recv_sem=mask_recv.at[side],
                    device_id=(shifted_x(dx), mz),
                    device_id_type=MESH,
                )
                copy.start()
                started.append(copy)
        for source, target, dx, dz, number in copies:
            copy = pltpu.make_async_remote_copy(
                src_ref=source,
                dst_ref=target,
                send_sem=halo_send.at[step, number],
                recv_sem=halo_recv.at[step, number],
                device_id=(shifted_x(dx), shifted_z(dz)),
                device_id_type=MESH,
            )
            copy.start()
            started.append(copy)
        return started

    def receive(step, started):
        for copy in started:
            copy.wait_recv()
        for side in range(2):
            row = TOP - 1 if side == 0 else TOP + extent_z
            first = Z_FIRST[1 if side == 0 else -1]
            for x in range(extent_x):
                for order in range(5):
                    rolled[step, (first + order) % 16, 1 + x, pl.ds(row, 1), :] = edges_in[
                        step, side, pl.ds(order * extent_x + x, 1), :
                    ]
                if step == 0:
                    walls[0, 1 + x, pl.ds(row, 1), :] = edges_in[step, side, pl.ds(5 * extent_x + x, 1), :]
        for diagonal, (cx, cz) in enumerate(DIAGONALS):
            plane = 0 if cx > 0 else extent_x + 1
            row = TOP - 1 if cz > 0 else TOP + extent_z
            slot = DIAGONAL_SLOT[diagonal]
            rolled[step, slot, plane, pl.ds(row, 1), :] = corners_in[step, diagonal, pl.ds(0, 1), :]
            if step == 0:
                walls[0, plane, pl.ds(row, 1), :] = corners_in[step, diagonal, pl.ds(1, 1), :]

    def shift_walls():
        around = lax.broadcasted_iota(jnp.int32, (extent_z + 2 * TOP, height), 1)
        for plane in range(extent_x + 2):
            value = walls[0, plane]
            walls[1, plane] = jnp.where(around == 0, 0.0, pltpu.roll(value, 1, 1))
            walls[2, plane] = jnp.where(around == height - 1, 0.0, pltpu.roll(value, height - 1, 1))

    def streamed(step, x):
        fluid = walls[0, 1 + x, inner, :] > 0

        def own(number):
            if VELOCITIES[number][1]:
                return plain[number, x]
            return rolled[step, SLOT[number], 1 + x, inner, :]

        owned = [own(number) for number in range(19)]
        f = [owned[0]]
        for number in range(1, 19):
            cx, cy, cz = VELOCITIES[number]
            slot = SLOT[number]
            rows = pl.ds(TOP - cz, extent_z)
            source_fluid = walls[(0, 1, 2)[cy], 1 + x - cx, rows, :] > 0
            value = rolled[step, slot, 1 + x - cx, rows, :]
            arrived = jnp.where(source_fluid, value, owned[OPPOSITES[number]])
            f.append(jnp.where(fluid, arrived, owned[number]))
        return f, fluid

    started = send(0)
    receive(0, started)
    shift_walls()
    for x in range(extent_x):
        f, fluid = streamed(0, x)
        g = collide(f, fluid)
        store(1, x, g)
    finish = started
    started = send(1)
    receive(1, started)
    for x in range(extent_x):
        f, fluid = streamed(1, x)
        density = f[0]
        forward = None
        for i in range(1, 19, 2):
            density = density + (f[i] + f[i + 1])
            c = VELOCITIES[i][0]
            if c:
                term = (f[i] - f[i + 1])
                forward = term if forward is None else forward + term
        speed = walls[0, 1 + x, inner, :] * forward / density
        if spectral:
            ux[pl.ds(x * extent_z, extent_z), :] = speed
        else:
            out_ref[x] = speed

    if spectral:
        whole = ux[...]
        both = jnp.concatenate([whole, pltpu.roll(whole, height - 8, 1)], axis=0)
        turned = both.T
        for a in range(count_x):
            sent_x[a] = turned[16 * a : 16 * a + 8, :]
        x_copies = []
        for p in range(1, count_x):
            there = shifted_x(p)
            copy = pltpu.make_async_remote_copy(
                src_ref=sent_x.at[there],
                dst_ref=got_x.at[mx],
                send_sem=x_send.at[p],
                recv_sem=x_recv.at[p],
                device_id=(there, mz),
                device_id_type=MESH,
            )
            copy.start()
            x_copies.append(copy)
        got_x[mx] = sent_x[mx]
        table_copy.wait()
        for copy in x_copies:
            copy.wait_recv()
        re, im = eight_point([got_x[s] for s in range(8)])
        low_lanes = lax.broadcasted_iota(jnp.int32, (8, 128), 1) < 64
        for k in range(8):
            c = weights[pl.ds(k, 1), :]
            s = weights[pl.ds(8 + k, 1), :]
            if im[k] is None:
                real, imag = re[k] * c, -re[k] * s
            else:
                real, imag = re[k] * c + im[k] * s, im[k] * c - re[k] * s
            left[pl.ds(k, 8, stride=8), :] = jnp.where(low_lanes, real, pltpu.roll(imag, 64, 1))
            left[pl.ds(64 + k, 8, stride=8), :] = jnp.where(low_lanes, pltpu.roll(real, 64, 1), imag)
        high, low = halves(left[...])
        first = weights[pl.ds(16, 128), :].astype(jnp.bfloat16)
        contract = (((1,), (1,)), ((), ()))
        along = lax.dot_general(
            jnp.concatenate([first, first], axis=1),
            jnp.concatenate([high, low], axis=1),
            contract,
            preferred_element_type=jnp.float32,
        )
        for b in range(count_z):
            sent_z[b] = along[32 * b : 32 * b + 32, :]
        z_copies = []
        for p in range(1, count_z):
            there = shifted_z(p)
            copy = pltpu.make_async_remote_copy(
                src_ref=sent_z.at[there],
                dst_ref=got_z.at[mz],
                send_sem=z_send.at[p],
                recv_sem=z_recv.at[p],
                device_id=(mx, there),
                device_id_type=MESH,
            )
            copy.start()
            z_copies.append(copy)
        got_z[mz] = sent_z[mz]
        second_high, second_low = halves(weights[pl.ds(144, 128), :])
        second_twice = jnp.concatenate([second_high, second_high], axis=0)
        for copy in z_copies:
            copy.wait_recv()
        lines = got_z[...].reshape(128, 128).T
        high, low = halves(lines)
        result = jnp.dot(
            jnp.concatenate([high, low], axis=1), second_twice, preferred_element_type=jnp.float32
        ) + jnp.dot(high, second_low, preferred_element_type=jnp.float32)
        out_ref[0] = result[:, :64].reshape(16, 8, 64)
        out_ref[1] = result[:, 64:].reshape(16, 8, 64)
        for copy in x_copies + z_copies:
            copy.wait_send()
    for copy in finish + started:
        copy.wait_send()


def shards(populations, fluid_mask):
    number, extent_x, extent_z, height = populations.shape
    count_x, count_z = lax.axis_size("gx"), lax.axis_size("gz")
    full_x, full_z = count_x * extent_x, count_z * extent_z
    norm_scale = 1.0 / (math.sqrt(full_x * full_z) * SPEED_UNIT)
    spectral = (count_x, count_z, extent_x, extent_z, height) == (8, 4, 4, 16, 128)
    if spectral:
        table = jnp.asarray(tables(count_x, count_z, extent_x, extent_z, norm_scale))
    else:
        table = jnp.zeros((8, 128), jnp.float32)
    f32 = jnp.float32
    padded = (extent_x + 2, extent_z + 2 * TOP, height)
    edge_rows = 6 * extent_x
    dma = pltpu.SemaphoreType.DMA
    scratch = [
        pltpu.VMEM((extent_x, 19, extent_z, height), f32),
        pltpu.VMEM((extent_x, extent_z, height), jnp.int32),
        pltpu.VMEM((2, 19) + padded, f32),
        pltpu.VMEM((19, extent_x, extent_z, height), f32),
        pltpu.VMEM((3,) + padded, f32),
        pltpu.VMEM((2, 2, edge_rows, height), f32),
        pltpu.VMEM((2, 2, edge_rows, height), f32),
        pltpu.VMEM((2, 4, 2, height), f32),
        pltpu.VMEM((2, 4, 2, height), f32),
        dma((extent_x + 1,)),
        dma((2, 8)),
        dma((2, 8)),
        dma((2,)),
        dma((2,)),
    ]
    if spectral:
        scratch += [
            pltpu.VMEM((64, 128), f32),
            pltpu.VMEM((8, 8, 128), f32),
            pltpu.VMEM((8, 8, 128), f32),
            pltpu.VMEM((128, 128), f32),
            pltpu.VMEM((4, 32, 128), f32),
            pltpu.VMEM((4, 32, 128), f32),
            pltpu.VMEM(table.shape, f32),
            dma((1,)),
            dma((8,)),
            dma((8,)),
            dma((4,)),
            dma((4,)),
        ]
        out_shape = jax.ShapeDtypeStruct((2, 16, 8, 64), f32)
    else:
        out_shape = jax.ShapeDtypeStruct((extent_x, extent_z, height), f32)
    anywhere = pl.BlockSpec(memory_space=pl.ANY)
    result = pl.pallas_call(
        functools.partial(kernel, spectral),
        out_shape=out_shape,
        in_specs=[anywhere] * 3,
        out_specs=pl.BlockSpec(memory_space=pltpu.VMEM),
        scratch_shapes=scratch,
        compiler_params=pltpu.CompilerParams(
            collective_id=0, has_side_effects=True, vmem_limit_bytes=32 * 1024 * 1024
        ),
    )(populations, fluid_mask, table)
    if spectral:
        return result
    return spectrum(result, norm_scale)


def dft_tables(length, factor):
    index = jnp.arange(length, dtype=jnp.int32)
    products = index[:, None] * index[None, :] % length
    angles = products.astype(jnp.float32) * (2.0 * math.pi / length)
    return (jnp.cos(angles) * factor, jnp.sin(angles) * factor)


def spectrum(speed_x, norm_scale):
    columns = jnp.transpose(speed_x, (2, 1, 0))
    highest = lax.Precision.HIGHEST
    block = lax.all_to_all(columns, "gx", split_axis=0, concat_axis=2, tiled=True)
    cosine, sine = dft_tables(block.shape[2], norm_scale)
    real_part = jnp.einsum("yzx,xk->yzk", block, cosine, precision=highest)
    imag_part = -jnp.einsum("yzx,xk->yzk", block, sine, precision=highest)
    along_kx = jnp.stack([real_part, imag_part], axis=0)
    block = lax.all_to_all(along_kx, "gz", split_axis=3, concat_axis=2, tiled=True)
    cosine, sine = dft_tables(block.shape[2], 1.0)
    real_in = block[0]
    imag_in = block[1]
    real_part = jnp.einsum("ync,nk->yck", real_in, cosine, precision=highest) + jnp.einsum(
        "ync,nk->yck", imag_in, sine, precision=highest
    )
    imag_part = jnp.einsum("ync,nk->yck", imag_in, cosine, precision=highest) - jnp.einsum(
        "ync,nk->yck", real_in, sine, precision=highest
    )
    return jnp.stack([real_part, imag_part], axis=0)


def solution(mesh):
    placed = (P(None, "gx", "gz", None), P("gx", "gz", None))
    return jax.shard_map(
        shards, mesh=mesh, in_specs=placed, out_specs=P(None, "gx", "gz", None), check_vma=False
    )
```

```python
import functools
import math

import jax
import jax.numpy as jnp
import numpy as np
from jax import lax
from jax.experimental import pallas as pl
from jax.experimental.pallas import tpu as pltpu
from jax.sharding import PartitionSpec as P

VELOCITIES = (
    (0, 0, 0),
    (1, 0, 0),
    (-1, 0, 0),
    (0, 1, 0),
    (0, -1, 0),
    (0, 0, 1),
    (0, 0, -1),
    (1, 1, 0),
    (-1, -1, 0),
    (1, -1, 0),
    (-1, 1, 0),
    (1, 0, 1),
    (-1, 0, -1),
    (1, 0, -1),
    (-1, 0, 1),
    (0, 1, 1),
    (0, -1, -1),
    (0, 1, -1),
    (0, -1, 1),
)
LATTICE_WEIGHTS = (1.0 / 3.0,) + (1.0 / 18.0,) * 6 + (1.0 / 36.0,) * 12
OPPOSITES = (0, 2, 1, 4, 3, 6, 5, 8, 7, 10, 9, 12, 11, 14, 13, 16, 15, 18, 17)
RELAX_TIME = 0.6
BODY_FORCE = 0.0001
SPEED_UNIT = 0.05

CHAIN = (13, 1, 7, 9, 11, 5, 15, 18, 14, 2, 8, 10, 12, 6, 16, 17, 0, 3, 4)
SLOT = {number: CHAIN.index(number) for number in CHAIN}
X_FIRST = {1: 0, -1: 8}
Z_FIRST = {1: 4, -1: 12}
SIDES = ((1, 0), (-1, 0), (0, 1), (0, -1))
DIAGONALS = ((1, 1), (1, -1), (-1, 1), (-1, -1))
DIAGONAL_SLOT = (4, 0, 8, 12)
TOP = 8
MESH = pl.DeviceIdType.MESH


def collide(f, fluid):
    omega = 1.0 / RELAX_TIME
    keep = 1.0 - omega
    plus = {}
    minus = {}
    for i in range(1, 19, 2):
        plus[i] = f[i] + f[i + 1]
        minus[i] = f[i] - f[i + 1]
    density = f[0]
    momentum = [None, None, None]
    for i in range(1, 19, 2):
        density = density + plus[i]
        for axis in range(3):
            c = VELOCITIES[i][axis]
            if c:
                term = minus[i] if c > 0 else -minus[i]
                momentum[axis] = term if momentum[axis] is None else momentum[axis] + term
    inverse = 1.0 / density
    jx, jy, jz = momentum
    square = (jx * jx + jy * jy + jz * jz) * inverse
    base = density - 1.5 * square
    force = density * BODY_FORCE
    out = [None] * 19
    w0 = LATTICE_WEIGHTS[0] * omega
    out[0] = jnp.where(fluid, keep * f[0] + w0 * base, f[0])
    for i in range(1, 19, 2):
        w = LATTICE_WEIGHTS[i]
        cj = None
        for axis in range(3):
            c = VELOCITIES[i][axis]
            if c:
                j = momentum[axis]
                if cj is None:
                    cj = j if c > 0 else -j
                else:
                    cj = cj + j if c > 0 else cj - j
        even = (w * omega) * (base + 4.5 * (cj * cj * inverse))
        odd = (3.0 * w * omega) * cj
        if VELOCITIES[i][0]:
            odd = odd + (3.0 * w * VELOCITIES[i][0]) * force
        out[i] = jnp.where(fluid, keep * f[i] + (even + odd), f[i])
        out[i + 1] = jnp.where(fluid, keep * f[i + 1] + (even - odd), f[i + 1])
    return out


def tables(count_x, count_z, extent_x, extent_z, norm):
    lane = np.arange(128)
    step = (lane // extent_z) % extent_x
    k0 = np.arange(8)[:, None]
    angle = 2.0 * np.pi * k0 * step[None, :] / (count_x * extent_x)
    twiddle = np.concatenate([np.cos(angle), np.sin(angle)], axis=0)
    quarter_cos = np.array([1.0, 0.0, -1.0, 0.0])
    quarter_sin = np.array([0.0, 1.0, 0.0, -1.0])
    k1 = np.arange(4)[:, None]
    xl = np.arange(4)[None, :]
    c = quarter_cos[(k1 * xl) % 4]
    s = quarter_sin[(k1 * xl) % 4]
    block = np.zeros((4, 2, 2, 4))
    block[:, 0, 0] = c
    block[:, 0, 1] = s
    block[:, 1, 1] = c
    block[:, 1, 0] = -s
    first = np.einsum("kpqx,zw->kpzqxw", block, np.eye(extent_z)).reshape(128, 128)
    full_z = count_z * extent_z
    z = np.arange(full_z)
    angle = 2.0 * np.pi * ((z[:, None] * z[None, :]) % full_z) / full_z
    c = np.cos(angle) * norm
    s = np.sin(angle) * norm
    second = np.zeros((2, full_z, 2, full_z))
    second[0, :, 0] = c
    second[1, :, 0] = s
    second[1, :, 1] = c
    second[0, :, 1] = -s
    second = second.reshape(2, count_z, extent_z, 2, full_z).transpose(1, 0, 2, 3, 4)
    second = second.reshape(128, 128)
    return np.concatenate([twiddle, first, second], axis=0).astype(np.float32)


def halves(value):
    high = value.astype(jnp.bfloat16)
    low = (value - high.astype(jnp.float32)).astype(jnp.bfloat16)
    return high, low


def eight_point(v):
    r = math.sqrt(0.5)
    a0, a1, a2, a3 = v[0] + v[4], v[1] + v[5], v[2] + v[6], v[3] + v[7]
    b0, b1, b2, b3 = v[0] - v[4], v[1] - v[5], v[2] - v[6], v[3] - v[7]
    e0, e1 = a0 + a2, a1 + a3
    d, t = r * (b1 - b3), r * (b1 + b3)
    re = [e0 + e1, b0 + d, a0 - a2, b0 - d, e0 - e1]
    im = [None, -b2 - t, a3 - a1, b2 - t, None]
    re = re + [re[3], re[2], re[1]]
    im = im + [-im[3], -im[2], -im[1]]
    return re, im


def kernel(spectral, populations, fluid_mask, table, *rest):
    (out_ref, held, mask_i, rolled, plain, walls, edges_out, edges_in, corners_out, corners_in,
     sums_in, rims_out, rims_in, tips_out, tips_in, density, forward, ahead, behind,
     in_sem, halo_send, halo_recv, mask_send, mask_recv) = rest[:24]
    if spectral:
        (ux, sent_x, got_x, left, sent_z, got_z, weights,
         table_sem, x_send, x_recv, z_send, z_recv) = rest[24:]
    extent_x, extent_z, height = fluid_mask.shape
    last = extent_x - 1
    count_x, count_z = lax.axis_size("gx"), lax.axis_size("gz")
    mx, mz = lax.axis_index("gx"), lax.axis_index("gz")

    def shifted_x(step):
        return lax.rem(mx + step + count_x, count_x)

    def shifted_z(step):
        return lax.rem(mz + step + count_z, count_z)

    inner = pl.ds(TOP, extent_z)
    outer_rows = (0, last)
    inner_rows = tuple(range(1, last))

    mask_copy = pltpu.make_async_copy(fluid_mask, mask_i, in_sem.at[extent_x])
    mask_copy.start()
    fetches = {}
    for x in outer_rows + inner_rows:
        fetches[x] = pltpu.make_async_copy(populations.at[:, x], held.at[x], in_sem.at[x])
        fetches[x].start()

    barrier = pltpu.get_barrier_semaphore()
    partners = [(shifted_x(dx), shifted_z(dz)) for dx, dz in SIDES + DIAGONALS]
    if spectral:
        partners += [(shifted_x(p), mz) for p in range(2, count_x - 1)]
        partners += [(mx, shifted_z(p)) for p in range(2, count_z - 1)]
    for partner in partners:
        pl.semaphore_signal(barrier, inc=1, device_id=partner, device_id_type=MESH)
    if spectral:
        table_copy = pltpu.make_async_copy(table, weights, table_sem.at[0])
        table_copy.start()

    lanes = lax.broadcasted_iota(jnp.int32, (extent_z, height), 1)
    rows = lax.broadcasted_iota(jnp.int32, (extent_z, height), 0)

    def edge_of(value, cz):
        row = extent_z - 1 if cz > 0 else 0
        return value[row : row + 1, :]

    def first_collision(x):
        fetches[x].wait()
        solid = mask_i[x].astype(jnp.float32)
        walls[0, 1 + x, inner, :] = solid
        for side, cz in enumerate((1, -1)):
            edges_out[side, pl.ds(5 * extent_x + x, 1), :] = edge_of(solid, cz)
        for diagonal, (cx, cz) in enumerate(DIAGONALS):
            if x == (last if cx > 0 else 0):
                corners_out[diagonal, pl.ds(1, 1), :] = edge_of(solid, cz)
        g = collide([held[x, number] for number in range(19)], solid > 0)
        for number in range(19):
            cx, cy, cz = VELOCITIES[number]
            value = g[number]
            if cy:
                plain[number, x] = value
                value = pltpu.roll(value, cy % height, 1)
            slot = SLOT[number]
            rolled[slot, 1 + x, inner, :] = value
            if cz:
                order = (slot - Z_FIRST[cz]) % 16
                edge = edge_of(value, cz)
                edges_out[0 if cz > 0 else 1, pl.ds(order * extent_x + x, 1), :] = edge
                if cx and x == (last if cx > 0 else 0):
                    corners_out[DIAGONALS.index((cx, cz)), pl.ds(0, 1), :] = edge

    def send(source, target, send_sem, recv_sem, dx, dz):
        copy = pltpu.make_async_remote_copy(
            src_ref=source,
            dst_ref=target,
            send_sem=send_sem,
            recv_sem=recv_sem,
            device_id=(shifted_x(dx), shifted_z(dz)),
            device_id_type=MESH,
        )
        copy.start()
        return copy

    mask_copy.wait()
    for x in outer_rows:
        first_collision(x)
    pl.semaphore_wait(barrier, len(partners))
    x_sides, z_sides, corners = [], [], []
    for side, dx in enumerate((1, -1)):
        here, there = (extent_x, 0) if dx > 0 else (1, extent_x + 1)
        group = pl.ds(X_FIRST[dx], 5)
        x_sides.append(
            send(rolled.at[group, here, inner], rolled.at[group, there, inner],
                 halo_send.at[0, side], halo_recv.at[0, side], dx, 0)
        )
        x_sides.append(
            send(walls.at[0, here, inner], walls.at[0, there, inner],
                 mask_send.at[side], mask_recv.at[side], dx, 0)
        )
    for x in inner_rows:
        first_collision(x)
    for side, dz in enumerate((1, -1)):
        z_sides.append(
            send(edges_out.at[side], edges_in.at[side],
                 halo_send.at[0, 2 + side], halo_recv.at[0, 2 + side], 0, dz)
        )
    for diagonal, (dx, dz) in enumerate(DIAGONALS):
        corners.append(
            send(corners_out.at[diagonal], corners_in.at[diagonal],
                 halo_send.at[0, 4 + diagonal], halo_recv.at[0, 4 + diagonal], dx, dz)
        )

    around = lax.broadcasted_iota(jnp.int32, (extent_z + 2 * TOP, height), 1)

    def shift_walls(plane):
        value = walls[0, plane]
        walls[1, plane] = jnp.where(around == 0, 0.0, pltpu.roll(value, 1, 1))
        walls[2, plane] = jnp.where(around == height - 1, 0.0, pltpu.roll(value, height - 1, 1))

    def wall_from(number, x):
        cx, cy, cz = VELOCITIES[number]
        return walls[(0, 1, 2)[cy], 1 + x - cx, pl.ds(TOP - cz, extent_z), :] > 0

    def streamed(x, fluid):
        owned = []
        for number in range(19):
            if VELOCITIES[number][1]:
                owned.append(plain[number, x])
            else:
                owned.append(rolled[SLOT[number], 1 + x, inner, :])
        f = [owned[0]]
        for number in range(1, 19):
            cx, cy, cz = VELOCITIES[number]
            value = rolled[SLOT[number], 1 + x - cx, pl.ds(TOP - cz, extent_z), :]
            arrived = jnp.where(wall_from(number, x), value, owned[OPPOSITES[number]])
            f.append(jnp.where(fluid, arrived, owned[number]))
        return f

    rims = {}

    def second_collision(x):
        fluid = walls[0, 1 + x, inner, :] > 0
        g = collide(streamed(x, fluid), fluid)
        for number in range(19):
            held[x, number] = g[number]
        leaving = {}
        for number in range(1, 19):
            cx, cy, cz = VELOCITIES[number]
            value = jnp.where(fluid, g[number], 0.0)
            if cy:
                value = pltpu.roll(value, cy % height, 1)
                value = jnp.where(lanes == (0 if cy > 0 else height - 1), 0.0, value)
            leaving[cx, cz] = leaving[cx, cz] + value if (cx, cz) in leaving else value
        for cx, keep in ((1, ahead), (-1, behind), (0, None)):
            total = leaving[cx, 0]
            for cz in (1, -1):
                value = leaving[cx, cz]
                rims[x, cx, cz] = edge_of(value, cz)
                moved = pltpu.roll(value, cz % extent_z, 0)
                total = total + jnp.where(rows == (0 if cz > 0 else extent_z - 1), 0.0, moved)
            if keep is None:
                density[x] = g[0] + total
            else:
                keep[x] = total

    def bounced(x):
        sums = {}
        for number in range(1, 19):
            cx = VELOCITIES[number][0]
            value = jnp.where(wall_from(number, x), 0.0, held[x, OPPOSITES[number]])
            sums[cx] = sums[cx] + value if cx in sums else value
        density[x] = density[x] + (sums[0] + sums[1] + sums[-1])
        forward[x] = sums[1] - sums[-1]

    for copy in z_sides:
        copy.wait_recv()
    for side, cz in enumerate((1, -1)):
        row = TOP - 1 if cz > 0 else TOP + extent_z
        for x in range(extent_x):
            for order in range(5):
                rolled[(Z_FIRST[cz] + order) % 16, 1 + x, pl.ds(row, 1), :] = edges_in[
                    side, pl.ds(order * extent_x + x, 1), :
                ]
            walls[0, 1 + x, pl.ds(row, 1), :] = edges_in[side, pl.ds(5 * extent_x + x, 1), :]
    for x in range(extent_x):
        shift_walls(1 + x)
    for x in inner_rows:
        second_collision(x)
        bounced(x)
    for copy in x_sides + corners:
        copy.wait_recv()
    for diagonal, (cx, cz) in enumerate(DIAGONALS):
        plane = 0 if cx > 0 else extent_x + 1
        row = TOP - 1 if cz > 0 else TOP + extent_z
        rolled[DIAGONAL_SLOT[diagonal], plane, pl.ds(row, 1), :] = corners_in[diagonal, pl.ds(0, 1), :]
        walls[0, plane, pl.ds(row, 1), :] = corners_in[diagonal, pl.ds(1, 1), :]
    for plane in (0, extent_x + 1):
        shift_walls(plane)
    for x in outer_rows:
        second_collision(x)

    sums = []
    for side, (dx, x, keep) in enumerate(((1, last, ahead), (-1, 0, behind))):
        sums.append(
            send(keep.at[x], sums_in.at[side],
                 halo_send.at[1, side], halo_recv.at[1, side], dx, 0)
        )
    for side, dz in enumerate((1, -1)):
        for x in range(extent_x):
            total, along = rims[x, 0, dz], None
            if x > 0:
                total, along = total + rims[x - 1, 1, dz], rims[x - 1, 1, dz]
            if x < last:
                back = rims[x + 1, -1, dz]
                total, along = total + back, -back if along is None else along - back
            rims_out[side, pl.ds(x, 1), :] = total
            rims_out[side, pl.ds(extent_x + x, 1), :] = along
        sums.append(
            send(rims_out.at[side], rims_in.at[side],
                 halo_send.at[1, 2 + side], halo_recv.at[1, 2 + side], 0, dz)
        )
    for diagonal, (dx, dz) in enumerate(DIAGONALS):
        tips_out[diagonal] = rims[last if dx > 0 else 0, dx, dz]
        sums.append(
            send(tips_out.at[diagonal], tips_in.at[diagonal],
                 halo_send.at[1, 4 + diagonal], halo_recv.at[1, 4 + diagonal], dx, dz)
        )
    for x in outer_rows:
        bounced(x)
    for x in range(extent_x):
        total, along = density[x], forward[x]
        if x > 0:
            total, along = total + ahead[x - 1], along + ahead[x - 1]
        if x < last:
            total, along = total + behind[x + 1], along - behind[x + 1]
        density[x] = total
        forward[x] = along
    for copy in sums:
        copy.wait_recv()
    for side, dz in enumerate((1, -1)):
        row = 0 if dz > 0 else extent_z - 1
        for x in range(extent_x):
            total = rims_in[side, pl.ds(x, 1), :]
            along = rims_in[side, pl.ds(extent_x + x, 1), :]
            for diagonal, (cx, cz) in enumerate(DIAGONALS):
                if cz == dz and x == (0 if cx > 0 else last):
                    total = total + tips_in[diagonal]
                    along = along + tips_in[diagonal] if cx > 0 else along - tips_in[diagonal]
            density[x, pl.ds(row, 1), :] = density[x, pl.ds(row, 1), :] + total
            forward[x, pl.ds(row, 1), :] = forward[x, pl.ds(row, 1), :] + along
    for x in range(extent_x):
        total, along = density[x], forward[x]
        if x == 0:
            total, along = total + sums_in[0], along + sums_in[0]
        if x == last:
            total, along = total + sums_in[1], along - sums_in[1]
        speed = jnp.where(walls[0, 1 + x, inner, :] > 0, along / total, 0.0)
        if spectral:
            ux[pl.ds(x * extent_z, extent_z), :] = speed
        else:
            out_ref[x] = speed

    if spectral:
        whole = ux[...]
        both = jnp.concatenate([whole, pltpu.roll(whole, height - 8, 1)], axis=0)
        turned = both.T
        for a in range(count_x):
            sent_x[a] = turned[16 * a : 16 * a + 8, :]
        x_copies = []
        for p in range(1, count_x):
            there = shifted_x(p)
            copy = pltpu.make_async_remote_copy(
                src_ref=sent_x.at[there],
                dst_ref=got_x.at[mx],
                send_sem=x_send.at[p],
                recv_sem=x_recv.at[p],
                device_id=(there, mz),
                device_id_type=MESH,
            )
            copy.start()
            x_copies.append(copy)
        got_x[mx] = sent_x[mx]
        table_copy.wait()
        first = weights[pl.ds(16, 128), :].astype(jnp.bfloat16)
        for copy in x_copies:
            copy.wait_recv()
        re, im = eight_point([got_x[s] for s in range(8)])
        low_lanes = lax.broadcasted_iota(jnp.int32, (8, 128), 1) < 64
        for k in range(8):
            c = weights[pl.ds(k, 1), :]
            s = weights[pl.ds(8 + k, 1), :]
            if im[k] is None:
                real, imag = re[k] * c, -re[k] * s
            else:
                real, imag = re[k] * c + im[k] * s, im[k] * c - re[k] * s
            left[pl.ds(k, 8, stride=8), :] = jnp.where(low_lanes, real, pltpu.roll(imag, 64, 1))
            left[pl.ds(64 + k, 8, stride=8), :] = jnp.where(low_lanes, pltpu.roll(real, 64, 1), imag)
        high, low = halves(left[...])
        contract = (((1,), (1,)), ((), ()))
        along = lax.dot_general(
            jnp.concatenate([first, first], axis=1),
            jnp.concatenate([high, low], axis=1),
            contract,
            preferred_element_type=jnp.float32,
        )
        for b in range(count_z):
            sent_z[b] = along[32 * b : 32 * b + 32, :]
        z_copies = []
        for p in range(1, count_z):
            there = shifted_z(p)
            copy = pltpu.make_async_remote_copy(
                src_ref=sent_z.at[there],
                dst_ref=got_z.at[mz],
                send_sem=z_send.at[p],
                recv_sem=z_recv.at[p],
                device_id=(mx, there),
                device_id_type=MESH,
            )
            copy.start()
            z_copies.append(copy)
        got_z[mz] = sent_z[mz]
        second_high, second_low = halves(weights[pl.ds(144, 128), :])
        second_twice = jnp.concatenate([second_high, second_high], axis=0)
        for copy in z_copies:
            copy.wait_recv()
        lines = got_z[...].reshape(128, 128).T
        high, low = halves(lines)
        result = jnp.dot(
            jnp.concatenate([high, low], axis=1), second_twice, preferred_element_type=jnp.float32
        ) + jnp.dot(high, second_low, preferred_element_type=jnp.float32)
        out_ref[0] = result[:, :64].reshape(16, 8, 64)
        out_ref[1] = result[:, 64:].reshape(16, 8, 64)
        for copy in x_copies + z_copies:
            copy.wait_send()
    for copy in x_sides + z_sides + corners + sums:
        copy.wait_send()


def shards(populations, fluid_mask):
    number, extent_x, extent_z, height = populations.shape
    count_x, count_z = lax.axis_size("gx"), lax.axis_size("gz")
    full_x, full_z = count_x * extent_x, count_z * extent_z
    norm_scale = 1.0 / (math.sqrt(full_x * full_z) * SPEED_UNIT)
    spectral = (count_x, count_z, extent_x, extent_z, height) == (8, 4, 4, 16, 128)
    if spectral:
        table = jnp.asarray(tables(count_x, count_z, extent_x, extent_z, norm_scale))
    else:
        table = jnp.zeros((8, 128), jnp.float32)
    f32 = jnp.float32
    padded = (extent_x + 2, extent_z + 2 * TOP, height)
    edge_rows = 6 * extent_x
    dma = pltpu.SemaphoreType.DMA
    scratch = [
        pltpu.VMEM((extent_x, 19, extent_z, height), f32),
        pltpu.VMEM((extent_x, extent_z, height), jnp.int32),
        pltpu.VMEM((19,) + padded, f32),
        pltpu.VMEM((19, extent_x, extent_z, height), f32),
        pltpu.VMEM((3,) + padded, f32),
        pltpu.VMEM((2, edge_rows, height), f32),
        pltpu.VMEM((2, edge_rows, height), f32),
        pltpu.VMEM((4, 2, height), f32),
        pltpu.VMEM((4, 2, height), f32),
        pltpu.VMEM((2, extent_z, height), f32),
        pltpu.VMEM((2, 2 * extent_x, height), f32),
        pltpu.VMEM((2, 2 * extent_x, height), f32),
        pltpu.VMEM((4, 1, height), f32),
        pltpu.VMEM((4, 1, height), f32),
        pltpu.VMEM((extent_x, extent_z, height), f32),
        pltpu.VMEM((extent_x, extent_z, height), f32),
        pltpu.VMEM((extent_x, extent_z, height), f32),
        pltpu.VMEM((extent_x, extent_z, height), f32),
        dma((extent_x + 1,)),
        dma((2, 8)),
        dma((2, 8)),
        dma((2,)),
        dma((2,)),
    ]
    if spectral:
        scratch += [
            pltpu.VMEM((64, 128), f32),
            pltpu.VMEM((8, 8, 128), f32),
            pltpu.VMEM((8, 8, 128), f32),
            pltpu.VMEM((128, 128), f32),
            pltpu.VMEM((4, 32, 128), f32),
            pltpu.VMEM((4, 32, 128), f32),
            pltpu.VMEM(table.shape, f32),
            dma((1,)),
            dma((8,)),
            dma((8,)),
            dma((4,)),
            dma((4,)),
        ]
        out_shape = jax.ShapeDtypeStruct((2, 16, 8, 64), f32)
    else:
        out_shape = jax.ShapeDtypeStruct((extent_x, extent_z, height), f32)
    in_hbm = pl.BlockSpec(memory_space=pltpu.HBM)
    result = pl.pallas_call(
        functools.partial(kernel, spectral),
        out_shape=out_shape,
        in_specs=[in_hbm] * 3,
        out_specs=pl.BlockSpec(memory_space=pltpu.VMEM),
        scratch_shapes=scratch,
        compiler_params=pltpu.CompilerParams(
            collective_id=0, has_side_effects=True, vmem_limit_bytes=32 * 1024 * 1024
        ),
    )(populations, fluid_mask, table)
    if spectral:
        return result
    return spectrum(result, norm_scale)


def dft_tables(length, factor):
    index = jnp.arange(length, dtype=jnp.int32)
    products = index[:, None] * index[None, :] % length
    angles = products.astype(jnp.float32) * (2.0 * math.pi / length)
    return (jnp.cos(angles) * factor, jnp.sin(angles) * factor)


def spectrum(speed_x, norm_scale):
    columns = jnp.transpose(speed_x, (2, 1, 0))
    highest = lax.Precision.HIGHEST
    block = lax.all_to_all(columns, "gx", split_axis=0, concat_axis=2, tiled=True)
    cosine, sine = dft_tables(block.shape[2], norm_scale)
    real_part = jnp.einsum("yzx,xk->yzk", block, cosine, precision=highest)
    imag_part = -jnp.einsum("yzx,xk->yzk", block, sine, precision=highest)
    along_kx = jnp.stack([real_part, imag_part], axis=0)
    block = lax.all_to_all(along_kx, "gz", split_axis=3, concat_axis=2, tiled=True)
    cosine, sine = dft_tables(block.shape[2], 1.0)
    real_in = block[0]
    imag_in = block[1]
    real_part = jnp.einsum("ync,nk->yck", real_in, cosine, precision=highest) + jnp.einsum(
        "ync,nk->yck", imag_in, sine, precision=highest
    )
    imag_part = jnp.einsum("ync,nk->yck", imag_in, cosine, precision=highest) - jnp.einsum(
        "ync,nk->yck", real_in, sine, precision=highest
    )
    return jnp.stack([real_part, imag_part], axis=0)


def solution(mesh):
    placed = (P(None, "gx", "gz", None), P("gx", "gz", None))
    return jax.shard_map(
        shards, mesh=mesh, in_specs=placed, out_specs=P(None, "gx", "gz", None), check_vma=False
    )
```

```python
import functools
import math

import jax
import jax.numpy as jnp
import numpy as np
from jax import lax
from jax.experimental import pallas as pl
from jax.experimental.pallas import tpu as pltpu
from jax.sharding import PartitionSpec as P

VELOCITIES = (
    (0, 0, 0),
    (1, 0, 0),
    (-1, 0, 0),
    (0, 1, 0),
    (0, -1, 0),
    (0, 0, 1),
    (0, 0, -1),
    (1, 1, 0),
    (-1, -1, 0),
    (1, -1, 0),
    (-1, 1, 0),
    (1, 0, 1),
    (-1, 0, -1),
    (1, 0, -1),
    (-1, 0, 1),
    (0, 1, 1),
    (0, -1, -1),
    (0, 1, -1),
    (0, -1, 1),
)
LATTICE_WEIGHTS = (1.0 / 3.0,) + (1.0 / 18.0,) * 6 + (1.0 / 36.0,) * 12
OPPOSITES = (0, 2, 1, 4, 3, 6, 5, 8, 7, 10, 9, 12, 11, 14, 13, 16, 15, 18, 17)
RELAX_TIME = 0.6
BODY_FORCE = 0.0001
SPEED_UNIT = 0.05

CHAIN = (13, 1, 7, 9, 11, 5, 15, 18, 14, 2, 8, 10, 12, 6, 16, 17, 0, 3, 4)
SLOT = {number: CHAIN.index(number) for number in CHAIN}
X_FIRST = {1: 0, -1: 8}
Z_FIRST = {1: 4, -1: 12}
SIDES = ((1, 0), (-1, 0), (0, 1), (0, -1))
DIAGONALS = ((1, 1), (1, -1), (-1, 1), (-1, -1))
DIAGONAL_SLOT = (4, 0, 8, 12)
TOP = 8
MESH = pl.DeviceIdType.MESH


def collide(f, fluid):
    omega = 1.0 / RELAX_TIME
    keep = 1.0 - omega
    plus = {}
    minus = {}
    for i in range(1, 19, 2):
        plus[i] = f[i] + f[i + 1]
        minus[i] = f[i] - f[i + 1]
    density = f[0]
    momentum = [None, None, None]
    for i in range(1, 19, 2):
        density = density + plus[i]
        for axis in range(3):
            c = VELOCITIES[i][axis]
            if c:
                term = minus[i] if c > 0 else -minus[i]
                momentum[axis] = term if momentum[axis] is None else momentum[axis] + term
    inverse = 1.0 / density
    jx, jy, jz = momentum
    square = (jx * jx + jy * jy + jz * jz) * inverse
    base = density - 1.5 * square
    force = density * BODY_FORCE
    out = [None] * 19
    w0 = LATTICE_WEIGHTS[0] * omega
    out[0] = jnp.where(fluid, keep * f[0] + w0 * base, f[0])
    for i in range(1, 19, 2):
        w = LATTICE_WEIGHTS[i]
        cj = None
        for axis in range(3):
            c = VELOCITIES[i][axis]
            if c:
                j = momentum[axis]
                if cj is None:
                    cj = j if c > 0 else -j
                else:
                    cj = cj + j if c > 0 else cj - j
        even = (w * omega) * (base + 4.5 * (cj * cj * inverse))
        odd = (3.0 * w * omega) * cj
        if VELOCITIES[i][0]:
            odd = odd + (3.0 * w * VELOCITIES[i][0]) * force
        out[i] = jnp.where(fluid, keep * f[i] + (even + odd), f[i])
        out[i + 1] = jnp.where(fluid, keep * f[i + 1] + (even - odd), f[i + 1])
    return out


def tables(count_x, count_z, extent_x, extent_z, norm):
    lane = np.arange(128)
    step = (lane // extent_z) % extent_x
    k0 = np.arange(8)[:, None]
    angle = 2.0 * np.pi * k0 * step[None, :] / (count_x * extent_x)
    twiddle = np.concatenate([np.cos(angle), np.sin(angle)], axis=0)
    quarter_cos = np.array([1.0, 0.0, -1.0, 0.0])
    quarter_sin = np.array([0.0, 1.0, 0.0, -1.0])
    k1 = np.arange(4)[:, None]
    xl = np.arange(4)[None, :]
    c = quarter_cos[(k1 * xl) % 4]
    s = quarter_sin[(k1 * xl) % 4]
    block = np.zeros((4, 2, 2, 4))
    block[:, 0, 0] = c
    block[:, 0, 1] = s
    block[:, 1, 1] = c
    block[:, 1, 0] = -s
    first = np.einsum("kpqx,zw->kpzqxw", block, np.eye(extent_z)).reshape(128, 128)
    full_z = count_z * extent_z
    z = np.arange(full_z)
    angle = 2.0 * np.pi * ((z[:, None] * z[None, :]) % full_z) / full_z
    c = np.cos(angle) * norm
    s = np.sin(angle) * norm
    second = np.zeros((2, full_z, 2, full_z))
    second[0, :, 0] = c
    second[1, :, 0] = s
    second[1, :, 1] = c
    second[0, :, 1] = -s
    second = second.reshape(2, count_z, extent_z, 2, full_z).transpose(1, 0, 2, 3, 4)
    second = second.reshape(128, 128)
    return np.concatenate([twiddle, first, second], axis=0).astype(np.float32)


def halves(value):
    high = value.astype(jnp.bfloat16)
    low = (value - high.astype(jnp.float32)).astype(jnp.bfloat16)
    return high, low


def eight_point(v):
    r = math.sqrt(0.5)
    a0, a1, a2, a3 = v[0] + v[4], v[1] + v[5], v[2] + v[6], v[3] + v[7]
    b0, b1, b2, b3 = v[0] - v[4], v[1] - v[5], v[2] - v[6], v[3] - v[7]
    e0, e1 = a0 + a2, a1 + a3
    d, t = r * (b1 - b3), r * (b1 + b3)
    re = [e0 + e1, b0 + d, a0 - a2, b0 - d, e0 - e1]
    im = [None, -b2 - t, a3 - a1, b2 - t, None]
    re = re + [re[3], re[2], re[1]]
    im = im + [-im[3], -im[2], -im[1]]
    return re, im


def kernel(spectral, populations, fluid_mask, table, *rest):
    (out_ref, held, mask_i, rolled, plain, walls, edges_out, edges_in, corners_out, corners_in,
     sums_in, rims_out, rims_in, tips_out, tips_in, density, forward, ahead, behind,
     in_sem, halo_send, halo_recv, mask_send, mask_recv) = rest[:24]
    if spectral:
        (ux, sent_x, got_x, left, sent_z, got_z, weights,
         table_sem, x_send, x_recv, z_send, z_recv) = rest[24:]
    extent_x, extent_z, height = fluid_mask.shape
    last = extent_x - 1
    count_x, count_z = lax.axis_size("gx"), lax.axis_size("gz")
    mx, mz = lax.axis_index("gx"), lax.axis_index("gz")

    def shifted_x(step):
        return lax.rem(mx + step + count_x, count_x)

    def shifted_z(step):
        return lax.rem(mz + step + count_z, count_z)

    inner = pl.ds(TOP, extent_z)
    outer_rows = (0, last)
    inner_rows = tuple(range(1, last))

    mask_copy = pltpu.make_async_copy(fluid_mask, mask_i, in_sem.at[extent_x])
    mask_copy.start()
    fetches = {}
    for x in outer_rows + inner_rows:
        fetches[x] = pltpu.make_async_copy(populations.at[:, x], held.at[x], in_sem.at[x])
        fetches[x].start()

    barrier = pltpu.get_barrier_semaphore()
    partners = [(shifted_x(dx), shifted_z(dz)) for dx, dz in SIDES + DIAGONALS]
    if spectral:
        partners += [(shifted_x(p), mz) for p in range(2, count_x - 1)]
        partners += [(mx, shifted_z(p)) for p in range(2, count_z - 1)]
    for partner in partners:
        pl.semaphore_signal(barrier, inc=1, device_id=partner, device_id_type=MESH)
    if spectral:
        table_copy = pltpu.make_async_copy(table, weights, table_sem.at[0])
        table_copy.start()

    lanes = lax.broadcasted_iota(jnp.int32, (extent_z, height), 1)
    rows = lax.broadcasted_iota(jnp.int32, (extent_z, height), 0)

    def edge_of(value, cz):
        row = extent_z - 1 if cz > 0 else 0
        return value[row : row + 1, :]

    def first_collision(x):
        fetches[x].wait()
        solid = mask_i[x].astype(jnp.float32)
        walls[0, 1 + x, inner, :] = solid
        for side, cz in enumerate((1, -1)):
            edges_out[side, pl.ds(5 * extent_x + x, 1), :] = edge_of(solid, cz)
        for diagonal, (cx, cz) in enumerate(DIAGONALS):
            if x == (last if cx > 0 else 0):
                corners_out[diagonal, pl.ds(1, 1), :] = edge_of(solid, cz)
        g = collide([held[x, number] for number in range(19)], solid > 0)
        for number in range(19):
            cx, cy, cz = VELOCITIES[number]
            value = g[number]
            if cy:
                plain[number, x] = value
                value = pltpu.roll(value, cy % height, 1)
            slot = SLOT[number]
            rolled[slot, 1 + x, inner, :] = value
            if cz:
                order = (slot - Z_FIRST[cz]) % 16
                edge = edge_of(value, cz)
                edges_out[0 if cz > 0 else 1, pl.ds(order * extent_x + x, 1), :] = edge
                if cx and x == (last if cx > 0 else 0):
                    corners_out[DIAGONALS.index((cx, cz)), pl.ds(0, 1), :] = edge

    def send(source, target, send_sem, recv_sem, dx, dz):
        copy = pltpu.make_async_remote_copy(
            src_ref=source,
            dst_ref=target,
            send_sem=send_sem,
            recv_sem=recv_sem,
            device_id=(shifted_x(dx), shifted_z(dz)),
            device_id_type=MESH,
        )
        copy.start()
        return copy

    mask_copy.wait()
    for x in outer_rows:
        first_collision(x)
    pl.semaphore_wait(barrier, len(partners))
    x_sides, z_sides, corners = [], [], []
    for side, dx in enumerate((1, -1)):
        here, there = (extent_x, 0) if dx > 0 else (1, extent_x + 1)
        group = pl.ds(X_FIRST[dx], 5)
        x_sides.append(
            send(rolled.at[group, here, inner], rolled.at[group, there, inner],
                 halo_send.at[0, side], halo_recv.at[0, side], dx, 0)
        )
        x_sides.append(
            send(walls.at[0, here, inner], walls.at[0, there, inner],
                 mask_send.at[side], mask_recv.at[side], dx, 0)
        )
    for x in inner_rows:
        first_collision(x)
    for side, dz in enumerate((1, -1)):
        z_sides.append(
            send(edges_out.at[side], edges_in.at[side],
                 halo_send.at[0, 2 + side], halo_recv.at[0, 2 + side], 0, dz)
        )
    for diagonal, (dx, dz) in enumerate(DIAGONALS):
        corners.append(
            send(corners_out.at[diagonal], corners_in.at[diagonal],
                 halo_send.at[0, 4 + diagonal], halo_recv.at[0, 4 + diagonal], dx, dz)
        )

    around = lax.broadcasted_iota(jnp.int32, (extent_z + 2 * TOP, height), 1)

    def shift_walls(plane):
        value = walls[0, plane]
        walls[1, plane] = jnp.where(around == 0, 0.0, pltpu.roll(value, 1, 1))
        walls[2, plane] = jnp.where(around == height - 1, 0.0, pltpu.roll(value, height - 1, 1))

    def wall_from(number, x):
        cx, cy, cz = VELOCITIES[number]
        return walls[(0, 1, 2)[cy], 1 + x - cx, pl.ds(TOP - cz, extent_z), :] > 0

    def streamed(x, fluid):
        owned = []
        for number in range(19):
            if VELOCITIES[number][1]:
                owned.append(plain[number, x])
            else:
                owned.append(rolled[SLOT[number], 1 + x, inner, :])
        f = [owned[0]]
        for number in range(1, 19):
            cx, cy, cz = VELOCITIES[number]
            value = rolled[SLOT[number], 1 + x - cx, pl.ds(TOP - cz, extent_z), :]
            arrived = jnp.where(wall_from(number, x), value, owned[OPPOSITES[number]])
            f.append(jnp.where(fluid, arrived, owned[number]))
        return f

    rims = {}

    def second_collision(x):
        fluid = walls[0, 1 + x, inner, :] > 0
        g = collide(streamed(x, fluid), fluid)
        for number in range(19):
            held[x, number] = g[number]
        leaving = {}
        for number in range(1, 19):
            cx, cy, cz = VELOCITIES[number]
            value = jnp.where(fluid, g[number], 0.0)
            if cy:
                value = pltpu.roll(value, cy % height, 1)
                value = jnp.where(lanes == (0 if cy > 0 else height - 1), 0.0, value)
            leaving[cx, cz] = leaving[cx, cz] + value if (cx, cz) in leaving else value
        for cx, keep in ((1, ahead), (-1, behind), (0, None)):
            total = leaving[cx, 0]
            for cz in (1, -1):
                value = leaving[cx, cz]
                rims[x, cx, cz] = edge_of(value, cz)
                moved = pltpu.roll(value, cz % extent_z, 0)
                total = total + jnp.where(rows == (0 if cz > 0 else extent_z - 1), 0.0, moved)
            if keep is None:
                density[x] = g[0] + total
            else:
                keep[x] = total

    def bounced(x):
        sums = {}
        for number in range(1, 19):
            cx = VELOCITIES[number][0]
            value = jnp.where(wall_from(number, x), 0.0, held[x, OPPOSITES[number]])
            sums[cx] = sums[cx] + value if cx in sums else value
        density[x] = density[x] + (sums[0] + sums[1] + sums[-1])
        forward[x] = sums[1] - sums[-1]

    for copy in z_sides:
        copy.wait_recv()
    for side, cz in enumerate((1, -1)):
        row = TOP - 1 if cz > 0 else TOP + extent_z
        for x in range(extent_x):
            for order in range(5):
                rolled[(Z_FIRST[cz] + order) % 16, 1 + x, pl.ds(row, 1), :] = edges_in[
                    side, pl.ds(order * extent_x + x, 1), :
                ]
            walls[0, 1 + x, pl.ds(row, 1), :] = edges_in[side, pl.ds(5 * extent_x + x, 1), :]
    for x in range(extent_x):
        shift_walls(1 + x)
    for x in inner_rows:
        second_collision(x)
        bounced(x)
    for copy in x_sides + corners:
        copy.wait_recv()
    for diagonal, (cx, cz) in enumerate(DIAGONALS):
        plane = 0 if cx > 0 else extent_x + 1
        row = TOP - 1 if cz > 0 else TOP + extent_z
        rolled[DIAGONAL_SLOT[diagonal], plane, pl.ds(row, 1), :] = corners_in[diagonal, pl.ds(0, 1), :]
        walls[0, plane, pl.ds(row, 1), :] = corners_in[diagonal, pl.ds(1, 1), :]
    for plane in (0, extent_x + 1):
        shift_walls(plane)
    for x in outer_rows:
        second_collision(x)

    sums = []
    for side, (dx, x, keep) in enumerate(((1, last, ahead), (-1, 0, behind))):
        sums.append(
            send(keep.at[x], sums_in.at[side],
                 halo_send.at[1, side], halo_recv.at[1, side], dx, 0)
        )
    for side, dz in enumerate((1, -1)):
        for x in range(extent_x):
            total, along = rims[x, 0, dz], None
            if x > 0:
                total, along = total + rims[x - 1, 1, dz], rims[x - 1, 1, dz]
            if x < last:
                back = rims[x + 1, -1, dz]
                total, along = total + back, -back if along is None else along - back
            rims_out[side, pl.ds(x, 1), :] = total
            rims_out[side, pl.ds(extent_x + x, 1), :] = along
        sums.append(
            send(rims_out.at[side], rims_in.at[side],
                 halo_send.at[1, 2 + side], halo_recv.at[1, 2 + side], 0, dz)
        )
    for diagonal, (dx, dz) in enumerate(DIAGONALS):
        tips_out[diagonal] = rims[last if dx > 0 else 0, dx, dz]
        sums.append(
            send(tips_out.at[diagonal], tips_in.at[diagonal],
                 halo_send.at[1, 4 + diagonal], halo_recv.at[1, 4 + diagonal], dx, dz)
        )
    for x in outer_rows:
        bounced(x)
    for x in range(extent_x):
        total, along = density[x], forward[x]
        if x > 0:
            total, along = total + ahead[x - 1], along + ahead[x - 1]
        if x < last:
            total, along = total + behind[x + 1], along - behind[x + 1]
        density[x] = total
        forward[x] = along
    for copy in sums:
        copy.wait_recv()
    for side, dz in enumerate((1, -1)):
        row = 0 if dz > 0 else extent_z - 1
        for x in range(extent_x):
            total = rims_in[side, pl.ds(x, 1), :]
            along = rims_in[side, pl.ds(extent_x + x, 1), :]
            for diagonal, (cx, cz) in enumerate(DIAGONALS):
                if cz == dz and x == (0 if cx > 0 else last):
                    total = total + tips_in[diagonal]
                    along = along + tips_in[diagonal] if cx > 0 else along - tips_in[diagonal]
            density[x, pl.ds(row, 1), :] = density[x, pl.ds(row, 1), :] + total
            forward[x, pl.ds(row, 1), :] = forward[x, pl.ds(row, 1), :] + along
    for x in range(extent_x):
        total, along = density[x], forward[x]
        if x == 0:
            total, along = total + sums_in[0], along + sums_in[0]
        if x == last:
            total, along = total + sums_in[1], along - sums_in[1]
        speed = jnp.where(walls[0, 1 + x, inner, :] > 0, along / total, 0.0)
        if spectral:
            ux[pl.ds(x * extent_z, extent_z), :] = speed
        else:
            out_ref[x] = speed

    if spectral:
        whole = ux[...]
        both = jnp.concatenate([whole, pltpu.roll(whole, height - 8, 1)], axis=0)
        turned = both.T
        for a in range(count_x):
            sent_x[a] = turned[16 * a : 16 * a + 8, :]
        x_copies = []
        for p in range(1, count_x):
            there = shifted_x(p)
            copy = pltpu.make_async_remote_copy(
                src_ref=sent_x.at[there],
                dst_ref=got_x.at[mx],
                send_sem=x_send.at[p],
                recv_sem=x_recv.at[p],
                device_id=(there, mz),
                device_id_type=MESH,
            )
            copy.start()
            x_copies.append(copy)
        got_x[mx] = sent_x[mx]
        table_copy.wait()
        first = weights[pl.ds(16, 128), :].astype(jnp.bfloat16)
        for copy in x_copies:
            copy.wait_recv()
        re, im = eight_point([got_x[s] for s in range(8)])
        low_lanes = lax.broadcasted_iota(jnp.int32, (8, 128), 1) < 64
        for k in range(8):
            c = weights[pl.ds(k, 1), :]
            s = weights[pl.ds(8 + k, 1), :]
            if im[k] is None:
                real, imag = re[k] * c, -re[k] * s
            else:
                real, imag = re[k] * c + im[k] * s, im[k] * c - re[k] * s
            left[pl.ds(k, 8, stride=8), :] = jnp.where(low_lanes, real, pltpu.roll(imag, 64, 1))
            left[pl.ds(64 + k, 8, stride=8), :] = jnp.where(low_lanes, pltpu.roll(real, 64, 1), imag)
        high, low = halves(left[...])
        contract = (((1,), (1,)), ((), ()))
        along = lax.dot_general(
            jnp.concatenate([first, first], axis=1),
            jnp.concatenate([high, low], axis=1),
            contract,
            preferred_element_type=jnp.float32,
        )
        for b in range(count_z):
            sent_z[b] = along[32 * b : 32 * b + 32, :]
        z_copies = []
        for p in range(1, count_z):
            there = shifted_z(p)
            copy = pltpu.make_async_remote_copy(
                src_ref=sent_z.at[there],
                dst_ref=got_z.at[mz],
                send_sem=z_send.at[p],
                recv_sem=z_recv.at[p],
                device_id=(mx, there),
                device_id_type=MESH,
            )
            copy.start()
            z_copies.append(copy)
        got_z[mz] = sent_z[mz]
        second_high, second_low = halves(weights[pl.ds(144, 128), :])
        second_twice = jnp.concatenate([second_high, second_high], axis=0)
        for copy in z_copies:
            copy.wait_recv()
        lines = got_z[...].reshape(128, 128).T
        high, low = halves(lines)
        result = jnp.dot(
            jnp.concatenate([high, low], axis=1), second_twice, preferred_element_type=jnp.float32
        ) + jnp.dot(high, second_low, preferred_element_type=jnp.float32)
        out_ref[0] = result[:, :64].reshape(16, 8, 64)
        out_ref[1] = result[:, 64:].reshape(16, 8, 64)
        for copy in x_copies + z_copies:
            copy.wait_send()
    for copy in x_sides + z_sides + corners + sums:
        copy.wait_send()


def shards(populations, fluid_mask):
    number, extent_x, extent_z, height = populations.shape
    count_x, count_z = lax.axis_size("gx"), lax.axis_size("gz")
    full_x, full_z = count_x * extent_x, count_z * extent_z
    norm_scale = 1.0 / (math.sqrt(full_x * full_z) * SPEED_UNIT)
    spectral = (count_x, count_z, extent_x, extent_z, height) == (8, 4, 4, 16, 128)
    if spectral:
        table = jnp.asarray(tables(count_x, count_z, extent_x, extent_z, norm_scale))
    else:
        table = jnp.zeros((8, 128), jnp.float32)
    f32 = jnp.float32
    padded = (extent_x + 2, extent_z + 2 * TOP, height)
    edge_rows = 6 * extent_x
    dma = pltpu.SemaphoreType.DMA
    scratch = [
        pltpu.VMEM((extent_x, 19, extent_z, height), f32),
        pltpu.VMEM((extent_x, extent_z, height), jnp.int32),
        pltpu.VMEM((19,) + padded, f32),
        pltpu.VMEM((19, extent_x, extent_z, height), f32),
        pltpu.VMEM((3,) + padded, f32),
        pltpu.VMEM((2, edge_rows, height), f32),
        pltpu.VMEM((2, edge_rows, height), f32),
        pltpu.VMEM((4, 2, height), f32),
        pltpu.VMEM((4, 2, height), f32),
        pltpu.VMEM((2, extent_z, height), f32),
        pltpu.VMEM((2, 2 * extent_x, height), f32),
        pltpu.VMEM((2, 2 * extent_x, height), f32),
        pltpu.VMEM((4, 1, height), f32),
        pltpu.VMEM((4, 1, height), f32),
        pltpu.VMEM((extent_x, extent_z, height), f32),
        pltpu.VMEM((extent_x, extent_z, height), f32),
        pltpu.VMEM((extent_x, extent_z, height), f32),
        pltpu.VMEM((extent_x, extent_z, height), f32),
        dma((extent_x + 1,)),
        dma((2, 8)),
        dma((2, 8)),
        dma((2,)),
        dma((2,)),
    ]
    if spectral:
        scratch += [
            pltpu.VMEM((64, 128), f32),
            pltpu.VMEM((8, 8, 128), f32),
            pltpu.VMEM((8, 8, 128), f32),
            pltpu.VMEM((128, 128), f32),
            pltpu.VMEM((4, 32, 128), f32),
            pltpu.VMEM((4, 32, 128), f32),
            pltpu.VMEM(table.shape, f32),
            dma((1,)),
            dma((8,)),
            dma((8,)),
            dma((4,)),
            dma((4,)),
        ]
        out_shape = jax.ShapeDtypeStruct((2, 16, 8, 64), f32)
    else:
        out_shape = jax.ShapeDtypeStruct((extent_x, extent_z, height), f32)
    in_hbm = pl.BlockSpec(memory_space=pltpu.HBM)
    result = pl.pallas_call(
        functools.partial(kernel, spectral),
        out_shape=out_shape,
        in_specs=[in_hbm] * 3,
        out_specs=pl.BlockSpec(memory_space=pltpu.VMEM),
        scratch_shapes=scratch,
        compiler_params=pltpu.CompilerParams(
            collective_id=0, has_side_effects=True
        ),
    )(populations, fluid_mask, table)
    if spectral:
        return result
    return spectrum(result, norm_scale)


def dft_tables(length, factor):
    index = jnp.arange(length, dtype=jnp.int32)
    products = index[:, None] * index[None, :] % length
    angles = products.astype(jnp.float32) * (2.0 * math.pi / length)
    return (jnp.cos(angles) * factor, jnp.sin(angles) * factor)


def spectrum(speed_x, norm_scale):
    columns = jnp.transpose(speed_x, (2, 1, 0))
    highest = lax.Precision.HIGHEST
    block = lax.all_to_all(columns, "gx", split_axis=0, concat_axis=2, tiled=True)
    cosine, sine = dft_tables(block.shape[2], norm_scale)
    real_part = jnp.einsum("yzx,xk->yzk", block, cosine, precision=highest)
    imag_part = -jnp.einsum("yzx,xk->yzk", block, sine, precision=highest)
    along_kx = jnp.stack([real_part, imag_part], axis=0)
    block = lax.all_to_all(along_kx, "gz", split_axis=3, concat_axis=2, tiled=True)
    cosine, sine = dft_tables(block.shape[2], 1.0)
    real_in = block[0]
    imag_in = block[1]
    real_part = jnp.einsum("ync,nk->yck", real_in, cosine, precision=highest) + jnp.einsum(
        "ync,nk->yck", imag_in, sine, precision=highest
    )
    imag_part = jnp.einsum("ync,nk->yck", imag_in, cosine, precision=highest) - jnp.einsum(
        "ync,nk->yck", real_in, sine, precision=highest
    )
    return jnp.stack([real_part, imag_part], axis=0)


def solution(mesh):
    placed = (P(None, "gx", "gz", None), P("gx", "gz", None))
    return jax.shard_map(
        shards, mesh=mesh, in_specs=placed, out_specs=P(None, "gx", "gz", None), check_vma=False
    )
```

```python
import functools
import math

import jax
import jax.numpy as jnp
import numpy as np
from jax import lax
from jax.experimental import pallas as pl
from jax.experimental.pallas import tpu as pltpu
from jax.sharding import PartitionSpec as P

VELOCITIES = (
    (0, 0, 0),
    (1, 0, 0),
    (-1, 0, 0),
    (0, 1, 0),
    (0, -1, 0),
    (0, 0, 1),
    (0, 0, -1),
    (1, 1, 0),
    (-1, -1, 0),
    (1, -1, 0),
    (-1, 1, 0),
    (1, 0, 1),
    (-1, 0, -1),
    (1, 0, -1),
    (-1, 0, 1),
    (0, 1, 1),
    (0, -1, -1),
    (0, 1, -1),
    (0, -1, 1),
)
LATTICE_WEIGHTS = (1.0 / 3.0,) + (1.0 / 18.0,) * 6 + (1.0 / 36.0,) * 12
OPPOSITES = (0, 2, 1, 4, 3, 6, 5, 8, 7, 10, 9, 12, 11, 14, 13, 16, 15, 18, 17)
RELAX_TIME = 0.6
BODY_FORCE = 0.0001
SPEED_UNIT = 0.05

CHAIN = (13, 1, 7, 9, 11, 5, 15, 18, 14, 2, 8, 10, 12, 6, 16, 17, 0, 3, 4)
SLOT = {number: CHAIN.index(number) for number in CHAIN}
X_FIRST = {1: 0, -1: 8}
Z_FIRST = {1: 4, -1: 12}
SIDES = ((1, 0), (-1, 0), (0, 1), (0, -1))
DIAGONALS = ((1, 1), (1, -1), (-1, 1), (-1, -1))
DIAGONAL_SLOT = (4, 0, 8, 12)
TOP = 8
MESH = pl.DeviceIdType.MESH


def collide(f, fluid):
    omega = 1.0 / RELAX_TIME
    keep = 1.0 - omega
    plus = {}
    minus = {}
    for i in range(1, 19, 2):
        plus[i] = f[i] + f[i + 1]
        minus[i] = f[i] - f[i + 1]
    density = f[0]
    momentum = [None, None, None]
    for i in range(1, 19, 2):
        density = density + plus[i]
        for axis in range(3):
            c = VELOCITIES[i][axis]
            if c:
                term = minus[i] if c > 0 else -minus[i]
                momentum[axis] = term if momentum[axis] is None else momentum[axis] + term
    inverse = 1.0 / density
    jx, jy, jz = momentum
    square = (jx * jx + jy * jy + jz * jz) * inverse
    base = density - 1.5 * square
    force = density * BODY_FORCE
    out = [None] * 19
    w0 = LATTICE_WEIGHTS[0] * omega
    out[0] = jnp.where(fluid, keep * f[0] + w0 * base, f[0])
    for i in range(1, 19, 2):
        w = LATTICE_WEIGHTS[i]
        cj = None
        for axis in range(3):
            c = VELOCITIES[i][axis]
            if c:
                j = momentum[axis]
                if cj is None:
                    cj = j if c > 0 else -j
                else:
                    cj = cj + j if c > 0 else cj - j
        even = (w * omega) * (base + 4.5 * (cj * cj * inverse))
        odd = (3.0 * w * omega) * cj
        if VELOCITIES[i][0]:
            odd = odd + (3.0 * w * VELOCITIES[i][0]) * force
        out[i] = jnp.where(fluid, keep * f[i] + (even + odd), f[i])
        out[i + 1] = jnp.where(fluid, keep * f[i + 1] + (even - odd), f[i + 1])
    return out


def tables(count_x, count_z, extent_x, extent_z, norm):
    lane = np.arange(128)
    step = (lane // extent_z) % extent_x
    k0 = np.arange(8)[:, None]
    angle = 2.0 * np.pi * k0 * step[None, :] / (count_x * extent_x)
    twiddle = np.concatenate([np.cos(angle), np.sin(angle)], axis=0)
    quarter_cos = np.array([1.0, 0.0, -1.0, 0.0])
    quarter_sin = np.array([0.0, 1.0, 0.0, -1.0])
    k1 = np.arange(4)[:, None]
    xl = np.arange(4)[None, :]
    c = quarter_cos[(k1 * xl) % 4]
    s = quarter_sin[(k1 * xl) % 4]
    block = np.zeros((4, 2, 2, 4))
    block[:, 0, 0] = c
    block[:, 0, 1] = s
    block[:, 1, 1] = c
    block[:, 1, 0] = -s
    first = np.einsum("kpqx,zw->kpzqxw", block, np.eye(extent_z)).reshape(128, 128)
    full_z = count_z * extent_z
    z = np.arange(full_z)
    angle = 2.0 * np.pi * ((z[:, None] * z[None, :]) % full_z) / full_z
    c = np.cos(angle) * norm
    s = np.sin(angle) * norm
    second = np.zeros((2, full_z, 2, full_z))
    second[0, :, 0] = c
    second[1, :, 0] = s
    second[1, :, 1] = c
    second[0, :, 1] = -s
    second = second.reshape(2, count_z, extent_z, 2, full_z).transpose(1, 0, 2, 3, 4)
    second = second.reshape(128, 128)
    return np.concatenate([twiddle, first, second], axis=0).astype(np.float32)


def halves(value):
    high = value.astype(jnp.bfloat16)
    low = (value - high.astype(jnp.float32)).astype(jnp.bfloat16)
    return high, low


def eight_point(v):
    r = math.sqrt(0.5)
    a0, a1, a2, a3 = v[0] + v[4], v[1] + v[5], v[2] + v[6], v[3] + v[7]
    b0, b1, b2, b3 = v[0] - v[4], v[1] - v[5], v[2] - v[6], v[3] - v[7]
    e0, e1 = a0 + a2, a1 + a3
    d, t = r * (b1 - b3), r * (b1 + b3)
    re = [e0 + e1, b0 + d, a0 - a2, b0 - d, e0 - e1]
    im = [None, -b2 - t, a3 - a1, b2 - t, None]
    re = re + [re[3], re[2], re[1]]
    im = im + [-im[3], -im[2], -im[1]]
    return re, im


def kernel(spectral, populations, fluid_mask, table, *rest):
    (out_ref, held, mask_i, rolled, plain, walls, edges_out, edges_in, corners_out, corners_in,
     sums_in, rims_out, rims_in, tips_out, tips_in, density, forward, ahead, behind,
     in_sem, halo_send, halo_recv, mask_send, mask_recv) = rest[:24]
    if spectral:
        (ux, sent_x, got_x, left, sent_z, got_z, weights,
         table_sem, x_send, x_recv, z_send, z_recv) = rest[24:]
    extent_x, extent_z, height = fluid_mask.shape
    last = extent_x - 1
    count_x, count_z = lax.axis_size("gx"), lax.axis_size("gz")
    mx, mz = lax.axis_index("gx"), lax.axis_index("gz")

    def shifted_x(step):
        return lax.rem(mx + step + count_x, count_x)

    def shifted_z(step):
        return lax.rem(mz + step + count_z, count_z)

    inner = pl.ds(TOP, extent_z)
    outer_rows = (0, last)
    inner_rows = tuple(range(1, last))

    mask_copy = pltpu.make_async_copy(fluid_mask, mask_i, in_sem.at[extent_x])
    mask_copy.start()
    fetches = {}
    for x in outer_rows + inner_rows:
        fetches[x] = pltpu.make_async_copy(populations.at[:, x], held.at[x], in_sem.at[x])
        fetches[x].start()

    barrier = pltpu.get_barrier_semaphore()
    partners = [(shifted_x(dx), shifted_z(dz)) for dx, dz in SIDES + DIAGONALS]
    if spectral:
        partners += [(shifted_x(p), mz) for p in range(2, count_x - 1)]
        partners += [(mx, shifted_z(p)) for p in range(2, count_z - 1)]
    for partner in partners:
        pl.semaphore_signal(barrier, inc=1, device_id=partner, device_id_type=MESH)
    if spectral:
        table_copy = pltpu.make_async_copy(table, weights, table_sem.at[0])
        table_copy.start()

    lanes = lax.broadcasted_iota(jnp.int32, (extent_z, height), 1)
    rows = lax.broadcasted_iota(jnp.int32, (extent_z, height), 0)

    def edge_of(value, cz):
        row = extent_z - 1 if cz > 0 else 0
        return value[row : row + 1, :]

    def first_collision(x):
        fetches[x].wait()
        solid = mask_i[x].astype(jnp.float32)
        walls[0, 1 + x, inner, :] = solid
        for side, cz in enumerate((1, -1)):
            edges_out[side, pl.ds(5 * extent_x + x, 1), :] = edge_of(solid, cz)
        for diagonal, (cx, cz) in enumerate(DIAGONALS):
            if x == (last if cx > 0 else 0):
                corners_out[diagonal, pl.ds(1, 1), :] = edge_of(solid, cz)
        g = collide([held[x, number] for number in range(19)], solid > 0)
        for number in range(19):
            cx, cy, cz = VELOCITIES[number]
            value = g[number]
            if cy:
                plain[number, x] = value
                value = pltpu.roll(value, cy % height, 1)
            slot = SLOT[number]
            rolled[slot, 1 + x, inner, :] = value
            if cz:
                order = (slot - Z_FIRST[cz]) % 16
                edge = edge_of(value, cz)
                edges_out[0 if cz > 0 else 1, pl.ds(order * extent_x + x, 1), :] = edge
                if cx and x == (last if cx > 0 else 0):
                    corners_out[DIAGONALS.index((cx, cz)), pl.ds(0, 1), :] = edge

    def send(source, target, send_sem, recv_sem, dx, dz):
        copy = pltpu.make_async_remote_copy(
            src_ref=source,
            dst_ref=target,
            send_sem=send_sem,
            recv_sem=recv_sem,
            device_id=(shifted_x(dx), shifted_z(dz)),
            device_id_type=MESH,
        )
        copy.start()
        return copy

    mask_copy.wait()
    for x in outer_rows:
        first_collision(x)
    pl.semaphore_wait(barrier, len(partners))
    x_sides, z_sides, corners = [], [], []
    for side, dx in enumerate((1, -1)):
        here, there = (extent_x, 0) if dx > 0 else (1, extent_x + 1)
        group = pl.ds(X_FIRST[dx], 5)
        x_sides.append(
            send(rolled.at[group, here, inner], rolled.at[group, there, inner],
                 halo_send.at[0, side], halo_recv.at[0, side], dx, 0)
        )
        x_sides.append(
            send(walls.at[0, here, inner], walls.at[0, there, inner],
                 mask_send.at[side], mask_recv.at[side], dx, 0)
        )
    for x in inner_rows:
        first_collision(x)
    for side, dz in enumerate((1, -1)):
        z_sides.append(
            send(edges_out.at[side], edges_in.at[side],
                 halo_send.at[0, 2 + side], halo_recv.at[0, 2 + side], 0, dz)
        )
    for diagonal, (dx, dz) in enumerate(DIAGONALS):
        corners.append(
            send(corners_out.at[diagonal], corners_in.at[diagonal],
                 halo_send.at[0, 4 + diagonal], halo_recv.at[0, 4 + diagonal], dx, dz)
        )

    around = lax.broadcasted_iota(jnp.int32, (extent_z + 2 * TOP, height), 1)

    def shift_walls(plane):
        value = walls[0, plane]
        walls[1, plane] = jnp.where(around == 0, 0.0, pltpu.roll(value, 1, 1))
        walls[2, plane] = jnp.where(around == height - 1, 0.0, pltpu.roll(value, height - 1, 1))

    def wall_from(number, x):
        cx, cy, cz = VELOCITIES[number]
        return walls[(0, 1, 2)[cy], 1 + x - cx, pl.ds(TOP - cz, extent_z), :] > 0

    def streamed(x, fluid):
        owned = []
        for number in range(19):
            if VELOCITIES[number][1]:
                owned.append(plain[number, x])
            else:
                owned.append(rolled[SLOT[number], 1 + x, inner, :])
        f = [owned[0]]
        for number in range(1, 19):
            cx, cy, cz = VELOCITIES[number]
            value = rolled[SLOT[number], 1 + x - cx, pl.ds(TOP - cz, extent_z), :]
            arrived = jnp.where(wall_from(number, x), value, owned[OPPOSITES[number]])
            f.append(jnp.where(fluid, arrived, owned[number]))
        return f

    rims = {}

    def second_collision(x):
        fluid = walls[0, 1 + x, inner, :] > 0
        g = collide(streamed(x, fluid), fluid)
        for number in range(19):
            held[x, number] = g[number]
        leaving = {}
        for number in range(1, 19):
            cx, cy, cz = VELOCITIES[number]
            value = jnp.where(fluid, g[number], 0.0)
            if cy:
                value = pltpu.roll(value, cy % height, 1)
                value = jnp.where(lanes == (0 if cy > 0 else height - 1), 0.0, value)
            leaving[cx, cz] = leaving[cx, cz] + value if (cx, cz) in leaving else value
        for cx, keep in ((1, ahead), (-1, behind), (0, None)):
            total = leaving[cx, 0]
            for cz in (1, -1):
                value = leaving[cx, cz]
                rims[x, cx, cz] = edge_of(value, cz)
                moved = pltpu.roll(value, cz % extent_z, 0)
                total = total + jnp.where(rows == (0 if cz > 0 else extent_z - 1), 0.0, moved)
            if keep is None:
                density[x] = g[0] + total
            else:
                keep[x] = total

    def bounced(x):
        sums = {}
        for number in range(1, 19):
            cx = VELOCITIES[number][0]
            value = jnp.where(wall_from(number, x), 0.0, held[x, OPPOSITES[number]])
            sums[cx] = sums[cx] + value if cx in sums else value
        density[x] = density[x] + (sums[0] + sums[1] + sums[-1])
        forward[x] = sums[1] - sums[-1]

    for copy in z_sides:
        copy.wait_recv()
    for side, cz in enumerate((1, -1)):
        row = TOP - 1 if cz > 0 else TOP + extent_z
        for x in range(extent_x):
            for order in range(5):
                rolled[(Z_FIRST[cz] + order) % 16, 1 + x, pl.ds(row, 1), :] = edges_in[
                    side, pl.ds(order * extent_x + x, 1), :
                ]
            walls[0, 1 + x, pl.ds(row, 1), :] = edges_in[side, pl.ds(5 * extent_x + x, 1), :]
    for x in range(extent_x):
        shift_walls(1 + x)
    for x in inner_rows:
        second_collision(x)
        bounced(x)
    for copy in x_sides + corners:
        copy.wait_recv()
    for diagonal, (cx, cz) in enumerate(DIAGONALS):
        plane = 0 if cx > 0 else extent_x + 1
        row = TOP - 1 if cz > 0 else TOP + extent_z
        rolled[DIAGONAL_SLOT[diagonal], plane, pl.ds(row, 1), :] = corners_in[diagonal, pl.ds(0, 1), :]
        walls[0, plane, pl.ds(row, 1), :] = corners_in[diagonal, pl.ds(1, 1), :]
    for plane in (0, extent_x + 1):
        shift_walls(plane)
    for x in outer_rows:
        second_collision(x)

    sums = []
    for side, (dx, x, keep) in enumerate(((1, last, ahead), (-1, 0, behind))):
        sums.append(
            send(keep.at[x], sums_in.at[side],
                 halo_send.at[1, side], halo_recv.at[1, side], dx, 0)
        )
    for side, dz in enumerate((1, -1)):
        for x in range(extent_x):
            total, along = rims[x, 0, dz], None
            if x > 0:
                total, along = total + rims[x - 1, 1, dz], rims[x - 1, 1, dz]
            if x < last:
                back = rims[x + 1, -1, dz]
                total, along = total + back, -back if along is None else along - back
            rims_out[side, pl.ds(x, 1), :] = total
            rims_out[side, pl.ds(extent_x + x, 1), :] = along
        sums.append(
            send(rims_out.at[side], rims_in.at[side],
                 halo_send.at[1, 2 + side], halo_recv.at[1, 2 + side], 0, dz)
        )
    for diagonal, (dx, dz) in enumerate(DIAGONALS):
        tips_out[diagonal] = rims[last if dx > 0 else 0, dx, dz]
        sums.append(
            send(tips_out.at[diagonal], tips_in.at[diagonal],
                 halo_send.at[1, 4 + diagonal], halo_recv.at[1, 4 + diagonal], dx, dz)
        )
    for x in outer_rows:
        bounced(x)
    for x in range(extent_x):
        total, along = density[x], forward[x]
        if x > 0:
            total, along = total + ahead[x - 1], along + ahead[x - 1]
        if x < last:
            total, along = total + behind[x + 1], along - behind[x + 1]
        density[x] = total
        forward[x] = along
    for copy in sums:
        copy.wait_recv()
    for side, dz in enumerate((1, -1)):
        row = 0 if dz > 0 else extent_z - 1
        for x in range(extent_x):
            total = rims_in[side, pl.ds(x, 1), :]
            along = rims_in[side, pl.ds(extent_x + x, 1), :]
            for diagonal, (cx, cz) in enumerate(DIAGONALS):
                if cz == dz and x == (0 if cx > 0 else last):
                    total = total + tips_in[diagonal]
                    along = along + tips_in[diagonal] if cx > 0 else along - tips_in[diagonal]
            density[x, pl.ds(row, 1), :] = density[x, pl.ds(row, 1), :] + total
            forward[x, pl.ds(row, 1), :] = forward[x, pl.ds(row, 1), :] + along
    for x in range(extent_x):
        total, along = density[x], forward[x]
        if x == 0:
            total, along = total + sums_in[0], along + sums_in[0]
        if x == last:
            total, along = total + sums_in[1], along - sums_in[1]
        speed = jnp.where(walls[0, 1 + x, inner, :] > 0, along / total, 0.0)
        if spectral:
            ux[pl.ds(x * extent_z, extent_z), :] = speed
        else:
            out_ref[x] = speed

    if spectral:
        whole = ux[...]
        both = jnp.concatenate([whole, pltpu.roll(whole, height - 8, 1)], axis=0)
        turned = both.T
        for a in range(count_x):
            sent_x[a] = turned[16 * a : 16 * a + 8, :]
        x_copies = []
        for p in range(1, count_x):
            there = shifted_x(p)
            copy = pltpu.make_async_remote_copy(
                src_ref=sent_x.at[there],
                dst_ref=got_x.at[mx],
                send_sem=x_send.at[p],
                recv_sem=x_recv.at[p],
                device_id=(there, mz),
                device_id_type=MESH,
            )
            copy.start()
            x_copies.append(copy)
        got_x[mx] = sent_x[mx]
        table_copy.wait()
        first = weights[pl.ds(16, 128), :].astype(jnp.bfloat16)
        for copy in x_copies:
            copy.wait_recv()
        re, im = eight_point([got_x[s] for s in range(8)])
        low_lanes = lax.broadcasted_iota(jnp.int32, (8, 128), 1) < 64
        for k in range(8):
            c = weights[pl.ds(k, 1), :]
            s = weights[pl.ds(8 + k, 1), :]
            if im[k] is None:
                real, imag = re[k] * c, -re[k] * s
            else:
                real, imag = re[k] * c + im[k] * s, im[k] * c - re[k] * s
            left[pl.ds(k, 8, stride=8), :] = jnp.where(low_lanes, real, pltpu.roll(imag, 64, 1))
            left[pl.ds(64 + k, 8, stride=8), :] = jnp.where(low_lanes, pltpu.roll(real, 64, 1), imag)
        high, low = halves(left[...])
        contract = (((1,), (1,)), ((), ()))
        along = lax.dot_general(
            jnp.concatenate([first, first], axis=1),
            jnp.concatenate([high, low], axis=1),
            contract,
            preferred_element_type=jnp.float32,
        )
        for b in range(count_z):
            sent_z[b] = along[32 * b : 32 * b + 32, :]
        z_copies = []
        for p in range(1, count_z):
            there = shifted_z(p)
            copy = pltpu.make_async_remote_copy(
                src_ref=sent_z.at[there],
                dst_ref=got_z.at[mz],
                send_sem=z_send.at[p],
                recv_sem=z_recv.at[p],
                device_id=(mx, there),
                device_id_type=MESH,
            )
            copy.start()
            z_copies.append(copy)
        got_z[mz] = sent_z[mz]
        second_high, second_low = halves(weights[pl.ds(144, 128), :])
        second_twice = jnp.concatenate([second_high, second_high], axis=0)
        for copy in z_copies:
            copy.wait_recv()
        lines = got_z[...].reshape(128, 128).T
        high, low = halves(lines)
        result = jnp.dot(
            jnp.concatenate([high, low], axis=1), second_twice, preferred_element_type=jnp.float32
        ) + jnp.dot(high, second_low, preferred_element_type=jnp.float32)
        out_ref[0] = result[:, :64].reshape(16, 8, 64)
        out_ref[1] = result[:, 64:].reshape(16, 8, 64)
        for copy in x_copies + z_copies:
            copy.wait_send()
    for copy in x_sides + z_sides + corners + sums:
        copy.wait_send()


def shards(populations, fluid_mask):
    number, extent_x, extent_z, height = populations.shape
    count_x, count_z = lax.axis_size("gx"), lax.axis_size("gz")
    full_x, full_z = count_x * extent_x, count_z * extent_z
    norm_scale = 1.0 / (math.sqrt(full_x * full_z) * SPEED_UNIT)
    spectral = (count_x, count_z, extent_x, extent_z, height) == (8, 4, 4, 16, 128)
    if spectral:
        table = jnp.asarray(tables(count_x, count_z, extent_x, extent_z, norm_scale))
    else:
        table = jnp.zeros((8, 128), jnp.float32)
    f32 = jnp.float32
    padded = (extent_x + 2, extent_z + 2 * TOP, height)
    edge_rows = 6 * extent_x
    dma = pltpu.SemaphoreType.DMA
    scratch = [
        pltpu.VMEM((extent_x, 19, extent_z, height), f32),
        pltpu.VMEM((extent_x, extent_z, height), jnp.int32),
        pltpu.VMEM((19,) + padded, f32),
        pltpu.VMEM((19, extent_x, extent_z, height), f32),
        pltpu.VMEM((3,) + padded, f32),
        pltpu.VMEM((2, edge_rows, height), f32),
        pltpu.VMEM((2, edge_rows, height), f32),
        pltpu.VMEM((4, 2, height), f32),
        pltpu.VMEM((4, 2, height), f32),
        pltpu.VMEM((2, extent_z, height), f32),
        pltpu.VMEM((2, 2 * extent_x, height), f32),
        pltpu.VMEM((2, 2 * extent_x, height), f32),
        pltpu.VMEM((4, 1, height), f32),
        pltpu.VMEM((4, 1, height), f32),
        pltpu.VMEM((extent_x, extent_z, height), f32),
        pltpu.VMEM((extent_x, extent_z, height), f32),
        pltpu.VMEM((extent_x, extent_z, height), f32),
        pltpu.VMEM((extent_x, extent_z, height), f32),
        dma((extent_x + 1,)),
        dma((2, 8)),
        dma((2, 8)),
        dma((2,)),
        dma((2,)),
    ]
    if spectral:
        scratch += [
            pltpu.VMEM((64, 128), f32),
            pltpu.VMEM((8, 8, 128), f32),
            pltpu.VMEM((8, 8, 128), f32),
            pltpu.VMEM((128, 128), f32),
            pltpu.VMEM((4, 32, 128), f32),
            pltpu.VMEM((4, 32, 128), f32),
            pltpu.VMEM(table.shape, f32),
            dma((1,)),
            dma((8,)),
            dma((8,)),
            dma((4,)),
            dma((4,)),
        ]
        out_shape = jax.ShapeDtypeStruct((2, 16, 8, 64), f32)
    else:
        out_shape = jax.ShapeDtypeStruct((extent_x, extent_z, height), f32)
    in_hbm = pl.BlockSpec(memory_space=pltpu.HBM)
    result = pl.pallas_call(
        functools.partial(kernel, spectral),
        out_shape=out_shape,
        in_specs=[in_hbm] * 3,
        out_specs=pl.BlockSpec(memory_space=pltpu.VMEM),
        scratch_shapes=scratch,
        compiler_params=pltpu.CompilerParams(
            collective_id=0, has_side_effects=True, vmem_limit_bytes=32 * 1024 * 1024
        ),
    )(*(pltpu.with_memory_space_constraint(array, pltpu.HBM) for array in (populations, fluid_mask, table)))
    if spectral:
        return result
    return spectrum(result, norm_scale)


def dft_tables(length, factor):
    index = jnp.arange(length, dtype=jnp.int32)
    products = index[:, None] * index[None, :] % length
    angles = products.astype(jnp.float32) * (2.0 * math.pi / length)
    return (jnp.cos(angles) * factor, jnp.sin(angles) * factor)


def spectrum(speed_x, norm_scale):
    columns = jnp.transpose(speed_x, (2, 1, 0))
    highest = lax.Precision.HIGHEST
    block = lax.all_to_all(columns, "gx", split_axis=0, concat_axis=2, tiled=True)
    cosine, sine = dft_tables(block.shape[2], norm_scale)
    real_part = jnp.einsum("yzx,xk->yzk", block, cosine, precision=highest)
    imag_part = -jnp.einsum("yzx,xk->yzk", block, sine, precision=highest)
    along_kx = jnp.stack([real_part, imag_part], axis=0)
    block = lax.all_to_all(along_kx, "gz", split_axis=3, concat_axis=2, tiled=True)
    cosine, sine = dft_tables(block.shape[2], 1.0)
    real_in = block[0]
    imag_in = block[1]
    real_part = jnp.einsum("ync,nk->yck", real_in, cosine, precision=highest) + jnp.einsum(
        "ync,nk->yck", imag_in, sine, precision=highest
    )
    imag_part = jnp.einsum("ync,nk->yck", imag_in, cosine, precision=highest) - jnp.einsum(
        "ync,nk->yck", real_in, sine, precision=highest
    )
    return jnp.stack([real_part, imag_part], axis=0)


def solution(mesh):
    placed = (P(None, "gx", "gz", None), P("gx", "gz", None))
    return jax.shard_map(
        shards, mesh=mesh, in_specs=placed, out_specs=P(None, "gx", "gz", None), check_vma=False
    )
```

```python
import functools
import math

import jax
import jax.numpy as jnp
import numpy as np
from jax import lax
from jax.experimental import pallas as pl
from jax.experimental.pallas import tpu as pltpu
from jax.sharding import PartitionSpec as P

VELOCITIES = (
    (0, 0, 0),
    (1, 0, 0),
    (-1, 0, 0),
    (0, 1, 0),
    (0, -1, 0),
    (0, 0, 1),
    (0, 0, -1),
    (1, 1, 0),
    (-1, -1, 0),
    (1, -1, 0),
    (-1, 1, 0),
    (1, 0, 1),
    (-1, 0, -1),
    (1, 0, -1),
    (-1, 0, 1),
    (0, 1, 1),
    (0, -1, -1),
    (0, 1, -1),
    (0, -1, 1),
)
LATTICE_WEIGHTS = (1.0 / 3.0,) + (1.0 / 18.0,) * 6 + (1.0 / 36.0,) * 12
OPPOSITES = (0, 2, 1, 4, 3, 6, 5, 8, 7, 10, 9, 12, 11, 14, 13, 16, 15, 18, 17)
RELAX_TIME = 0.6
BODY_FORCE = 0.0001
SPEED_UNIT = 0.05

CHAIN = (13, 1, 7, 9, 11, 5, 15, 18, 14, 2, 8, 10, 12, 6, 16, 17, 0, 3, 4)
SLOT = {number: CHAIN.index(number) for number in CHAIN}
X_FIRST = {1: 0, -1: 8}
Z_FIRST = {1: 4, -1: 12}
SIDES = ((1, 0), (-1, 0), (0, 1), (0, -1))
DIAGONALS = ((1, 1), (1, -1), (-1, 1), (-1, -1))
DIAGONAL_SLOT = (4, 0, 8, 12)
RIM = {(cx, cz): 2 * (cx + 1) + (cz + 1) // 2 for cx in (-1, 0, 1) for cz in (-1, 1)}
TOP = 8
MESH = pl.DeviceIdType.MESH


def collide(f, fluid):
    omega = 1.0 / RELAX_TIME
    keep = 1.0 - omega
    plus = {}
    minus = {}
    for i in range(1, 19, 2):
        plus[i] = f[i] + f[i + 1]
        minus[i] = f[i] - f[i + 1]
    density = f[0]
    momentum = [None, None, None]
    for i in range(1, 19, 2):
        density = density + plus[i]
        for axis in range(3):
            c = VELOCITIES[i][axis]
            if c:
                term = minus[i] if c > 0 else -minus[i]
                momentum[axis] = term if momentum[axis] is None else momentum[axis] + term
    inverse = 1.0 / density
    jx, jy, jz = momentum
    square = (jx * jx + jy * jy + jz * jz) * inverse
    base = density - 1.5 * square
    force = density * BODY_FORCE
    out = [None] * 19
    w0 = LATTICE_WEIGHTS[0] * omega
    out[0] = jnp.where(fluid, keep * f[0] + w0 * base, f[0])
    for i in range(1, 19, 2):
        w = LATTICE_WEIGHTS[i]
        cj = None
        for axis in range(3):
            c = VELOCITIES[i][axis]
            if c:
                j = momentum[axis]
                if cj is None:
                    cj = j if c > 0 else -j
                else:
                    cj = cj + j if c > 0 else cj - j
        even = (w * omega) * (base + 4.5 * (cj * cj * inverse))
        odd = (3.0 * w * omega) * cj
        if VELOCITIES[i][0]:
            odd = odd + (3.0 * w * VELOCITIES[i][0]) * force
        out[i] = jnp.where(fluid, keep * f[i] + (even + odd), f[i])
        out[i + 1] = jnp.where(fluid, keep * f[i + 1] + (even - odd), f[i + 1])
    return out


def tables(count_x, count_z, extent_x, extent_z, norm):
    lane = np.arange(128)
    step = (lane // extent_z) % extent_x
    k0 = np.arange(8)[:, None]
    angle = 2.0 * np.pi * k0 * step[None, :] / (count_x * extent_x)
    twiddle = np.concatenate([np.cos(angle), np.sin(angle)], axis=0)
    quarter_cos = np.array([1.0, 0.0, -1.0, 0.0])
    quarter_sin = np.array([0.0, 1.0, 0.0, -1.0])
    k1 = np.arange(4)[:, None]
    xl = np.arange(4)[None, :]
    c = quarter_cos[(k1 * xl) % 4]
    s = quarter_sin[(k1 * xl) % 4]
    block = np.zeros((4, 2, 2, 4))
    block[:, 0, 0] = c
    block[:, 0, 1] = s
    block[:, 1, 1] = c
    block[:, 1, 0] = -s
    first = np.einsum("kpqx,zw->kpzqxw", block, np.eye(extent_z)).reshape(128, 128)
    full_z = count_z * extent_z
    z = np.arange(full_z)
    angle = 2.0 * np.pi * ((z[:, None] * z[None, :]) % full_z) / full_z
    c = np.cos(angle) * norm
    s = np.sin(angle) * norm
    second = np.zeros((2, full_z, 2, full_z))
    second[0, :, 0] = c
    second[1, :, 0] = s
    second[1, :, 1] = c
    second[0, :, 1] = -s
    second = second.reshape(2, count_z, extent_z, 2, full_z).transpose(1, 0, 2, 3, 4)
    second = second.reshape(128, 128)
    return np.concatenate([twiddle, first, second], axis=0).astype(np.float32)


def halves(value):
    high = value.astype(jnp.bfloat16)
    low = (value - high.astype(jnp.float32)).astype(jnp.bfloat16)
    return high, low


def eight_point(v):
    r = math.sqrt(0.5)
    a0, a1, a2, a3 = v[0] + v[4], v[1] + v[5], v[2] + v[6], v[3] + v[7]
    b0, b1, b2, b3 = v[0] - v[4], v[1] - v[5], v[2] - v[6], v[3] - v[7]
    e0, e1 = a0 + a2, a1 + a3
    d, t = r * (b1 - b3), r * (b1 + b3)
    re = [e0 + e1, b0 + d, a0 - a2, b0 - d, e0 - e1]
    im = [None, -b2 - t, a3 - a1, b2 - t, None]
    re = re + [re[3], re[2], re[1]]
    im = im + [-im[3], -im[2], -im[1]]
    return re, im


def kernel(spectral, populations, fluid_mask, table, *rest):
    (out_ref, held, mask_i, rolled, plain, walls, edges_out, edges_in, corners_out, corners_in,
     sums_in, rims_out, rims_in, tips_out, tips_in, density, forward, ahead, behind, rims,
     in_sem, halo_send, halo_recv, mask_send, mask_recv) = rest[:25]
    if spectral:
        (ux, sent_x, got_x, left, sent_z, got_z, weights,
         table_sem, x_send, x_recv, z_send, z_recv) = rest[25:]
    extent_x, extent_z, height = fluid_mask.shape
    last = extent_x - 1
    count_x, count_z = lax.axis_size("gx"), lax.axis_size("gz")
    mx, mz = lax.axis_index("gx"), lax.axis_index("gz")

    def shifted_x(step):
        return lax.rem(mx + step + count_x, count_x)

    def shifted_z(step):
        return lax.rem(mz + step + count_z, count_z)

    inner = pl.ds(TOP, extent_z)

    def fetch(x):
        return pltpu.make_async_copy(populations.at[:, x], held.at[x], in_sem.at[x])

    mask_copy = pltpu.make_async_copy(fluid_mask, mask_i, in_sem.at[extent_x])
    mask_copy.start()
    for k in range(extent_x):
        fetch((extent_x - k) % extent_x).start()

    barrier = pltpu.get_barrier_semaphore()
    partners = [(shifted_x(dx), shifted_z(dz)) for dx, dz in SIDES + DIAGONALS]
    if spectral:
        partners += [(shifted_x(p), mz) for p in range(2, count_x - 1)]
        partners += [(mx, shifted_z(p)) for p in range(2, count_z - 1)]
    for partner in partners:
        pl.semaphore_signal(barrier, inc=1, device_id=partner, device_id_type=MESH)
    if spectral:
        table_copy = pltpu.make_async_copy(table, weights, table_sem.at[0])
        table_copy.start()

    lanes = lax.broadcasted_iota(jnp.int32, (extent_z, height), 1)
    rows = lax.broadcasted_iota(jnp.int32, (extent_z, height), 0)

    def edge_of(value, cz):
        row = extent_z - 1 if cz > 0 else 0
        return value[row : row + 1, :]

    def remote(source, target, send_sem, recv_sem, dx, dz):
        return pltpu.make_async_remote_copy(
            src_ref=source,
            dst_ref=target,
            send_sem=send_sem,
            recv_sem=recv_sem,
            device_id=(shifted_x(dx), shifted_z(dz)),
            device_id_type=MESH,
        )

    def send(*arguments):
        copy = remote(*arguments)
        copy.start()
        return copy

    x_sides = []
    for side, dx in enumerate((1, -1)):
        here, there = (extent_x, 0) if dx > 0 else (1, extent_x + 1)
        group = pl.ds(X_FIRST[dx], 5)
        x_sides.append(
            remote(rolled.at[group, here, inner], rolled.at[group, there, inner],
                   halo_send.at[0, side], halo_recv.at[0, side], dx, 0)
        )
        x_sides.append(
            remote(walls.at[0, here, inner], walls.at[0, there, inner],
                   mask_send.at[side], mask_recv.at[side], dx, 0)
        )

    mask_copy.wait()
    for x in range(extent_x):
        walls[0, 1 + x, inner, :] = mask_i[x].astype(jnp.float32)

    def first_collision(k, carry):
        x = lax.rem(extent_x - k, extent_x)
        fetch(x).wait()
        g = collide([held[x, number] for number in range(19)], walls[0, 1 + x, inner, :] > 0)
        for number in range(19):
            cy = VELOCITIES[number][1]
            value = g[number]
            if cy:
                plain[number, x] = value
                value = pltpu.roll(value, cy % height, 1)
            rolled[SLOT[number], 1 + x, inner, :] = value

        @pl.when(k == 1)
        def _():
            pl.semaphore_wait(barrier, len(partners))
            for copy in x_sides:
                copy.start()

        return carry

    lax.fori_loop(0, extent_x, first_collision, 0)
    z_sides, corners = [], []
    for side, cz in enumerate((1, -1)):
        row = pl.ds(TOP + extent_z - 1 if cz > 0 else TOP, 1)
        for x in range(extent_x):
            for order in range(5):
                edges_out[side, pl.ds(order * extent_x + x, 1), :] = rolled[
                    (Z_FIRST[cz] + order) % 16, 1 + x, row, :
                ]
            edges_out[side, pl.ds(5 * extent_x + x, 1), :] = walls[0, 1 + x, row, :]
        z_sides.append(
            send(edges_out.at[side], edges_in.at[side],
                 halo_send.at[0, 2 + side], halo_recv.at[0, 2 + side], 0, cz)
        )
    for diagonal, (dx, dz) in enumerate(DIAGONALS):
        row = pl.ds(TOP + extent_z - 1 if dz > 0 else TOP, 1)
        plane = extent_x if dx > 0 else 1
        corners_out[diagonal, pl.ds(0, 1), :] = rolled[DIAGONAL_SLOT[diagonal], plane, row, :]
        corners_out[diagonal, pl.ds(1, 1), :] = walls[0, plane, row, :]
        corners.append(
            send(corners_out.at[diagonal], corners_in.at[diagonal],
                 halo_send.at[0, 4 + diagonal], halo_recv.at[0, 4 + diagonal], dx, dz)
        )

    around = lax.broadcasted_iota(jnp.int32, (extent_z + 2 * TOP, height), 1)

    def shift_walls(plane):
        value = walls[0, plane]
        walls[1, plane] = jnp.where(around == 0, 0.0, pltpu.roll(value, 1, 1))
        walls[2, plane] = jnp.where(around == height - 1, 0.0, pltpu.roll(value, height - 1, 1))

    def wall_from(number, x):
        cx, cy, cz = VELOCITIES[number]
        return walls[(0, 1, 2)[cy], 1 + x - cx, pl.ds(TOP - cz, extent_z), :] > 0

    def second_collision(k, carry):
        x = lax.rem(k + 1, extent_x)

        @pl.when(k == extent_x - 2)
        def _():
            for copy in x_sides + corners:
                copy.wait_recv()
            for diagonal, (cx, cz) in enumerate(DIAGONALS):
                plane = 0 if cx > 0 else extent_x + 1
                row = pl.ds(TOP - 1 if cz > 0 else TOP + extent_z, 1)
                rolled[DIAGONAL_SLOT[diagonal], plane, row, :] = corners_in[diagonal, pl.ds(0, 1), :]
                walls[0, plane, row, :] = corners_in[diagonal, pl.ds(1, 1), :]
            for plane in (0, extent_x + 1):
                shift_walls(plane)

        fluid = walls[0, 1 + x, inner, :] > 0
        owned = []
        for number in range(19):
            if VELOCITIES[number][1]:
                owned.append(plain[number, x])
            else:
                owned.append(rolled[SLOT[number], 1 + x, inner, :])
        f = [owned[0]]
        for number in range(1, 19):
            cx, cy, cz = VELOCITIES[number]
            value = rolled[SLOT[number], 1 + x - cx, pl.ds(TOP - cz, extent_z), :]
            arrived = jnp.where(wall_from(number, x), value, owned[OPPOSITES[number]])
            f.append(jnp.where(fluid, arrived, owned[number]))
        g = collide(f, fluid)
        leaving = {}
        turned_back = {}
        for number in range(1, 19):
            cx, cy, cz = VELOCITIES[number]
            value = jnp.where(fluid, g[number], 0.0)
            if cy:
                value = pltpu.roll(value, cy % height, 1)
                value = jnp.where(lanes == (0 if cy > 0 else height - 1), 0.0, value)
            leaving[cx, cz] = leaving[cx, cz] + value if (cx, cz) in leaving else value
            value = jnp.where(wall_from(number, x), 0.0, g[OPPOSITES[number]])
            turned_back[cx] = turned_back[cx] + value if cx in turned_back else value
        for cx, keep in ((1, ahead), (-1, behind), (0, None)):
            total = leaving[cx, 0]
            for cz in (1, -1):
                value = leaving[cx, cz]
                rims[RIM[cx, cz], x] = edge_of(value, cz)
                moved = pltpu.roll(value, cz % extent_z, 0)
                total = total + jnp.where(rows == (0 if cz > 0 else extent_z - 1), 0.0, moved)
            if keep is None:
                density[x] = (g[0] + total) + (turned_back[0] + turned_back[1] + turned_back[-1])
            else:
                keep[x] = total
        forward[x] = turned_back[1] - turned_back[-1]
        return carry

    for copy in z_sides:
        copy.wait_recv()
    for side, cz in enumerate((1, -1)):
        row = pl.ds(TOP - 1 if cz > 0 else TOP + extent_z, 1)
        for x in range(extent_x):
            for order in range(5):
                rolled[(Z_FIRST[cz] + order) % 16, 1 + x, row, :] = edges_in[
                    side, pl.ds(order * extent_x + x, 1), :
                ]
            walls[0, 1 + x, row, :] = edges_in[side, pl.ds(5 * extent_x + x, 1), :]

    def shift_inner(plane, carry):
        shift_walls(plane)
        return carry

    lax.fori_loop(1, 1 + extent_x, shift_inner, 0)
    lax.fori_loop(0, extent_x, second_collision, 0)

    sums = []
    for side, (dx, x, keep) in enumerate(((1, last, ahead), (-1, 0, behind))):
        sums.append(
            send(keep.at[x], sums_in.at[side],
                 halo_send.at[1, side], halo_recv.at[1, side], dx, 0)
        )
    for side, dz in enumerate((1, -1)):
        for x in range(extent_x):
            total, along = rims[RIM[0, dz], x], None
            if x > 0:
                total, along = total + rims[RIM[1, dz], x - 1], rims[RIM[1, dz], x - 1]
            if x < last:
                back = rims[RIM[-1, dz], x + 1]
                total, along = total + back, -back if along is None else along - back
            rims_out[side, pl.ds(x, 1), :] = total
            rims_out[side, pl.ds(extent_x + x, 1), :] = along
        sums.append(
            send(rims_out.at[side], rims_in.at[side],
                 halo_send.at[1, 2 + side], halo_recv.at[1, 2 + side], 0, dz)
        )
    for diagonal, (dx, dz) in enumerate(DIAGONALS):
        tips_out[diagonal] = rims[RIM[dx, dz], last if dx > 0 else 0]
        sums.append(
            send(tips_out.at[diagonal], tips_in.at[diagonal],
                 halo_send.at[1, 4 + diagonal], halo_recv.at[1, 4 + diagonal], dx, dz)
        )
    for x in range(extent_x):
        total, along = density[x], forward[x]
        if x > 0:
            total, along = total + ahead[x - 1], along + ahead[x - 1]
        if x < last:
            total, along = total + behind[x + 1], along - behind[x + 1]
        density[x] = total
        forward[x] = along
    for copy in sums:
        copy.wait_recv()
    for side, dz in enumerate((1, -1)):
        row = 0 if dz > 0 else extent_z - 1
        for x in range(extent_x):
            total = rims_in[side, pl.ds(x, 1), :]
            along = rims_in[side, pl.ds(extent_x + x, 1), :]
            for diagonal, (cx, cz) in enumerate(DIAGONALS):
                if cz == dz and x == (0 if cx > 0 else last):
                    total = total + tips_in[diagonal]
                    along = along + tips_in[diagonal] if cx > 0 else along - tips_in[diagonal]
            density[x, pl.ds(row, 1), :] = density[x, pl.ds(row, 1), :] + total
            forward[x, pl.ds(row, 1), :] = forward[x, pl.ds(row, 1), :] + along
    for x in range(extent_x):
        total, along = density[x], forward[x]
        if x == 0:
            total, along = total + sums_in[0], along + sums_in[0]
        if x == last:
            total, along = total + sums_in[1], along - sums_in[1]
        speed = jnp.where(walls[0, 1 + x, inner, :] > 0, along / total, 0.0)
        if spectral:
            ux[pl.ds(x * extent_z, extent_z), :] = speed
        else:
            out_ref[x] = speed

    if spectral:
        whole = ux[...]
        both = jnp.concatenate([whole, pltpu.roll(whole, height - 8, 1)], axis=0)
        turned = both.T
        for a in range(count_x):
            sent_x[a] = turned[16 * a : 16 * a + 8, :]
        x_copies = []
        for p in range(1, count_x):
            there = shifted_x(p)
            copy = pltpu.make_async_remote_copy(
                src_ref=sent_x.at[there],
                dst_ref=got_x.at[mx],
                send_sem=x_send.at[p],
                recv_sem=x_recv.at[p],
                device_id=(there, mz),
                device_id_type=MESH,
            )
            copy.start()
            x_copies.append(copy)
        got_x[mx] = sent_x[mx]
        table_copy.wait()
        first = weights[pl.ds(16, 128), :].astype(jnp.bfloat16)
        for copy in x_copies:
            copy.wait_recv()
        re, im = eight_point([got_x[s] for s in range(8)])
        low_lanes = lax.broadcasted_iota(jnp.int32, (8, 128), 1) < 64
        for k in range(8):
            c = weights[pl.ds(k, 1), :]
            s = weights[pl.ds(8 + k, 1), :]
            if im[k] is None:
                real, imag = re[k] * c, -re[k] * s
            else:
                real, imag = re[k] * c + im[k] * s, im[k] * c - re[k] * s
            left[pl.ds(k, 8, stride=8), :] = jnp.where(low_lanes, real, pltpu.roll(imag, 64, 1))
            left[pl.ds(64 + k, 8, stride=8), :] = jnp.where(low_lanes, pltpu.roll(real, 64, 1), imag)
        high, low = halves(left[...])
        contract = (((1,), (1,)), ((), ()))
        along = lax.dot_general(
            jnp.concatenate([first, first], axis=1),
            jnp.concatenate([high, low], axis=1),
            contract,
            preferred_element_type=jnp.float32,
        )
        for b in range(count_z):
            sent_z[b] = along[32 * b : 32 * b + 32, :]
        z_copies = []
        for p in range(1, count_z):
            there = shifted_z(p)
            copy = pltpu.make_async_remote_copy(
                src_ref=sent_z.at[there],
                dst_ref=got_z.at[mz],
                send_sem=z_send.at[p],
                recv_sem=z_recv.at[p],
                device_id=(mx, there),
                device_id_type=MESH,
            )
            copy.start()
            z_copies.append(copy)
        got_z[mz] = sent_z[mz]
        second_high, second_low = halves(weights[pl.ds(144, 128), :])
        second_twice = jnp.concatenate([second_high, second_high], axis=0)
        for copy in z_copies:
            copy.wait_recv()
        lines = got_z[...].reshape(128, 128).T
        high, low = halves(lines)
        result = jnp.dot(
            jnp.concatenate([high, low], axis=1), second_twice, preferred_element_type=jnp.float32
        ) + jnp.dot(high, second_low, preferred_element_type=jnp.float32)
        out_ref[0] = result[:, :64].reshape(16, 8, 64)
        out_ref[1] = result[:, 64:].reshape(16, 8, 64)
        for copy in x_copies + z_copies:
            copy.wait_send()
    for copy in x_sides + z_sides + corners + sums:
        copy.wait_send()


def shards(populations, fluid_mask):
    number, extent_x, extent_z, height = populations.shape
    count_x, count_z = lax.axis_size("gx"), lax.axis_size("gz")
    full_x, full_z = count_x * extent_x, count_z * extent_z
    norm_scale = 1.0 / (math.sqrt(full_x * full_z) * SPEED_UNIT)
    spectral = (count_x, count_z, extent_x, extent_z, height) == (8, 4, 4, 16, 128)
    if spectral:
        table = jnp.asarray(tables(count_x, count_z, extent_x, extent_z, norm_scale))
    else:
        table = jnp.zeros((8, 128), jnp.float32)
    f32 = jnp.float32
    padded = (extent_x + 2, extent_z + 2 * TOP, height)
    edge_rows = 6 * extent_x
    dma = pltpu.SemaphoreType.DMA
    scratch = [
        pltpu.VMEM((extent_x, 19, extent_z, height), f32),
        pltpu.VMEM((extent_x, extent_z, height), jnp.int32),
        pltpu.VMEM((19,) + padded, f32),
        pltpu.VMEM((19, extent_x, extent_z, height), f32),
        pltpu.VMEM((3,) + padded, f32),
        pltpu.VMEM((2, edge_rows, height), f32),
        pltpu.VMEM((2, edge_rows, height), f32),
        pltpu.VMEM((4, 2, height), f32),
        pltpu.VMEM((4, 2, height), f32),
        pltpu.VMEM((2, extent_z, height), f32),
        pltpu.VMEM((2, 2 * extent_x, height), f32),
        pltpu.VMEM((2, 2 * extent_x, height), f32),
        pltpu.VMEM((4, 1, height), f32),
        pltpu.VMEM((4, 1, height), f32),
        pltpu.VMEM((extent_x, extent_z, height), f32),
        pltpu.VMEM((extent_x, extent_z, height), f32),
        pltpu.VMEM((extent_x, extent_z, height), f32),
        pltpu.VMEM((extent_x, extent_z, height), f32),
        pltpu.VMEM((6, extent_x, 1, height), f32),
        dma((extent_x + 1,)),
        dma((2, 8)),
        dma((2, 8)),
        dma((2,)),
        dma((2,)),
    ]
    if spectral:
        scratch += [
            pltpu.VMEM((64, 128), f32),
            pltpu.VMEM((8, 8, 128), f32),
            pltpu.VMEM((8, 8, 128), f32),
            pltpu.VMEM((128, 128), f32),
            pltpu.VMEM((4, 32, 128), f32),
            pltpu.VMEM((4, 32, 128), f32),
            pltpu.VMEM(table.shape, f32),
            dma((1,)),
            dma((8,)),
            dma((8,)),
            dma((4,)),
            dma((4,)),
        ]
        out_shape = jax.ShapeDtypeStruct((2, 16, 8, 64), f32)
    else:
        out_shape = jax.ShapeDtypeStruct((extent_x, extent_z, height), f32)
    in_hbm = pl.BlockSpec(memory_space=pltpu.HBM)
    result = pl.pallas_call(
        functools.partial(kernel, spectral),
        out_shape=out_shape,
        in_specs=[in_hbm] * 3,
        out_specs=pl.BlockSpec(memory_space=pltpu.VMEM),
        scratch_shapes=scratch,
        compiler_params=pltpu.CompilerParams(
            collective_id=0, has_side_effects=True, vmem_limit_bytes=32 * 1024 * 1024
        ),
    )(*(pltpu.with_memory_space_constraint(array, pltpu.HBM) for array in (populations, fluid_mask, table)))
    if spectral:
        return result
    return spectrum(result, norm_scale)


def dft_tables(length, factor):
    index = jnp.arange(length, dtype=jnp.int32)
    products = index[:, None] * index[None, :] % length
    angles = products.astype(jnp.float32) * (2.0 * math.pi / length)
    return (jnp.cos(angles) * factor, jnp.sin(angles) * factor)


def spectrum(speed_x, norm_scale):
    columns = jnp.transpose(speed_x, (2, 1, 0))
    highest = lax.Precision.HIGHEST
    block = lax.all_to_all(columns, "gx", split_axis=0, concat_axis=2, tiled=True)
    cosine, sine = dft_tables(block.shape[2], norm_scale)
    real_part = jnp.einsum("yzx,xk->yzk", block, cosine, precision=highest)
    imag_part = -jnp.einsum("yzx,xk->yzk", block, sine, precision=highest)
    along_kx = jnp.stack([real_part, imag_part], axis=0)
    block = lax.all_to_all(along_kx, "gz", split_axis=3, concat_axis=2, tiled=True)
    cosine, sine = dft_tables(block.shape[2], 1.0)
    real_in = block[0]
    imag_in = block[1]
    real_part = jnp.einsum("ync,nk->yck", real_in, cosine, precision=highest) + jnp.einsum(
        "ync,nk->yck", imag_in, sine, precision=highest
    )
    imag_part = jnp.einsum("ync,nk->yck", imag_in, cosine, precision=highest) - jnp.einsum(
        "ync,nk->yck", real_in, sine, precision=highest
    )
    return jnp.stack([real_part, imag_part], axis=0)


def solution(mesh):
    placed = (P(None, "gx", "gz", None), P("gx", "gz", None))
    return jax.shard_map(
        shards, mesh=mesh, in_specs=placed, out_specs=P(None, "gx", "gz", None), check_vma=False
    )
```

```python
import functools
import math

import jax
import jax.numpy as jnp
import numpy as np
from jax import lax
from jax.experimental import pallas as pl
from jax.experimental.pallas import tpu as pltpu
from jax.sharding import PartitionSpec as P

VELOCITIES = (
    (0, 0, 0),
    (1, 0, 0),
    (-1, 0, 0),
    (0, 1, 0),
    (0, -1, 0),
    (0, 0, 1),
    (0, 0, -1),
    (1, 1, 0),
    (-1, -1, 0),
    (1, -1, 0),
    (-1, 1, 0),
    (1, 0, 1),
    (-1, 0, -1),
    (1, 0, -1),
    (-1, 0, 1),
    (0, 1, 1),
    (0, -1, -1),
    (0, 1, -1),
    (0, -1, 1),
)
LATTICE_WEIGHTS = (1.0 / 3.0,) + (1.0 / 18.0,) * 6 + (1.0 / 36.0,) * 12
OPPOSITES = (0, 2, 1, 4, 3, 6, 5, 8, 7, 10, 9, 12, 11, 14, 13, 16, 15, 18, 17)
RELAX_TIME = 0.6
BODY_FORCE = 0.0001
SPEED_UNIT = 0.05

CHAIN = (13, 1, 7, 9, 11, 5, 15, 18, 14, 2, 8, 10, 12, 6, 16, 17, 0, 3, 4)
SLOT = {number: CHAIN.index(number) for number in CHAIN}
X_FIRST = {1: 0, -1: 8}
Z_FIRST = {1: 4, -1: 12}
SIDES = ((1, 0), (-1, 0), (0, 1), (0, -1))
DIAGONALS = ((1, 1), (1, -1), (-1, 1), (-1, -1))
DIAGONAL_SLOT = (4, 0, 8, 12)
RIM = {(cx, cz): 2 * (cx + 1) + (cz + 1) // 2 for cx in (-1, 0, 1) for cz in (-1, 1)}
TOP = 8
MESH = pl.DeviceIdType.MESH


def collide(f, fluid):
    omega = 1.0 / RELAX_TIME
    keep = 1.0 - omega
    plus = {}
    minus = {}
    for i in range(1, 19, 2):
        plus[i] = f[i] + f[i + 1]
        minus[i] = f[i] - f[i + 1]
    density = f[0]
    momentum = [None, None, None]
    for i in range(1, 19, 2):
        density = density + plus[i]
        for axis in range(3):
            c = VELOCITIES[i][axis]
            if c:
                term = minus[i] if c > 0 else -minus[i]
                momentum[axis] = term if momentum[axis] is None else momentum[axis] + term
    inverse = 1.0 / density
    jx, jy, jz = momentum
    square = (jx * jx + jy * jy + jz * jz) * inverse
    base = density - 1.5 * square
    force = density * BODY_FORCE
    out = [None] * 19
    w0 = LATTICE_WEIGHTS[0] * omega
    out[0] = jnp.where(fluid, keep * f[0] + w0 * base, f[0])
    for i in range(1, 19, 2):
        w = LATTICE_WEIGHTS[i]
        cj = None
        for axis in range(3):
            c = VELOCITIES[i][axis]
            if c:
                j = momentum[axis]
                if cj is None:
                    cj = j if c > 0 else -j
                else:
                    cj = cj + j if c > 0 else cj - j
        even = (w * omega) * (base + 4.5 * (cj * cj * inverse))
        odd = (3.0 * w * omega) * cj
        if VELOCITIES[i][0]:
            odd = odd + (3.0 * w * VELOCITIES[i][0]) * force
        out[i] = jnp.where(fluid, keep * f[i] + (even + odd), f[i])
        out[i + 1] = jnp.where(fluid, keep * f[i + 1] + (even - odd), f[i + 1])
    return out


def tables(count_x, count_z, extent_x, extent_z, norm):
    lane = np.arange(128)
    step = (lane // extent_z) % extent_x
    k0 = np.arange(8)[:, None]
    angle = 2.0 * np.pi * k0 * step[None, :] / (count_x * extent_x)
    twiddle = np.concatenate([np.cos(angle), np.sin(angle)], axis=0)
    quarter_cos = np.array([1.0, 0.0, -1.0, 0.0])
    quarter_sin = np.array([0.0, 1.0, 0.0, -1.0])
    k1 = np.arange(4)[:, None]
    xl = np.arange(4)[None, :]
    c = quarter_cos[(k1 * xl) % 4]
    s = quarter_sin[(k1 * xl) % 4]
    block = np.zeros((4, 2, 2, 4))
    block[:, 0, 0] = c
    block[:, 0, 1] = s
    block[:, 1, 1] = c
    block[:, 1, 0] = -s
    first = np.einsum("kpqx,zw->kpzqxw", block, np.eye(extent_z)).reshape(128, 128)
    full_z = count_z * extent_z
    z = np.arange(full_z)
    angle = 2.0 * np.pi * ((z[:, None] * z[None, :]) % full_z) / full_z
    c = np.cos(angle) * norm
    s = np.sin(angle) * norm
    second = np.zeros((2, full_z, 2, full_z))
    second[0, :, 0] = c
    second[1, :, 0] = s
    second[1, :, 1] = c
    second[0, :, 1] = -s
    second = second.reshape(2, count_z, extent_z, 2, full_z).transpose(1, 0, 2, 3, 4)
    second = second.reshape(128, 128)
    return np.concatenate([twiddle, first, second], axis=0).astype(np.float32)


def halves(value):
    high = value.astype(jnp.bfloat16)
    low = (value - high.astype(jnp.float32)).astype(jnp.bfloat16)
    return high, low


def eight_point(v):
    r = math.sqrt(0.5)
    a0, a1, a2, a3 = v[0] + v[4], v[1] + v[5], v[2] + v[6], v[3] + v[7]
    b0, b1, b2, b3 = v[0] - v[4], v[1] - v[5], v[2] - v[6], v[3] - v[7]
    e0, e1 = a0 + a2, a1 + a3
    d, t = r * (b1 - b3), r * (b1 + b3)
    re = [e0 + e1, b0 + d, a0 - a2, b0 - d, e0 - e1]
    im = [None, -b2 - t, a3 - a1, b2 - t, None]
    re = re + [re[3], re[2], re[1]]
    im = im + [-im[3], -im[2], -im[1]]
    return re, im


def kernel(spectral, populations, fluid_mask, table, *rest):
    (out_ref, held, mask_i, rolled, plain, walls, edges_out, edges_in, corners_out, corners_in,
     sums_in, rims_out, rims_in, density, forward, ahead, behind, rims,
     in_sem, halo_send, halo_recv, mask_send, mask_recv) = rest[:23]
    if spectral:
        (sent_x, got_x, left, sent_z, got_z, weights,
         table_sem, x_send, x_recv, z_send, z_recv) = rest[23:]
    extent_x, extent_z, height = fluid_mask.shape
    last = extent_x - 1
    count_x, count_z = lax.axis_size("gx"), lax.axis_size("gz")
    mx, mz = lax.axis_index("gx"), lax.axis_index("gz")

    def shifted_x(step):
        return lax.rem(mx + step + count_x, count_x)

    def shifted_z(step):
        return lax.rem(mz + step + count_z, count_z)

    inner = pl.ds(TOP, extent_z)

    def fetch(x):
        return pltpu.make_async_copy(populations.at[:, x], held.at[x], in_sem.at[x])

    mask_copy = pltpu.make_async_copy(fluid_mask, mask_i, in_sem.at[extent_x])
    mask_copy.start()
    for k in range(extent_x):
        fetch((extent_x - k) % extent_x).start()

    barrier = pltpu.get_barrier_semaphore()
    partners = [(shifted_x(dx), shifted_z(dz)) for dx, dz in SIDES + DIAGONALS]
    if spectral:
        partners += [(shifted_x(p), mz) for p in range(2, count_x - 1)]
        partners += [(mx, shifted_z(p)) for p in range(2, count_z - 1)]
    for partner in partners:
        pl.semaphore_signal(barrier, inc=1, device_id=partner, device_id_type=MESH)
    if spectral:
        table_copy = pltpu.make_async_copy(table, weights, table_sem.at[0])
        table_copy.start()

    lanes = lax.broadcasted_iota(jnp.int32, (extent_z, height), 1)
    rows = lax.broadcasted_iota(jnp.int32, (extent_z, height), 0)

    def edge_of(value, cz):
        row = extent_z - 1 if cz > 0 else 0
        return value[row : row + 1, :]

    def remote(source, target, send_sem, recv_sem, dx, dz):
        return pltpu.make_async_remote_copy(
            src_ref=source,
            dst_ref=target,
            send_sem=send_sem,
            recv_sem=recv_sem,
            device_id=(shifted_x(dx), shifted_z(dz)),
            device_id_type=MESH,
        )

    def send(*arguments):
        copy = remote(*arguments)
        copy.start()
        return copy

    x_sides = []
    for side, dx in enumerate((1, -1)):
        here, there = (extent_x, 0) if dx > 0 else (1, extent_x + 1)
        group = pl.ds(X_FIRST[dx], 5)
        x_sides.append(
            remote(rolled.at[group, here, inner], rolled.at[group, there, inner],
                   halo_send.at[0, side], halo_recv.at[0, side], dx, 0)
        )
        x_sides.append(
            remote(walls.at[0, here, inner], walls.at[0, there, inner],
                   mask_send.at[side], mask_recv.at[side], dx, 0)
        )

    mask_copy.wait()
    for x in range(extent_x):
        walls[0, 1 + x, inner, :] = mask_i[x].astype(jnp.float32)

    def first_collision(k, carry):
        x = lax.rem(extent_x - k, extent_x)
        fetch(x).wait()
        g = collide([held[x, number] for number in range(19)], walls[0, 1 + x, inner, :] > 0)
        for number in range(19):
            cy = VELOCITIES[number][1]
            value = g[number]
            if cy:
                plain[number, x] = value
                value = pltpu.roll(value, cy % height, 1)
            rolled[SLOT[number], 1 + x, inner, :] = value

        @pl.when(k == 1)
        def _():
            pl.semaphore_wait(barrier, len(partners))
            for copy in x_sides:
                copy.start()

        return carry

    lax.fori_loop(0, extent_x, first_collision, 0)
    z_sides, corners = [], []
    for side, cz in enumerate((1, -1)):
        row = pl.ds(TOP + extent_z - 1 if cz > 0 else TOP, 1)
        for x in range(extent_x):
            for order in range(5):
                edges_out[side, pl.ds(order * extent_x + x, 1), :] = rolled[
                    (Z_FIRST[cz] + order) % 16, 1 + x, row, :
                ]
            edges_out[side, pl.ds(5 * extent_x + x, 1), :] = walls[0, 1 + x, row, :]
        z_sides.append(
            send(edges_out.at[side], edges_in.at[side],
                 halo_send.at[0, 2 + side], halo_recv.at[0, 2 + side], 0, cz)
        )
    for diagonal, (dx, dz) in enumerate(DIAGONALS):
        row = pl.ds(TOP + extent_z - 1 if dz > 0 else TOP, 1)
        plane = extent_x if dx > 0 else 1
        corners_out[diagonal, pl.ds(0, 1), :] = rolled[DIAGONAL_SLOT[diagonal], plane, row, :]
        corners_out[diagonal, pl.ds(1, 1), :] = walls[0, plane, row, :]
        corners.append(
            send(corners_out.at[diagonal], corners_in.at[diagonal],
                 halo_send.at[0, 4 + diagonal], halo_recv.at[0, 4 + diagonal], dx, dz)
        )

    around = lax.broadcasted_iota(jnp.int32, (extent_z + 2 * TOP, height), 1)

    def shift_walls(plane):
        value = walls[0, plane]
        walls[1, plane] = jnp.where(around == 0, 0.0, pltpu.roll(value, 1, 1))
        walls[2, plane] = jnp.where(around == height - 1, 0.0, pltpu.roll(value, height - 1, 1))

    def wall_from(number, x):
        cx, cy, cz = VELOCITIES[number]
        return walls[(0, 1, 2)[cy], 1 + x - cx, pl.ds(TOP - cz, extent_z), :] > 0

    def second_collision(k, carry):
        x = lax.rem(k + 1, extent_x)

        @pl.when(k == extent_x - 2)
        def _():
            for copy in x_sides + corners:
                copy.wait_recv()
            for diagonal, (cx, cz) in enumerate(DIAGONALS):
                plane = 0 if cx > 0 else extent_x + 1
                row = pl.ds(TOP - 1 if cz > 0 else TOP + extent_z, 1)
                rolled[DIAGONAL_SLOT[diagonal], plane, row, :] = corners_in[diagonal, pl.ds(0, 1), :]
                walls[0, plane, row, :] = corners_in[diagonal, pl.ds(1, 1), :]
            for plane in (0, extent_x + 1):
                shift_walls(plane)

        fluid = walls[0, 1 + x, inner, :] > 0
        owned = []
        for number in range(19):
            if VELOCITIES[number][1]:
                owned.append(plain[number, x])
            else:
                owned.append(rolled[SLOT[number], 1 + x, inner, :])
        f = [owned[0]]
        for number in range(1, 19):
            cx, cy, cz = VELOCITIES[number]
            value = rolled[SLOT[number], 1 + x - cx, pl.ds(TOP - cz, extent_z), :]
            arrived = jnp.where(wall_from(number, x), value, owned[OPPOSITES[number]])
            f.append(jnp.where(fluid, arrived, owned[number]))
        g = collide(f, fluid)
        leaving = {}
        turned_back = {}
        for number in range(1, 19):
            cx, cy, cz = VELOCITIES[number]
            value = jnp.where(fluid, g[number], 0.0)
            if cy:
                value = pltpu.roll(value, cy % height, 1)
                value = jnp.where(lanes == (0 if cy > 0 else height - 1), 0.0, value)
            leaving[cx, cz] = leaving[cx, cz] + value if (cx, cz) in leaving else value
            value = jnp.where(wall_from(number, x), 0.0, g[OPPOSITES[number]])
            turned_back[cx] = turned_back[cx] + value if cx in turned_back else value
        for cx, keep in ((1, ahead), (-1, behind), (0, None)):
            total = leaving[cx, 0]
            for cz in (1, -1):
                value = leaving[cx, cz]
                rims[RIM[cx, cz], x] = edge_of(value, cz)
                moved = pltpu.roll(value, cz % extent_z, 0)
                total = total + jnp.where(rows == (0 if cz > 0 else extent_z - 1), 0.0, moved)
            if keep is None:
                density[x] = (g[0] + total) + (turned_back[0] + turned_back[1] + turned_back[-1])
            else:
                keep[x] = total
        forward[x] = turned_back[1] - turned_back[-1]
        return carry

    for copy in z_sides:
        copy.wait_recv()
    for side, cz in enumerate((1, -1)):
        row = pl.ds(TOP - 1 if cz > 0 else TOP + extent_z, 1)
        for x in range(extent_x):
            for order in range(5):
                rolled[(Z_FIRST[cz] + order) % 16, 1 + x, row, :] = edges_in[
                    side, pl.ds(order * extent_x + x, 1), :
                ]
            walls[0, 1 + x, row, :] = edges_in[side, pl.ds(5 * extent_x + x, 1), :]

    def shift_inner(plane, carry):
        shift_walls(plane)
        return carry

    lax.fori_loop(1, 1 + extent_x, shift_inner, 0)
    lax.fori_loop(0, extent_x, second_collision, 0)

    rim_copies = []
    for side, dz in enumerate((1, -1)):
        for x in range(extent_x):
            total, along = rims[RIM[0, dz], x], None
            if x > 0:
                forth = rims[RIM[1, dz], x - 1]
                total, along = total + forth, forth
            if x < last:
                back = rims[RIM[-1, dz], x + 1]
                total, along = total + back, -back if along is None else along - back
            rims_out[side, pl.ds(x, 1), :] = total
            rims_out[side, pl.ds(extent_x + x, 1), :] = along
        rims_out[side, pl.ds(2 * extent_x, 1), :] = rims[RIM[1, dz], last]
        rims_out[side, pl.ds(2 * extent_x + 1, 1), :] = rims[RIM[-1, dz], 0]
        rim_copies.append(
            send(rims_out.at[side], rims_in.at[side],
                 halo_send.at[1, side], halo_recv.at[1, side], 0, dz)
        )
    for x in range(extent_x):
        total, along = density[x], forward[x]
        if x > 0:
            total, along = total + ahead[x - 1], along + ahead[x - 1]
        if x < last:
            total, along = total + behind[x + 1], along - behind[x + 1]
        density[x] = total
        forward[x] = along
    for copy in rim_copies:
        copy.wait_recv()
    for side, dz in enumerate((1, -1)):
        row = pl.ds(0 if dz > 0 else extent_z - 1, 1)
        for x in range(extent_x):
            density[x, row, :] = density[x, row, :] + rims_in[side, pl.ds(x, 1), :]
            forward[x, row, :] = forward[x, row, :] + rims_in[side, pl.ds(extent_x + x, 1), :]
        ahead[last, row, :] = ahead[last, row, :] + rims_in[side, pl.ds(2 * extent_x, 1), :]
        behind[0, row, :] = behind[0, row, :] + rims_in[side, pl.ds(2 * extent_x + 1, 1), :]

    def is_fluid(plane):
        return walls[0, plane, inner, :] > 0

    if not spectral:
        sums = []
        for side, (dx, x, keep) in enumerate(((1, last, ahead), (-1, 0, behind))):
            sums.append(
                send(keep.at[x], sums_in.at[side],
                     halo_send.at[1, 2 + side], halo_recv.at[1, 2 + side], dx, 0)
            )
        for copy in sums:
            copy.wait_recv()
        for x in range(extent_x):
            total, along = density[x], forward[x]
            if x == 0:
                total, along = total + sums_in[0], along + sums_in[0]
            if x == last:
                total, along = total + sums_in[1], along - sums_in[1]
            out_ref[x] = jnp.where(is_fluid(1 + x), along / total, 0.0)
        for copy in rim_copies + sums:
            copy.wait_send()

    if spectral:
        parts = []
        for x in range(extent_x):
            if x in (0, last):
                parts.append(jnp.where(is_fluid(1 + x), density[x], 1.0))
            else:
                parts.append(jnp.where(is_fluid(1 + x), forward[x] / density[x], 0.0))
        parts.append(jnp.where(is_fluid(1), forward[0], 0.0))
        parts.append(jnp.where(is_fluid(extent_x + 1), ahead[last], 0.0))
        parts.append(jnp.where(is_fluid(0), behind[0], 0.0))
        parts.append(jnp.where(is_fluid(extent_x), forward[last], 0.0))
        sent_x[...] = jnp.concatenate(parts, axis=0).T.reshape(8, 16, 128)
        x_copies = []
        for p in range(1, count_x):
            there = shifted_x(p)
            copy = pltpu.make_async_remote_copy(
                src_ref=sent_x.at[there],
                dst_ref=got_x.at[mx],
                send_sem=x_send.at[p],
                recv_sem=x_recv.at[p],
                device_id=(there, mz),
                device_id_type=MESH,
            )
            copy.start()
            x_copies.append(copy)
        got_x[mx] = sent_x[mx]
        table_copy.wait()
        first = weights[pl.ds(16, 128), :].astype(jnp.bfloat16)
        for copy in x_copies:
            copy.wait_recv()
        lane = lax.broadcasted_iota(jnp.int32, (16, 128), 1)
        head, tail = lane < 16, lane >= 48
        got = [got_x[s] for s in range(8)]
        speeds = []
        for s in range(8):
            forth = pltpu.roll(got[(s - 1) % 8], 128 - 80, 1)
            back = pltpu.roll(got[(s + 1) % 8], 128 - 48, 1)
            mine = pltpu.roll(got[s], 64, 1)
            total = got[s] + jnp.where(head, forth, back)
            along = mine + jnp.where(head, forth, -back)
            speeds.append(jnp.where(head | tail, along / total, got[s]))
        re, im = eight_point(speeds)
        low_lanes = lane < 64
        for k in range(8):
            c = weights[pl.ds(k, 1), :]
            s = weights[pl.ds(8 + k, 1), :]
            if im[k] is None:
                real, imag = re[k] * c, -re[k] * s
            else:
                real, imag = re[k] * c + im[k] * s, im[k] * c - re[k] * s
            left[pl.ds(k, 16, stride=8), :] = jnp.where(low_lanes, real, pltpu.roll(imag, 64, 1))
        high, low = halves(left[...])
        contract = (((1,), (1,)), ((), ()))
        along = lax.dot_general(
            jnp.concatenate([first, first], axis=1),
            jnp.concatenate([high, low], axis=1),
            contract,
            preferred_element_type=jnp.float32,
        )
        for b in range(count_z):
            sent_z[b] = along[32 * b : 32 * b + 32, :]
        z_copies = []
        for p in range(1, count_z):
            there = shifted_z(p)
            copy = pltpu.make_async_remote_copy(
                src_ref=sent_z.at[there],
                dst_ref=got_z.at[mz],
                send_sem=z_send.at[p],
                recv_sem=z_recv.at[p],
                device_id=(mx, there),
                device_id_type=MESH,
            )
            copy.start()
            z_copies.append(copy)
        got_z[mz] = sent_z[mz]
        second_high, second_low = halves(weights[pl.ds(144, 128), :])
        second_twice = jnp.concatenate([second_high, second_high], axis=0)
        for copy in z_copies:
            copy.wait_recv()
        lines = got_z[...].reshape(128, 128).T
        high, low = halves(lines)
        result = jnp.dot(
            jnp.concatenate([high, low], axis=1), second_twice, preferred_element_type=jnp.float32
        ) + jnp.dot(high, second_low, preferred_element_type=jnp.float32)
        out_ref[0] = result[:, :64].reshape(16, 8, 64)
        out_ref[1] = result[:, 64:].reshape(16, 8, 64)
        for copy in rim_copies + x_copies + z_copies:
            copy.wait_send()
    for copy in x_sides + z_sides + corners:
        copy.wait_send()


def shards(populations, fluid_mask):
    number, extent_x, extent_z, height = populations.shape
    count_x, count_z = lax.axis_size("gx"), lax.axis_size("gz")
    full_x, full_z = count_x * extent_x, count_z * extent_z
    norm_scale = 1.0 / (math.sqrt(full_x * full_z) * SPEED_UNIT)
    spectral = (count_x, count_z, extent_x, extent_z, height) == (8, 4, 4, 16, 128)
    if spectral:
        table = jnp.asarray(tables(count_x, count_z, extent_x, extent_z, norm_scale))
    else:
        table = jnp.zeros((8, 128), jnp.float32)
    f32 = jnp.float32
    padded = (extent_x + 2, extent_z + 2 * TOP, height)
    edge_rows = 6 * extent_x
    dma = pltpu.SemaphoreType.DMA
    scratch = [
        pltpu.VMEM((extent_x, 19, extent_z, height), f32),
        pltpu.VMEM((extent_x, extent_z, height), jnp.int32),
        pltpu.VMEM((19,) + padded, f32),
        pltpu.VMEM((19, extent_x, extent_z, height), f32),
        pltpu.VMEM((3,) + padded, f32),
        pltpu.VMEM((2, edge_rows, height), f32),
        pltpu.VMEM((2, edge_rows, height), f32),
        pltpu.VMEM((4, 2, height), f32),
        pltpu.VMEM((4, 2, height), f32),
        pltpu.VMEM((2, extent_z, height), f32),
        pltpu.VMEM((2, 2 * extent_x + 2, height), f32),
        pltpu.VMEM((2, 2 * extent_x + 2, height), f32),
        pltpu.VMEM((extent_x, extent_z, height), f32),
        pltpu.VMEM((extent_x, extent_z, height), f32),
        pltpu.VMEM((extent_x, extent_z, height), f32),
        pltpu.VMEM((extent_x, extent_z, height), f32),
        pltpu.VMEM((6, extent_x, 1, height), f32),
        dma((extent_x + 1,)),
        dma((2, 8)),
        dma((2, 8)),
        dma((2,)),
        dma((2,)),
    ]
    if spectral:
        scratch += [
            pltpu.VMEM((8, 16, 128), f32),
            pltpu.VMEM((8, 16, 128), f32),
            pltpu.VMEM((128, 128), f32),
            pltpu.VMEM((4, 32, 128), f32),
            pltpu.VMEM((4, 32, 128), f32),
            pltpu.VMEM(table.shape, f32),
            dma((1,)),
            dma((8,)),
            dma((8,)),
            dma((4,)),
            dma((4,)),
        ]
        out_shape = jax.ShapeDtypeStruct((2, 16, 8, 64), f32)
    else:
        out_shape = jax.ShapeDtypeStruct((extent_x, extent_z, height), f32)
    in_hbm = pl.BlockSpec(memory_space=pltpu.HBM)
    result = pl.pallas_call(
        functools.partial(kernel, spectral),
        out_shape=out_shape,
        in_specs=[in_hbm] * 3,
        out_specs=pl.BlockSpec(memory_space=pltpu.VMEM),
        scratch_shapes=scratch,
        compiler_params=pltpu.CompilerParams(
            collective_id=0, has_side_effects=True, vmem_limit_bytes=32 * 1024 * 1024
        ),
    )(*(pltpu.with_memory_space_constraint(array, pltpu.HBM) for array in (populations, fluid_mask, table)))
    if spectral:
        return result
    return spectrum(result, norm_scale)


def dft_tables(length, factor):
    index = jnp.arange(length, dtype=jnp.int32)
    products = index[:, None] * index[None, :] % length
    angles = products.astype(jnp.float32) * (2.0 * math.pi / length)
    return (jnp.cos(angles) * factor, jnp.sin(angles) * factor)


def spectrum(speed_x, norm_scale):
    columns = jnp.transpose(speed_x, (2, 1, 0))
    highest = lax.Precision.HIGHEST
    block = lax.all_to_all(columns, "gx", split_axis=0, concat_axis=2, tiled=True)
    cosine, sine = dft_tables(block.shape[2], norm_scale)
    real_part = jnp.einsum("yzx,xk->yzk", block, cosine, precision=highest)
    imag_part = -jnp.einsum("yzx,xk->yzk", block, sine, precision=highest)
    along_kx = jnp.stack([real_part, imag_part], axis=0)
    block = lax.all_to_all(along_kx, "gz", split_axis=3, concat_axis=2, tiled=True)
    cosine, sine = dft_tables(block.shape[2], 1.0)
    real_in = block[0]
    imag_in = block[1]
    real_part = jnp.einsum("ync,nk->yck", real_in, cosine, precision=highest) + jnp.einsum(
        "ync,nk->yck", imag_in, sine, precision=highest
    )
    imag_part = jnp.einsum("ync,nk->yck", imag_in, cosine, precision=highest) - jnp.einsum(
        "ync,nk->yck", real_in, sine, precision=highest
    )
    return jnp.stack([real_part, imag_part], axis=0)


def solution(mesh):
    placed = (P(None, "gx", "gz", None), P("gx", "gz", None))
    return jax.shard_map(
        shards, mesh=mesh, in_specs=placed, out_specs=P(None, "gx", "gz", None), check_vma=False
    )
```

```python
import functools
import math

import jax
import jax.numpy as jnp
import numpy as np
from jax import lax
from jax.experimental import pallas as pl
from jax.experimental.pallas import tpu as pltpu
from jax.sharding import PartitionSpec as P

VELOCITIES = (
    (0, 0, 0),
    (1, 0, 0),
    (-1, 0, 0),
    (0, 1, 0),
    (0, -1, 0),
    (0, 0, 1),
    (0, 0, -1),
    (1, 1, 0),
    (-1, -1, 0),
    (1, -1, 0),
    (-1, 1, 0),
    (1, 0, 1),
    (-1, 0, -1),
    (1, 0, -1),
    (-1, 0, 1),
    (0, 1, 1),
    (0, -1, -1),
    (0, 1, -1),
    (0, -1, 1),
)
LATTICE_WEIGHTS = (1.0 / 3.0,) + (1.0 / 18.0,) * 6 + (1.0 / 36.0,) * 12
OPPOSITES = (0, 2, 1, 4, 3, 6, 5, 8, 7, 10, 9, 12, 11, 14, 13, 16, 15, 18, 17)
RELAX_TIME = 0.6
BODY_FORCE = 0.0001
SPEED_UNIT = 0.05

CHAIN = (13, 1, 7, 9, 11, 5, 15, 18, 14, 2, 8, 10, 12, 6, 16, 17, 0, 3, 4)
SLOT = {number: CHAIN.index(number) for number in CHAIN}
X_FIRST = {1: 0, -1: 8}
Z_FIRST = {1: 4, -1: 12}
SIDES = ((1, 0), (-1, 0), (0, 1), (0, -1))
DIAGONALS = ((1, 1), (1, -1), (-1, 1), (-1, -1))
DIAGONAL_SLOT = (4, 0, 8, 12)
TOP = 8
MESH = pl.DeviceIdType.MESH


def collide(f, fluid):
    omega = 1.0 / RELAX_TIME
    keep = 1.0 - omega
    plus = {}
    minus = {}
    for i in range(1, 19, 2):
        plus[i] = f[i] + f[i + 1]
        minus[i] = f[i] - f[i + 1]
    density = f[0]
    momentum = [None, None, None]
    for i in range(1, 19, 2):
        density = density + plus[i]
        for axis in range(3):
            c = VELOCITIES[i][axis]
            if c:
                term = minus[i] if c > 0 else -minus[i]
                momentum[axis] = term if momentum[axis] is None else momentum[axis] + term
    inverse = 1.0 / density
    jx, jy, jz = momentum
    square = (jx * jx + jy * jy + jz * jz) * inverse
    base = density - 1.5 * square
    force = density * BODY_FORCE
    out = [None] * 19
    w0 = LATTICE_WEIGHTS[0] * omega
    out[0] = jnp.where(fluid, keep * f[0] + w0 * base, f[0])
    for i in range(1, 19, 2):
        w = LATTICE_WEIGHTS[i]
        cj = None
        for axis in range(3):
            c = VELOCITIES[i][axis]
            if c:
                j = momentum[axis]
                if cj is None:
                    cj = j if c > 0 else -j
                else:
                    cj = cj + j if c > 0 else cj - j
        even = (w * omega) * (base + 4.5 * (cj * cj * inverse))
        odd = (3.0 * w * omega) * cj
        if VELOCITIES[i][0]:
            odd = odd + (3.0 * w * VELOCITIES[i][0]) * force
        out[i] = jnp.where(fluid, keep * f[i] + (even + odd), f[i])
        out[i + 1] = jnp.where(fluid, keep * f[i + 1] + (even - odd), f[i + 1])
    return out


def tables(count_x, count_z, extent_x, extent_z, norm):
    lane = np.arange(128)
    step = (lane // extent_z) % extent_x
    k0 = np.arange(8)[:, None]
    angle = 2.0 * np.pi * k0 * step[None, :] / (count_x * extent_x)
    twiddle = np.concatenate([np.cos(angle), np.sin(angle)], axis=0)
    quarter_cos = np.array([1.0, 0.0, -1.0, 0.0])
    quarter_sin = np.array([0.0, 1.0, 0.0, -1.0])
    k1 = np.arange(4)[:, None]
    xl = np.arange(4)[None, :]
    c = quarter_cos[(k1 * xl) % 4]
    s = quarter_sin[(k1 * xl) % 4]
    block = np.zeros((4, 2, 2, 4))
    block[:, 0, 0] = c
    block[:, 0, 1] = s
    block[:, 1, 1] = c
    block[:, 1, 0] = -s
    first = np.einsum("kpqx,zw->kpzqxw", block, np.eye(extent_z)).reshape(128, 128)
    full_z = count_z * extent_z
    z = np.arange(full_z)
    angle = 2.0 * np.pi * ((z[:, None] * z[None, :]) % full_z) / full_z
    c = np.cos(angle) * norm
    s = np.sin(angle) * norm
    second = np.zeros((2, full_z, 2, full_z))
    second[0, :, 0] = c
    second[1, :, 0] = s
    second[1, :, 1] = c
    second[0, :, 1] = -s
    second = second.reshape(2, count_z, extent_z, 2, full_z).transpose(1, 0, 2, 3, 4)
    second = second.reshape(128, 128)
    return np.concatenate([twiddle, first, second], axis=0).astype(np.float32)


def halves(value):
    high = value.astype(jnp.bfloat16)
    low = (value - high.astype(jnp.float32)).astype(jnp.bfloat16)
    return high, low


def eight_point(v):
    r = math.sqrt(0.5)
    a0, a1, a2, a3 = v[0] + v[4], v[1] + v[5], v[2] + v[6], v[3] + v[7]
    b0, b1, b2, b3 = v[0] - v[4], v[1] - v[5], v[2] - v[6], v[3] - v[7]
    e0, e1 = a0 + a2, a1 + a3
    d, t = r * (b1 - b3), r * (b1 + b3)
    re = [e0 + e1, b0 + d, a0 - a2, b0 - d, e0 - e1]
    im = [None, -b2 - t, a3 - a1, b2 - t, None]
    re = re + [re[3], re[2], re[1]]
    im = im + [-im[3], -im[2], -im[1]]
    return re, im


def kernel(spectral, populations, fluid_mask, table, *rest):
    (out_ref, held, mask_i, rolled, plain, walls, edges_out, edges_in, corners_out, corners_in,
     sums_in, density, forward, ahead, behind,
     in_sem, halo_send, halo_recv, mask_send, mask_recv) = rest[:20]
    if spectral:
        (sent_x, got_x, left, sent_z, got_z, weights,
         table_sem, x_send, x_recv, z_send, z_recv) = rest[20:]
    extent_x, extent_z, height = fluid_mask.shape
    last = extent_x - 1
    count_x, count_z = lax.axis_size("gx"), lax.axis_size("gz")
    mx, mz = lax.axis_index("gx"), lax.axis_index("gz")

    def shifted_x(step):
        return lax.rem(mx + step + count_x, count_x)

    def shifted_z(step):
        return lax.rem(mz + step + count_z, count_z)

    inner = pl.ds(TOP, extent_z)

    def fetch(x):
        return pltpu.make_async_copy(populations.at[:, x], held.at[x], in_sem.at[x])

    mask_copy = pltpu.make_async_copy(fluid_mask, mask_i, in_sem.at[extent_x])
    mask_copy.start()
    for k in range(extent_x):
        fetch((extent_x - k) % extent_x).start()

    barrier = pltpu.get_barrier_semaphore()
    partners = [(shifted_x(dx), shifted_z(dz)) for dx, dz in SIDES + DIAGONALS]
    if spectral:
        partners += [(shifted_x(p), mz) for p in range(2, count_x - 1)]
        partners += [(mx, shifted_z(p)) for p in range(2, count_z - 1)]
    for partner in partners:
        pl.semaphore_signal(barrier, inc=1, device_id=partner, device_id_type=MESH)
    if spectral:
        table_copy = pltpu.make_async_copy(table, weights, table_sem.at[0])
        table_copy.start()

    wide = extent_z + 2
    lanes = lax.broadcasted_iota(jnp.int32, (wide, height), 1)

    def edge_rows(cz):
        if cz > 0:
            return pl.ds(TOP + extent_z - 1, 1), pl.ds(TOP + extent_z - 2, 1)
        return pl.ds(TOP, 1), pl.ds(TOP + 1, 1)

    def halo_rows(cz):
        if cz > 0:
            return pl.ds(TOP - 1, 1), pl.ds(TOP - 2, 1)
        return pl.ds(TOP + extent_z, 1), pl.ds(TOP + extent_z + 1, 1)

    def remote(source, target, send_sem, recv_sem, dx, dz):
        return pltpu.make_async_remote_copy(
            src_ref=source,
            dst_ref=target,
            send_sem=send_sem,
            recv_sem=recv_sem,
            device_id=(shifted_x(dx), shifted_z(dz)),
            device_id_type=MESH,
        )

    def send(*arguments):
        copy = remote(*arguments)
        copy.start()
        return copy

    x_sides, x_masks = [], []
    for side, dx in enumerate((1, -1)):
        here, there = (extent_x, 0) if dx > 0 else (1, extent_x + 1)
        group = pl.ds(X_FIRST[dx], 5)
        x_sides.append(
            remote(rolled.at[group, here, inner], rolled.at[group, there, inner],
                   halo_send.at[0, side], halo_recv.at[0, side], dx, 0)
        )
        x_masks.append(
            remote(walls.at[0, here, inner], walls.at[0, there, inner],
                   mask_send.at[side], mask_recv.at[side], dx, 0)
        )

    mask_copy.wait()
    for x in range(extent_x):
        walls[0, 1 + x, inner, :] = mask_i[x].astype(jnp.float32)

    def first_collision(k, carry):
        x = lax.rem(extent_x - k, extent_x)
        fetch(x).wait()
        g = collide([held[x, number] for number in range(19)], walls[0, 1 + x, inner, :] > 0)
        for number in range(19):
            cy = VELOCITIES[number][1]
            value = g[number]
            if cy:
                plain[number, x, inner, :] = value
                value = pltpu.roll(value, cy % height, 1)
            rolled[SLOT[number], 1 + x, inner, :] = value

        @pl.when(k == 1)
        def _():
            pl.semaphore_wait(barrier, len(partners))
            for copy in x_sides + x_masks:
                copy.start()

        return carry

    lax.fori_loop(0, extent_x, first_collision, 0)
    z_sides, corners = [], []

    def pack(x, carry):
        for side, cz in enumerate((1, -1)):
            edge, beside = edge_rows(cz)
            for number in range(19):
                if VELOCITIES[number][1]:
                    value = plain[number, x, edge, :]
                else:
                    value = rolled[SLOT[number], 1 + x, edge, :]
                edges_out[side, x, pl.ds(number, 1), :] = value
            for order in range(5):
                edges_out[side, x, pl.ds(19 + order, 1), :] = rolled[
                    (Z_FIRST[cz] + order) % 16, 1 + x, beside, :
                ]
            edges_out[side, x, pl.ds(24, 1), :] = walls[0, 1 + x, edge, :]
            edges_out[side, x, pl.ds(25, 1), :] = walls[0, 1 + x, beside, :]
        return carry

    lax.fori_loop(0, extent_x, pack, 0)
    for side, cz in enumerate((1, -1)):
        z_sides.append(
            send(edges_out.at[side], edges_in.at[side],
                 halo_send.at[0, 2 + side], halo_recv.at[0, 2 + side], 0, cz)
        )
    for diagonal, (dx, dz) in enumerate(DIAGONALS):
        edge, beside = edge_rows(dz)
        plane = extent_x if dx > 0 else 1
        for order in range(5):
            corners_out[diagonal, pl.ds(order, 1), :] = rolled[X_FIRST[dx] + order, plane, edge, :]
        corners_out[diagonal, pl.ds(5, 1), :] = rolled[DIAGONAL_SLOT[diagonal], plane, beside, :]
        corners_out[diagonal, pl.ds(6, 1), :] = walls[0, plane, edge, :]
        corners_out[diagonal, pl.ds(7, 1), :] = walls[0, plane, beside, :]
        corners.append(
            send(corners_out.at[diagonal], corners_in.at[diagonal],
                 halo_send.at[0, 4 + diagonal], halo_recv.at[0, 4 + diagonal], dx, dz)
        )

    around = lax.broadcasted_iota(jnp.int32, (extent_z + 2 * TOP, height), 1)

    def shift_walls(plane):
        value = walls[0, plane]
        walls[1, plane] = jnp.where(around == 0, 0.0, pltpu.roll(value, 1, 1))
        walls[2, plane] = jnp.where(around == height - 1, 0.0, pltpu.roll(value, height - 1, 1))

    def wall_from(number, x):
        cx, cy, cz = VELOCITIES[number]
        return walls[(0, 1, 2)[cy], 1 + x - cx, pl.ds(TOP - 1 - cz, wide), :] > 0

    def second_collision(k, carry):
        x = lax.rem(k + 1, extent_x)

        @pl.when(k == extent_x - 2)
        def _():
            for copy in x_masks + x_sides + corners:
                copy.wait_recv()
            for diagonal, (cx, cz) in enumerate(DIAGONALS):
                beside, further = halo_rows(cz)
                plane = 0 if cx > 0 else extent_x + 1
                for order in range(5):
                    rolled[X_FIRST[cx] + order, plane, beside, :] = corners_in[diagonal, pl.ds(order, 1), :]
                rolled[DIAGONAL_SLOT[diagonal], plane, further, :] = corners_in[diagonal, pl.ds(5, 1), :]
                walls[0, plane, beside, :] = corners_in[diagonal, pl.ds(6, 1), :]
                walls[0, plane, further, :] = corners_in[diagonal, pl.ds(7, 1), :]
            for plane in (0, extent_x + 1):
                shift_walls(plane)

        region = pl.ds(TOP - 1, wide)
        fluid = walls[0, 1 + x, region, :] > 0
        owned = []
        for number in range(19):
            if VELOCITIES[number][1]:
                owned.append(plain[number, x, region, :])
            else:
                owned.append(rolled[SLOT[number], 1 + x, region, :])
        f = [owned[0]]
        for number in range(1, 19):
            cx, cy, cz = VELOCITIES[number]
            value = rolled[SLOT[number], 1 + x - cx, pl.ds(TOP - 1 - cz, wide), :]
            arrived = jnp.where(wall_from(number, x), value, owned[OPPOSITES[number]])
            f.append(jnp.where(fluid, arrived, owned[number]))
        g = collide(f, fluid)
        leaving = {}
        turned_back = {}
        for number in range(1, 19):
            cx, cy, cz = VELOCITIES[number]
            value = jnp.where(fluid, g[number], 0.0)
            if cy:
                value = pltpu.roll(value, cy % height, 1)
                value = jnp.where(lanes == (0 if cy > 0 else height - 1), 0.0, value)
            leaving[cx, cz] = leaving[cx, cz] + value if (cx, cz) in leaving else value
            value = jnp.where(wall_from(number, x), 0.0, g[OPPOSITES[number]])
            turned_back[cx] = turned_back[cx] + value if cx in turned_back else value
        stay = slice(1, 1 + extent_z)
        leaving[0, 0] = leaving[0, 0] + g[0] + (turned_back[0] + turned_back[1] + turned_back[-1])
        for cx, keep in ((1, ahead), (-1, behind), (0, density)):
            keep[x] = leaving[cx, 0][stay] + leaving[cx, 1][:extent_z] + leaving[cx, -1][2:]
        forward[x] = (turned_back[1] - turned_back[-1])[stay]
        return carry

    for copy in z_sides:
        copy.wait_recv()
    def unpack(x, carry):
        for side, cz in enumerate((1, -1)):
            beside, further = halo_rows(cz)
            for number in range(19):
                value = edges_in[side, x, pl.ds(number, 1), :]
                cy = VELOCITIES[number][1]
                if cy:
                    plain[number, x, beside, :] = value
                    value = pltpu.roll(value, cy % height, 1)
                rolled[SLOT[number], 1 + x, beside, :] = value
            for order in range(5):
                rolled[(Z_FIRST[cz] + order) % 16, 1 + x, further, :] = edges_in[
                    side, x, pl.ds(19 + order, 1), :
                ]
            walls[0, 1 + x, beside, :] = edges_in[side, x, pl.ds(24, 1), :]
            walls[0, 1 + x, further, :] = edges_in[side, x, pl.ds(25, 1), :]
        return carry

    lax.fori_loop(0, extent_x, unpack, 0)

    def shift_inner(plane, carry):
        shift_walls(plane)
        return carry

    lax.fori_loop(1, 1 + extent_x, shift_inner, 0)
    lax.fori_loop(0, extent_x, second_collision, 0)

    for x in range(extent_x):
        total, along = density[x], forward[x]
        if x > 0:
            total, along = total + ahead[x - 1], along + ahead[x - 1]
        if x < last:
            total, along = total + behind[x + 1], along - behind[x + 1]
        density[x] = total
        forward[x] = along

    halo_copies = x_sides + x_masks + z_sides + corners

    def is_fluid(plane):
        return walls[0, plane, inner, :] > 0

    if not spectral:
        sums = []
        for side, (dx, x, keep) in enumerate(((1, last, ahead), (-1, 0, behind))):
            sums.append(
                send(keep.at[x], sums_in.at[side],
                     halo_send.at[1, 2 + side], halo_recv.at[1, 2 + side], dx, 0)
            )
        for copy in sums:
            copy.wait_recv()
        for x in range(extent_x):
            total, along = density[x], forward[x]
            if x == 0:
                total, along = total + sums_in[0], along + sums_in[0]
            if x == last:
                total, along = total + sums_in[1], along - sums_in[1]
            out_ref[x] = jnp.where(is_fluid(1 + x), along / total, 0.0)
        for copy in halo_copies + sums:
            copy.wait_send()

    if spectral:
        parts = []
        for x in range(extent_x):
            if x in (0, last):
                parts.append(jnp.where(is_fluid(1 + x), density[x], 1.0))
            else:
                parts.append(jnp.where(is_fluid(1 + x), forward[x] / density[x], 0.0))
        parts.append(jnp.where(is_fluid(1), forward[0], 0.0))
        parts.append(jnp.where(is_fluid(extent_x + 1), ahead[last], 0.0))
        parts.append(jnp.where(is_fluid(0), behind[0], 0.0))
        parts.append(jnp.where(is_fluid(extent_x), forward[last], 0.0))
        sent_x[...] = jnp.concatenate(parts, axis=0).T.reshape(8, 16, 128)
        x_copies = []
        for p in range(1, count_x):
            there = shifted_x(p)
            copy = pltpu.make_async_remote_copy(
                src_ref=sent_x.at[there],
                dst_ref=got_x.at[mx],
                send_sem=x_send.at[p],
                recv_sem=x_recv.at[p],
                device_id=(there, mz),
                device_id_type=MESH,
            )
            copy.start()
            x_copies.append(copy)
        got_x[mx] = sent_x[mx]
        table_copy.wait()
        first = weights[pl.ds(16, 128), :].astype(jnp.bfloat16)
        for copy in halo_copies:
            copy.wait_send()
        for copy in x_copies:
            copy.wait_recv()
        lane = lax.broadcasted_iota(jnp.int32, (16, 128), 1)
        head, tail = lane < 16, lane >= 48
        got = [got_x[s] for s in range(8)]
        speeds = []
        for s in range(8):
            forth = pltpu.roll(got[(s - 1) % 8], 128 - 80, 1)
            back = pltpu.roll(got[(s + 1) % 8], 128 - 48, 1)
            mine = pltpu.roll(got[s], 64, 1)
            total = got[s] + jnp.where(head, forth, back)
            along = mine + jnp.where(head, forth, -back)
            speeds.append(jnp.where(head | tail, along / total, got[s]))
        re, im = eight_point(speeds)
        low_lanes = lane < 64
        for k in range(8):
            c = weights[pl.ds(k, 1), :]
            s = weights[pl.ds(8 + k, 1), :]
            if im[k] is None:
                real, imag = re[k] * c, -re[k] * s
            else:
                real, imag = re[k] * c + im[k] * s, im[k] * c - re[k] * s
            left[pl.ds(k, 16, stride=8), :] = jnp.where(low_lanes, real, pltpu.roll(imag, 64, 1))
        high, low = halves(left[...])
        contract = (((1,), (1,)), ((), ()))
        along = lax.dot_general(
            jnp.concatenate([first, first], axis=1),
            jnp.concatenate([high, low], axis=1),
            contract,
            preferred_element_type=jnp.float32,
        )
        for b in range(count_z):
            sent_z[b] = along[32 * b : 32 * b + 32, :]
        z_copies = []
        for p in range(1, count_z):
            there = shifted_z(p)
            copy = pltpu.make_async_remote_copy(
                src_ref=sent_z.at[there],
                dst_ref=got_z.at[mz],
                send_sem=z_send.at[p],
                recv_sem=z_recv.at[p],
                device_id=(mx, there),
                device_id_type=MESH,
            )
            copy.start()
            z_copies.append(copy)
        got_z[mz] = sent_z[mz]
        second_high, second_low = halves(weights[pl.ds(144, 128), :])
        second_twice = jnp.concatenate([second_high, second_high], axis=0)
        for copy in x_copies:
            copy.wait_send()
        for copy in z_copies:
            copy.wait_recv()
        lines = got_z[...].reshape(128, 128).T
        high, low = halves(lines)
        result = jnp.dot(
            jnp.concatenate([high, low], axis=1), second_twice, preferred_element_type=jnp.float32
        ) + jnp.dot(high, second_low, preferred_element_type=jnp.float32)
        out_ref[0] = result[:, :64].reshape(16, 8, 64)
        out_ref[1] = result[:, 64:].reshape(16, 8, 64)
        for copy in z_copies:
            copy.wait_send()


def shards(populations, fluid_mask):
    number, extent_x, extent_z, height = populations.shape
    count_x, count_z = lax.axis_size("gx"), lax.axis_size("gz")
    full_x, full_z = count_x * extent_x, count_z * extent_z
    norm_scale = 1.0 / (math.sqrt(full_x * full_z) * SPEED_UNIT)
    spectral = (count_x, count_z, extent_x, extent_z, height) == (8, 4, 4, 16, 128)
    if spectral:
        table = jnp.asarray(tables(count_x, count_z, extent_x, extent_z, norm_scale))
    else:
        table = jnp.zeros((8, 128), jnp.float32)
    f32 = jnp.float32
    padded = (extent_x + 2, extent_z + 2 * TOP, height)
    dma = pltpu.SemaphoreType.DMA
    scratch = [
        pltpu.VMEM((extent_x, 19, extent_z, height), f32),
        pltpu.VMEM((extent_x, extent_z, height), jnp.int32),
        pltpu.VMEM((19,) + padded, f32),
        pltpu.VMEM((19, extent_x) + padded[1:], f32),
        pltpu.VMEM((3,) + padded, f32),
        pltpu.VMEM((2, extent_x, 26, height), f32),
        pltpu.VMEM((2, extent_x, 26, height), f32),
        pltpu.VMEM((4, 8, height), f32),
        pltpu.VMEM((4, 8, height), f32),
        pltpu.VMEM((2, extent_z, height), f32),
        pltpu.VMEM((extent_x, extent_z, height), f32),
        pltpu.VMEM((extent_x, extent_z, height), f32),
        pltpu.VMEM((extent_x, extent_z, height), f32),
        pltpu.VMEM((extent_x, extent_z, height), f32),
        dma((extent_x + 1,)),
        dma((2, 8)),
        dma((2, 8)),
        dma((2,)),
        dma((2,)),
    ]
    if spectral:
        scratch += [
            pltpu.VMEM((8, 16, 128), f32),
            pltpu.VMEM((8, 16, 128), f32),
            pltpu.VMEM((128, 128), f32),
            pltpu.VMEM((4, 32, 128), f32),
            pltpu.VMEM((4, 32, 128), f32),
            pltpu.VMEM(table.shape, f32),
            dma((1,)),
            dma((8,)),
            dma((8,)),
            dma((4,)),
            dma((4,)),
        ]
        out_shape = jax.ShapeDtypeStruct((2, 16, 8, 64), f32)
    else:
        out_shape = jax.ShapeDtypeStruct((extent_x, extent_z, height), f32)
    in_hbm = pl.BlockSpec(memory_space=pltpu.HBM)
    result = pl.pallas_call(
        functools.partial(kernel, spectral),
        out_shape=out_shape,
        in_specs=[in_hbm] * 3,
        out_specs=pl.BlockSpec(memory_space=pltpu.VMEM),
        scratch_shapes=scratch,
        compiler_params=pltpu.CompilerParams(
            collective_id=0, has_side_effects=True, vmem_limit_bytes=32 * 1024 * 1024
        ),
    )(*(pltpu.with_memory_space_constraint(array, pltpu.HBM) for array in (populations, fluid_mask, table)))
    if spectral:
        return result
    return spectrum(result, norm_scale)


def dft_tables(length, factor):
    index = jnp.arange(length, dtype=jnp.int32)
    products = index[:, None] * index[None, :] % length
    angles = products.astype(jnp.float32) * (2.0 * math.pi / length)
    return (jnp.cos(angles) * factor, jnp.sin(angles) * factor)


def spectrum(speed_x, norm_scale):
    columns = jnp.transpose(speed_x, (2, 1, 0))
    highest = lax.Precision.HIGHEST
    block = lax.all_to_all(columns, "gx", split_axis=0, concat_axis=2, tiled=True)
    cosine, sine = dft_tables(block.shape[2], norm_scale)
    real_part = jnp.einsum("yzx,xk->yzk", block, cosine, precision=highest)
    imag_part = -jnp.einsum("yzx,xk->yzk", block, sine, precision=highest)
    along_kx = jnp.stack([real_part, imag_part], axis=0)
    block = lax.all_to_all(along_kx, "gz", split_axis=3, concat_axis=2, tiled=True)
    cosine, sine = dft_tables(block.shape[2], 1.0)
    real_in = block[0]
    imag_in = block[1]
    real_part = jnp.einsum("ync,nk->yck", real_in, cosine, precision=highest) + jnp.einsum(
        "ync,nk->yck", imag_in, sine, precision=highest
    )
    imag_part = jnp.einsum("ync,nk->yck", imag_in, cosine, precision=highest) - jnp.einsum(
        "ync,nk->yck", real_in, sine, precision=highest
    )
    return jnp.stack([real_part, imag_part], axis=0)


def solution(mesh):
    placed = (P(None, "gx", "gz", None), P("gx", "gz", None))
    return jax.shard_map(
        shards, mesh=mesh, in_specs=placed, out_specs=P(None, "gx", "gz", None), check_vma=False
    )
```

```python
import functools
import math

import jax
import jax.numpy as jnp
import numpy as np
from jax import lax
from jax.experimental import pallas as pl
from jax.experimental.pallas import tpu as pltpu
from jax.sharding import PartitionSpec as P

VELOCITIES = (
    (0, 0, 0),
    (1, 0, 0),
    (-1, 0, 0),
    (0, 1, 0),
    (0, -1, 0),
    (0, 0, 1),
    (0, 0, -1),
    (1, 1, 0),
    (-1, -1, 0),
    (1, -1, 0),
    (-1, 1, 0),
    (1, 0, 1),
    (-1, 0, -1),
    (1, 0, -1),
    (-1, 0, 1),
    (0, 1, 1),
    (0, -1, -1),
    (0, 1, -1),
    (0, -1, 1),
)
LATTICE_WEIGHTS = (1.0 / 3.0,) + (1.0 / 18.0,) * 6 + (1.0 / 36.0,) * 12
OPPOSITES = (0, 2, 1, 4, 3, 6, 5, 8, 7, 10, 9, 12, 11, 14, 13, 16, 15, 18, 17)
RELAX_TIME = 0.6
BODY_FORCE = 0.0001
SPEED_UNIT = 0.05

CHAIN = (13, 1, 7, 9, 11, 5, 15, 18, 14, 2, 8, 10, 12, 6, 16, 17, 0, 3, 4)
SLOT = {number: CHAIN.index(number) for number in CHAIN}
X_FIRST = {1: 0, -1: 8}
Z_FIRST = {1: 4, -1: 12}
SIDES = ((1, 0), (-1, 0), (0, 1), (0, -1))
DIAGONALS = ((1, 1), (1, -1), (-1, 1), (-1, -1))
DIAGONAL_SLOT = (4, 0, 8, 12)
TOP = 8
MESH = pl.DeviceIdType.MESH


def collide(f, fluid):
    omega = 1.0 / RELAX_TIME
    keep = 1.0 - omega
    plus = {}
    minus = {}
    for i in range(1, 19, 2):
        plus[i] = f[i] + f[i + 1]
        minus[i] = f[i] - f[i + 1]
    density = f[0]
    momentum = [None, None, None]
    for i in range(1, 19, 2):
        density = density + plus[i]
        for axis in range(3):
            c = VELOCITIES[i][axis]
            if c:
                term = minus[i] if c > 0 else -minus[i]
                momentum[axis] = term if momentum[axis] is None else momentum[axis] + term
    inverse = 1.0 / density
    jx, jy, jz = momentum
    square = (jx * jx + jy * jy + jz * jz) * inverse
    base = density - 1.5 * square
    force = density * BODY_FORCE
    out = [None] * 19
    w0 = LATTICE_WEIGHTS[0] * omega
    out[0] = jnp.where(fluid, keep * f[0] + w0 * base, f[0])
    for i in range(1, 19, 2):
        w = LATTICE_WEIGHTS[i]
        cj = None
        for axis in range(3):
            c = VELOCITIES[i][axis]
            if c:
                j = momentum[axis]
                if cj is None:
                    cj = j if c > 0 else -j
                else:
                    cj = cj + j if c > 0 else cj - j
        even = (w * omega) * (base + 4.5 * (cj * cj * inverse))
        odd = (3.0 * w * omega) * cj
        if VELOCITIES[i][0]:
            odd = odd + (3.0 * w * VELOCITIES[i][0]) * force
        out[i] = jnp.where(fluid, keep * f[i] + (even + odd), f[i])
        out[i + 1] = jnp.where(fluid, keep * f[i + 1] + (even - odd), f[i + 1])
    return out


def tables(count_x, count_z, extent_x, extent_z, norm):
    lane = np.arange(128)
    step = (lane // extent_z) % extent_x
    k0 = np.arange(8)[:, None]
    angle = 2.0 * np.pi * k0 * step[None, :] / (count_x * extent_x)
    twiddle = np.concatenate([np.cos(angle), np.sin(angle)], axis=0)
    quarter_cos = np.array([1.0, 0.0, -1.0, 0.0])
    quarter_sin = np.array([0.0, 1.0, 0.0, -1.0])
    k1 = np.arange(4)[:, None]
    xl = np.arange(4)[None, :]
    c = quarter_cos[(k1 * xl) % 4]
    s = quarter_sin[(k1 * xl) % 4]
    block = np.zeros((4, 2, 2, 4))
    block[:, 0, 0] = c
    block[:, 0, 1] = s
    block[:, 1, 1] = c
    block[:, 1, 0] = -s
    first = np.einsum("kpqx,zw->kpzqxw", block, np.eye(extent_z)).reshape(128, 128)
    full_z = count_z * extent_z
    z = np.arange(full_z)
    angle = 2.0 * np.pi * ((z[:, None] * z[None, :]) % full_z) / full_z
    c = np.cos(angle) * norm
    s = np.sin(angle) * norm
    second = np.zeros((2, full_z, 2, full_z))
    second[0, :, 0] = c
    second[1, :, 0] = s
    second[1, :, 1] = c
    second[0, :, 1] = -s
    second = second.reshape(2, count_z, extent_z, 2, full_z).transpose(1, 0, 2, 3, 4)
    second = second.reshape(128, 128)
    return np.concatenate([twiddle, first, second], axis=0).astype(np.float32)


def halves(value):
    high = value.astype(jnp.bfloat16)
    low = (value - high.astype(jnp.float32)).astype(jnp.bfloat16)
    return high, low


def eight_point(v):
    r = math.sqrt(0.5)
    a0, a1, a2, a3 = v[0] + v[4], v[1] + v[5], v[2] + v[6], v[3] + v[7]
    b0, b1, b2, b3 = v[0] - v[4], v[1] - v[5], v[2] - v[6], v[3] - v[7]
    e0, e1 = a0 + a2, a1 + a3
    d, t = r * (b1 - b3), r * (b1 + b3)
    re = [e0 + e1, b0 + d, a0 - a2, b0 - d, e0 - e1]
    im = [None, -b2 - t, a3 - a1, b2 - t, None]
    re = re + [re[3], re[2], re[1]]
    im = im + [-im[3], -im[2], -im[1]]
    return re, im


def kernel(spectral, populations, fluid_mask, table, *rest):
    (out_ref, held, mask_i, rolled, plain, walls, edges_out, edges_in, corners_out, corners_in,
     sums_in, density, forward, ahead, behind,
     in_sem, halo_send, halo_recv, mask_send, mask_recv) = rest[:20]
    if spectral:
        (sent_x, got_x, left, sent_z, got_z, weights,
         table_sem, x_send, x_recv, z_send, z_recv) = rest[20:]
    extent_x, extent_z, height = fluid_mask.shape
    last = extent_x - 1
    count_x, count_z = lax.axis_size("gx"), lax.axis_size("gz")
    mx, mz = lax.axis_index("gx"), lax.axis_index("gz")

    def shifted_x(step):
        return lax.rem(mx + step + count_x, count_x)

    def shifted_z(step):
        return lax.rem(mz + step + count_z, count_z)

    inner = pl.ds(TOP, extent_z)

    def fetch(x):
        return pltpu.make_async_copy(populations.at[:, x], held.at[x], in_sem.at[x])

    barrier = pltpu.get_barrier_semaphore()
    partners = [(shifted_x(dx), shifted_z(dz)) for dx, dz in SIDES + DIAGONALS]
    if spectral:
        partners += [(shifted_x(p), mz) for p in range(2, count_x - 1)]
        partners += [(mx, shifted_z(p)) for p in range(2, count_z - 1)]
    for partner in partners:
        pl.semaphore_signal(barrier, inc=1, device_id=partner, device_id_type=MESH)
    mask_copy = pltpu.make_async_copy(fluid_mask, mask_i, in_sem.at[extent_x])
    mask_copy.start()
    for k in range(extent_x):
        fetch((extent_x - k) % extent_x).start()
    if spectral:
        table_copy = pltpu.make_async_copy(table, weights, table_sem.at[0])
        table_copy.start()

    wide = extent_z + 2
    lanes = lax.broadcasted_iota(jnp.int32, (wide, height), 1)

    def edge_rows(cz):
        if cz > 0:
            return pl.ds(TOP + extent_z - 1, 1), pl.ds(TOP + extent_z - 2, 1)
        return pl.ds(TOP, 1), pl.ds(TOP + 1, 1)

    def halo_rows(cz):
        if cz > 0:
            return pl.ds(TOP - 1, 1), pl.ds(TOP - 2, 1)
        return pl.ds(TOP + extent_z, 1), pl.ds(TOP + extent_z + 1, 1)

    def remote(source, target, send_sem, recv_sem, dx, dz):
        return pltpu.make_async_remote_copy(
            src_ref=source,
            dst_ref=target,
            send_sem=send_sem,
            recv_sem=recv_sem,
            device_id=(shifted_x(dx), shifted_z(dz)),
            device_id_type=MESH,
        )

    def send(*arguments):
        copy = remote(*arguments)
        copy.start()
        return copy

    x_sides, x_masks = [], []
    for side, dx in enumerate((1, -1)):
        here, there = (extent_x, 0) if dx > 0 else (1, extent_x + 1)
        group = pl.ds(X_FIRST[dx], 5)
        x_sides.append(
            remote(rolled.at[group, here, inner], rolled.at[group, there, inner],
                   halo_send.at[0, side], halo_recv.at[0, side], dx, 0)
        )
        x_masks.append(
            remote(walls.at[0, here, inner], walls.at[0, there, inner],
                   mask_send.at[side], mask_recv.at[side], dx, 0)
        )

    def send_along_x():
        odd = lax.rem(mx, 2)
        for up in (odd, 1 - odd):
            here, there = 1 + up * last, (1 - up) * (extent_x + 1)
            side, start = 1 - up, X_FIRST[-1] * (1 - up)
            target = (shifted_x(2 * up - 1), mz)
            pltpu.make_async_remote_copy(
                src_ref=rolled.at[pl.ds(start, 5), here, inner],
                dst_ref=rolled.at[pl.ds(start, 5), there, inner],
                send_sem=halo_send.at[0, side],
                recv_sem=halo_recv.at[0, side],
                device_id=target,
                device_id_type=MESH,
            ).start()
            pltpu.make_async_remote_copy(
                src_ref=walls.at[0, here, inner],
                dst_ref=walls.at[0, there, inner],
                send_sem=mask_send.at[side],
                recv_sem=mask_recv.at[side],
                device_id=target,
                device_id_type=MESH,
            ).start()

    mask_copy.wait()
    for x in range(extent_x):
        walls[0, 1 + x, inner, :] = mask_i[x].astype(jnp.float32)

    def first_collision(k, carry):
        x = lax.rem(extent_x - k, extent_x)
        fetch(x).wait()
        g = collide([held[x, number] for number in range(19)], walls[0, 1 + x, inner, :] > 0)
        for number in range(19):
            cy = VELOCITIES[number][1]
            value = g[number]
            if cy:
                plain[number, x, inner, :] = value
                value = pltpu.roll(value, cy % height, 1)
            rolled[SLOT[number], 1 + x, inner, :] = value

        @pl.when(k == 1)
        def _():
            pl.semaphore_wait(barrier, len(partners))
            send_along_x()

        return carry

    lax.fori_loop(0, extent_x, first_collision, 0)
    z_sides, corners = [], []

    def pack(x, carry):
        for side, cz in enumerate((1, -1)):
            edge, beside = edge_rows(cz)
            for number in range(19):
                if VELOCITIES[number][1]:
                    value = plain[number, x, edge, :]
                else:
                    value = rolled[SLOT[number], 1 + x, edge, :]
                edges_out[side, x, pl.ds(number, 1), :] = value
            for order in range(5):
                edges_out[side, x, pl.ds(19 + order, 1), :] = rolled[
                    (Z_FIRST[cz] + order) % 16, 1 + x, beside, :
                ]
            edges_out[side, x, pl.ds(24, 1), :] = walls[0, 1 + x, edge, :]
            edges_out[side, x, pl.ds(25, 1), :] = walls[0, 1 + x, beside, :]
        return carry

    lax.fori_loop(0, extent_x, pack, 0)
    for side, cz in enumerate((1, -1)):
        z_sides.append(
            send(edges_out.at[side], edges_in.at[side],
                 halo_send.at[0, 2 + side], halo_recv.at[0, 2 + side], 0, cz)
        )
    for diagonal, (dx, dz) in enumerate(DIAGONALS):
        edge, beside = edge_rows(dz)
        plane = extent_x if dx > 0 else 1
        for order in range(5):
            corners_out[diagonal, pl.ds(order, 1), :] = rolled[X_FIRST[dx] + order, plane, edge, :]
        corners_out[diagonal, pl.ds(5, 1), :] = rolled[DIAGONAL_SLOT[diagonal], plane, beside, :]
        corners_out[diagonal, pl.ds(6, 1), :] = walls[0, plane, edge, :]
        corners_out[diagonal, pl.ds(7, 1), :] = walls[0, plane, beside, :]
        corners.append(
            send(corners_out.at[diagonal], corners_in.at[diagonal],
                 halo_send.at[0, 4 + diagonal], halo_recv.at[0, 4 + diagonal], dx, dz)
        )

    around = lax.broadcasted_iota(jnp.int32, (extent_z + 2 * TOP, height), 1)

    def shift_walls(plane):
        value = walls[0, plane]
        walls[1, plane] = jnp.where(around == 0, 0.0, pltpu.roll(value, 1, 1))
        walls[2, plane] = jnp.where(around == height - 1, 0.0, pltpu.roll(value, height - 1, 1))

    def wall_from(number, x):
        cx, cy, cz = VELOCITIES[number]
        return walls[(0, 1, 2)[cy], 1 + x - cx, pl.ds(TOP - 1 - cz, wide), :] > 0

    def second_collision(k, carry):
        x = lax.rem(k + 1, extent_x)

        @pl.when(k == extent_x - 2)
        def _():
            for copy in x_masks + x_sides + corners:
                copy.wait_recv()
            for diagonal, (cx, cz) in enumerate(DIAGONALS):
                beside, further = halo_rows(cz)
                plane = 0 if cx > 0 else extent_x + 1
                for order in range(5):
                    rolled[X_FIRST[cx] + order, plane, beside, :] = corners_in[diagonal, pl.ds(order, 1), :]
                rolled[DIAGONAL_SLOT[diagonal], plane, further, :] = corners_in[diagonal, pl.ds(5, 1), :]
                walls[0, plane, beside, :] = corners_in[diagonal, pl.ds(6, 1), :]
                walls[0, plane, further, :] = corners_in[diagonal, pl.ds(7, 1), :]
            for plane in (0, extent_x + 1):
                shift_walls(plane)

        region = pl.ds(TOP - 1, wide)
        fluid = walls[0, 1 + x, region, :] > 0
        owned = []
        for number in range(19):
            if VELOCITIES[number][1]:
                owned.append(plain[number, x, region, :])
            else:
                owned.append(rolled[SLOT[number], 1 + x, region, :])
        f = [owned[0]]
        for number in range(1, 19):
            cx, cy, cz = VELOCITIES[number]
            value = rolled[SLOT[number], 1 + x - cx, pl.ds(TOP - 1 - cz, wide), :]
            arrived = jnp.where(wall_from(number, x), value, owned[OPPOSITES[number]])
            f.append(jnp.where(fluid, arrived, owned[number]))
        g = collide(f, fluid)
        leaving = {}
        turned_back = {}
        for number in range(1, 19):
            cx, cy, cz = VELOCITIES[number]
            value = jnp.where(fluid, g[number], 0.0)
            if cy:
                value = pltpu.roll(value, cy % height, 1)
                value = jnp.where(lanes == (0 if cy > 0 else height - 1), 0.0, value)
            leaving[cx, cz] = leaving[cx, cz] + value if (cx, cz) in leaving else value
            value = jnp.where(wall_from(number, x), 0.0, g[OPPOSITES[number]])
            turned_back[cx] = turned_back[cx] + value if cx in turned_back else value
        stay = slice(1, 1 + extent_z)
        leaving[0, 0] = leaving[0, 0] + g[0] + (turned_back[0] + turned_back[1] + turned_back[-1])
        for cx, keep in ((1, ahead), (-1, behind), (0, density)):
            keep[x] = leaving[cx, 0][stay] + leaving[cx, 1][:extent_z] + leaving[cx, -1][2:]
        forward[x] = (turned_back[1] - turned_back[-1])[stay]
        return carry

    for copy in z_sides:
        copy.wait_recv()
    def unpack(x, carry):
        for side, cz in enumerate((1, -1)):
            beside, further = halo_rows(cz)
            for number in range(19):
                value = edges_in[side, x, pl.ds(number, 1), :]
                cy = VELOCITIES[number][1]
                if cy:
                    plain[number, x, beside, :] = value
                    value = pltpu.roll(value, cy % height, 1)
                rolled[SLOT[number], 1 + x, beside, :] = value
            for order in range(5):
                rolled[(Z_FIRST[cz] + order) % 16, 1 + x, further, :] = edges_in[
                    side, x, pl.ds(19 + order, 1), :
                ]
            walls[0, 1 + x, beside, :] = edges_in[side, x, pl.ds(24, 1), :]
            walls[0, 1 + x, further, :] = edges_in[side, x, pl.ds(25, 1), :]
        return carry

    lax.fori_loop(0, extent_x, unpack, 0)

    def shift_inner(plane, carry):
        shift_walls(plane)
        return carry

    lax.fori_loop(1, 1 + extent_x, shift_inner, 0)
    lax.fori_loop(0, extent_x, second_collision, 0)

    for x in range(extent_x):
        total, along = density[x], forward[x]
        if x > 0:
            total, along = total + ahead[x - 1], along + ahead[x - 1]
        if x < last:
            total, along = total + behind[x + 1], along - behind[x + 1]
        density[x] = total
        forward[x] = along

    halo_copies = x_sides + x_masks + z_sides + corners

    def is_fluid(plane):
        return walls[0, plane, inner, :] > 0

    if not spectral:
        sums = []
        for side, (dx, x, keep) in enumerate(((1, last, ahead), (-1, 0, behind))):
            sums.append(
                send(keep.at[x], sums_in.at[side],
                     halo_send.at[1, 2 + side], halo_recv.at[1, 2 + side], dx, 0)
            )
        for copy in sums:
            copy.wait_recv()
        for x in range(extent_x):
            total, along = density[x], forward[x]
            if x == 0:
                total, along = total + sums_in[0], along + sums_in[0]
            if x == last:
                total, along = total + sums_in[1], along - sums_in[1]
            out_ref[x] = jnp.where(is_fluid(1 + x), along / total, 0.0)
        for copy in halo_copies + sums:
            copy.wait_send()

    if spectral:
        parts = []
        for x in range(extent_x):
            if x in (0, last):
                parts.append(jnp.where(is_fluid(1 + x), density[x], 1.0))
            else:
                parts.append(jnp.where(is_fluid(1 + x), forward[x] / density[x], 0.0))
        parts.append(jnp.where(is_fluid(1), forward[0], 0.0))
        parts.append(jnp.where(is_fluid(extent_x + 1), ahead[last], 0.0))
        parts.append(jnp.where(is_fluid(0), behind[0], 0.0))
        parts.append(jnp.where(is_fluid(extent_x), forward[last], 0.0))
        sent_x[...] = jnp.concatenate(parts, axis=0).T.reshape(8, 16, 128)
        x_copies = []
        lower = jnp.where(mx < count_x // 2, 1, 0)
        for order in range(count_x - 1):
            down = count_x - 1 - order
            down = down - jnp.where(down <= mx, 1, 0)
            up = order + jnp.where(order >= mx, 1, 0)
            there = lower * down + (1 - lower) * up
            copy = pltpu.make_async_remote_copy(
                src_ref=sent_x.at[there],
                dst_ref=got_x.at[mx],
                send_sem=x_send.at[order],
                recv_sem=x_recv.at[mx],
                device_id=(there, mz),
                device_id_type=MESH,
            )
            copy.start()
            x_copies.append(copy)
        got_x[mx] = sent_x[mx]
        table_copy.wait()
        first = weights[pl.ds(16, 128), :].astype(jnp.bfloat16)
        for copy in halo_copies:
            copy.wait_send()
        for p in range(1, count_x):
            source = shifted_x(p)
            pltpu.make_async_remote_copy(
                src_ref=sent_x.at[source],
                dst_ref=got_x.at[source],
                send_sem=x_send.at[0],
                recv_sem=x_recv.at[source],
                device_id=(source, mz),
                device_id_type=MESH,
            ).wait_recv()
        lane = lax.broadcasted_iota(jnp.int32, (16, 128), 1)
        head, tail = lane < 16, lane >= 48
        got = [got_x[s] for s in range(8)]
        speeds = []
        for s in range(8):
            forth = pltpu.roll(got[(s - 1) % 8], 128 - 80, 1)
            back = pltpu.roll(got[(s + 1) % 8], 128 - 48, 1)
            mine = pltpu.roll(got[s], 64, 1)
            total = got[s] + jnp.where(head, forth, back)
            along = mine + jnp.where(head, forth, -back)
            speeds.append(jnp.where(head | tail, along / total, got[s]))
        re, im = eight_point(speeds)
        low_lanes = lane < 64
        for k in range(8):
            c = weights[pl.ds(k, 1), :]
            s = weights[pl.ds(8 + k, 1), :]
            if im[k] is None:
                real, imag = re[k] * c, -re[k] * s
            else:
                real, imag = re[k] * c + im[k] * s, im[k] * c - re[k] * s
            left[pl.ds(k, 16, stride=8), :] = jnp.where(low_lanes, real, pltpu.roll(imag, 64, 1))
        high, low = halves(left[...])
        contract = (((1,), (1,)), ((), ()))
        along = lax.dot_general(
            jnp.concatenate([first, first], axis=1),
            jnp.concatenate([high, low], axis=1),
            contract,
            preferred_element_type=jnp.float32,
        )
        for b in range(count_z):
            sent_z[b] = along[32 * b : 32 * b + 32, :]
        z_copies = []
        for p in range(1, count_z):
            there = shifted_z(p)
            copy = pltpu.make_async_remote_copy(
                src_ref=sent_z.at[there],
                dst_ref=got_z.at[mz],
                send_sem=z_send.at[p],
                recv_sem=z_recv.at[p],
                device_id=(mx, there),
                device_id_type=MESH,
            )
            copy.start()
            z_copies.append(copy)
        got_z[mz] = sent_z[mz]
        second_high, second_low = halves(weights[pl.ds(144, 128), :])
        second_twice = jnp.concatenate([second_high, second_high], axis=0)
        for copy in x_copies:
            copy.wait_send()
        for copy in z_copies:
            copy.wait_recv()
        lines = got_z[...].reshape(128, 128).T
        high, low = halves(lines)
        result = jnp.dot(
            jnp.concatenate([high, low], axis=1), second_twice, preferred_element_type=jnp.float32
        ) + jnp.dot(high, second_low, preferred_element_type=jnp.float32)
        out_ref[0] = result[:, :64].reshape(16, 8, 64)
        out_ref[1] = result[:, 64:].reshape(16, 8, 64)
        for copy in z_copies:
            copy.wait_send()


def shards(populations, fluid_mask):
    number, extent_x, extent_z, height = populations.shape
    count_x, count_z = lax.axis_size("gx"), lax.axis_size("gz")
    full_x, full_z = count_x * extent_x, count_z * extent_z
    norm_scale = 1.0 / (math.sqrt(full_x * full_z) * SPEED_UNIT)
    spectral = (count_x, count_z, extent_x, extent_z, height) == (8, 4, 4, 16, 128)
    if spectral:
        table = jnp.asarray(tables(count_x, count_z, extent_x, extent_z, norm_scale))
    else:
        table = jnp.zeros((8, 128), jnp.float32)
    f32 = jnp.float32
    padded = (extent_x + 2, extent_z + 2 * TOP, height)
    dma = pltpu.SemaphoreType.DMA
    scratch = [
        pltpu.VMEM((extent_x, 19, extent_z, height), f32),
        pltpu.VMEM((extent_x, extent_z, height), jnp.int32),
        pltpu.VMEM((19,) + padded, f32),
        pltpu.VMEM((19, extent_x) + padded[1:], f32),
        pltpu.VMEM((3,) + padded, f32),
        pltpu.VMEM((2, extent_x, 26, height), f32),
        pltpu.VMEM((2, extent_x, 26, height), f32),
        pltpu.VMEM((4, 8, height), f32),
        pltpu.VMEM((4, 8, height), f32),
        pltpu.VMEM((2, extent_z, height), f32),
        pltpu.VMEM((extent_x, extent_z, height), f32),
        pltpu.VMEM((extent_x, extent_z, height), f32),
        pltpu.VMEM((extent_x, extent_z, height), f32),
        pltpu.VMEM((extent_x, extent_z, height), f32),
        dma((extent_x + 1,)),
        dma((2, 8)),
        dma((2, 8)),
        dma((2,)),
        dma((2,)),
    ]
    if spectral:
        scratch += [
            pltpu.VMEM((8, 16, 128), f32),
            pltpu.VMEM((8, 16, 128), f32),
            pltpu.VMEM((128, 128), f32),
            pltpu.VMEM((4, 32, 128), f32),
            pltpu.VMEM((4, 32, 128), f32),
            pltpu.VMEM(table.shape, f32),
            dma((1,)),
            dma((8,)),
            dma((8,)),
            dma((4,)),
            dma((4,)),
        ]
        out_shape = jax.ShapeDtypeStruct((2, 16, 8, 64), f32)
    else:
        out_shape = jax.ShapeDtypeStruct((extent_x, extent_z, height), f32)
    in_hbm = pl.BlockSpec(memory_space=pltpu.HBM)
    result = pl.pallas_call(
        functools.partial(kernel, spectral),
        out_shape=out_shape,
        in_specs=[in_hbm] * 3,
        out_specs=pl.BlockSpec(memory_space=pltpu.VMEM),
        scratch_shapes=scratch,
        compiler_params=pltpu.CompilerParams(
            collective_id=0, has_side_effects=True, vmem_limit_bytes=32 * 1024 * 1024
        ),
    )(*(pltpu.with_memory_space_constraint(array, pltpu.HBM) for array in (populations, fluid_mask, table)))
    if spectral:
        return result
    return spectrum(result, norm_scale)


def dft_tables(length, factor):
    index = jnp.arange(length, dtype=jnp.int32)
    products = index[:, None] * index[None, :] % length
    angles = products.astype(jnp.float32) * (2.0 * math.pi / length)
    return (jnp.cos(angles) * factor, jnp.sin(angles) * factor)


def spectrum(speed_x, norm_scale):
    columns = jnp.transpose(speed_x, (2, 1, 0))
    highest = lax.Precision.HIGHEST
    block = lax.all_to_all(columns, "gx", split_axis=0, concat_axis=2, tiled=True)
    cosine, sine = dft_tables(block.shape[2], norm_scale)
    real_part = jnp.einsum("yzx,xk->yzk", block, cosine, precision=highest)
    imag_part = -jnp.einsum("yzx,xk->yzk", block, sine, precision=highest)
    along_kx = jnp.stack([real_part, imag_part], axis=0)
    block = lax.all_to_all(along_kx, "gz", split_axis=3, concat_axis=2, tiled=True)
    cosine, sine = dft_tables(block.shape[2], 1.0)
    real_in = block[0]
    imag_in = block[1]
    real_part = jnp.einsum("ync,nk->yck", real_in, cosine, precision=highest) + jnp.einsum(
        "ync,nk->yck", imag_in, sine, precision=highest
    )
    imag_part = jnp.einsum("ync,nk->yck", imag_in, cosine, precision=highest) - jnp.einsum(
        "ync,nk->yck", real_in, sine, precision=highest
    )
    return jnp.stack([real_part, imag_part], axis=0)


def solution(mesh):
    placed = (P(None, "gx", "gz", None), P("gx", "gz", None))
    return jax.shard_map(
        shards, mesh=mesh, in_specs=placed, out_specs=P(None, "gx", "gz", None), check_vma=False
    )
```

```python
import functools
import math

import jax
import jax.numpy as jnp
import numpy as np
from jax import lax
from jax.experimental import pallas as pl
from jax.experimental.pallas import tpu as pltpu
from jax.sharding import PartitionSpec as P

VELOCITIES = (
    (0, 0, 0),
    (1, 0, 0),
    (-1, 0, 0),
    (0, 1, 0),
    (0, -1, 0),
    (0, 0, 1),
    (0, 0, -1),
    (1, 1, 0),
    (-1, -1, 0),
    (1, -1, 0),
    (-1, 1, 0),
    (1, 0, 1),
    (-1, 0, -1),
    (1, 0, -1),
    (-1, 0, 1),
    (0, 1, 1),
    (0, -1, -1),
    (0, 1, -1),
    (0, -1, 1),
)
LATTICE_WEIGHTS = (1.0 / 3.0,) + (1.0 / 18.0,) * 6 + (1.0 / 36.0,) * 12
OPPOSITES = (0, 2, 1, 4, 3, 6, 5, 8, 7, 10, 9, 12, 11, 14, 13, 16, 15, 18, 17)
RELAX_TIME = 0.6
BODY_FORCE = 0.0001
SPEED_UNIT = 0.05

X_GROUP = {1: (13, 1, 7, 9, 11), -1: (14, 2, 8, 10, 12)}
Z_GROUP = {1: (11, 5, 15, 18, 14), -1: (12, 6, 16, 17, 13)}
CHAIN = (-1,) + X_GROUP[1] + (5, 15, 18, 6, 16, 17, 0, 3, 4) + X_GROUP[-1] + (-1,)
SLOT = {number: CHAIN.index(number) for number in range(19)}
X_FIRST = {1: 0, -1: len(CHAIN) - 6}
SOLIDITY = {1: 0, -1: len(CHAIN) - 1}
SIDES = ((1, 0), (-1, 0), (0, 1), (0, -1))
DIAGONALS = ((1, 1), (1, -1), (-1, 1), (-1, -1))
DIAGONAL_MOVER = (11, 13, 14, 12)
TOP = 8
MESH = pl.DeviceIdType.MESH


def collide(f, fluid):
    omega = 1.0 / RELAX_TIME
    keep = 1.0 - omega
    plus = {}
    minus = {}
    for i in range(1, 19, 2):
        plus[i] = f[i] + f[i + 1]
        minus[i] = f[i] - f[i + 1]
    density = f[0]
    momentum = [None, None, None]
    for i in range(1, 19, 2):
        density = density + plus[i]
        for axis in range(3):
            c = VELOCITIES[i][axis]
            if c:
                term = minus[i] if c > 0 else -minus[i]
                momentum[axis] = term if momentum[axis] is None else momentum[axis] + term
    inverse = 1.0 / density
    jx, jy, jz = momentum
    square = (jx * jx + jy * jy + jz * jz) * inverse
    base = density - 1.5 * square
    force = density * BODY_FORCE
    out = [None] * 19
    w0 = LATTICE_WEIGHTS[0] * omega
    out[0] = jnp.where(fluid, keep * f[0] + w0 * base, f[0])
    for i in range(1, 19, 2):
        w = LATTICE_WEIGHTS[i]
        cj = None
        for axis in range(3):
            c = VELOCITIES[i][axis]
            if c:
                j = momentum[axis]
                if cj is None:
                    cj = j if c > 0 else -j
                else:
                    cj = cj + j if c > 0 else cj - j
        even = (w * omega) * (base + 4.5 * (cj * cj * inverse))
        odd = (3.0 * w * omega) * cj
        if VELOCITIES[i][0]:
            odd = odd + (3.0 * w * VELOCITIES[i][0]) * force
        out[i] = jnp.where(fluid, keep * f[i] + (even + odd), f[i])
        out[i + 1] = jnp.where(fluid, keep * f[i + 1] + (even - odd), f[i + 1])
    return out


def tables(count_x, count_z, extent_x, extent_z, norm):
    lane = np.arange(128)
    step = (lane // extent_z) % extent_x
    k0 = np.arange(8)[:, None]
    angle = 2.0 * np.pi * k0 * step[None, :] / (count_x * extent_x)
    twiddle = np.concatenate([np.cos(angle), np.sin(angle)], axis=0)
    quarter_cos = np.array([1.0, 0.0, -1.0, 0.0])
    quarter_sin = np.array([0.0, 1.0, 0.0, -1.0])
    k1 = np.arange(4)[:, None]
    xl = np.arange(4)[None, :]
    c = quarter_cos[(k1 * xl) % 4]
    s = quarter_sin[(k1 * xl) % 4]
    block = np.zeros((4, 2, 2, 4))
    block[:, 0, 0] = c
    block[:, 0, 1] = s
    block[:, 1, 1] = c
    block[:, 1, 0] = -s
    first = np.einsum("kpqx,zw->kpzqxw", block, np.eye(extent_z)).reshape(128, 128)
    full_z = count_z * extent_z
    z = np.arange(full_z)
    angle = 2.0 * np.pi * ((z[:, None] * z[None, :]) % full_z) / full_z
    c = np.cos(angle) * norm
    s = np.sin(angle) * norm
    second = np.zeros((2, full_z, 2, full_z))
    second[0, :, 0] = c
    second[1, :, 0] = s
    second[1, :, 1] = c
    second[0, :, 1] = -s
    second = second.reshape(2, count_z, extent_z, 2, full_z).transpose(1, 0, 2, 3, 4)
    second = second.reshape(128, 128)
    return np.concatenate([twiddle, first, second], axis=0).astype(np.float32)


def halves(value):
    high = value.astype(jnp.bfloat16)
    low = (value - high.astype(jnp.float32)).astype(jnp.bfloat16)
    return high, low


def eight_point(v):
    r = math.sqrt(0.5)
    a0, a1, a2, a3 = v[0] + v[4], v[1] + v[5], v[2] + v[6], v[3] + v[7]
    b0, b1, b2, b3 = v[0] - v[4], v[1] - v[5], v[2] - v[6], v[3] - v[7]
    e0, e1 = a0 + a2, a1 + a3
    d, t = r * (b1 - b3), r * (b1 + b3)
    re = [e0 + e1, b0 + d, a0 - a2, b0 - d, e0 - e1]
    im = [None, -b2 - t, a3 - a1, b2 - t, None]
    re = re + [re[3], re[2], re[1]]
    im = im + [-im[3], -im[2], -im[1]]
    return re, im


def kernel(spectral, populations, fluid_mask, table, *rest):
    (out_ref, held, mask_i, rolled, plain, walls, edges_out, edges_in, corners_out, corners_in,
     sums_in, density, forward, ahead, behind,
     in_sem, halo_send, halo_recv) = rest[:18]
    if spectral:
        (sent_x, got_x, left, sent_z, got_z, weights,
         table_sem, x_send, x_recv, z_send, z_recv) = rest[18:]
    extent_x, extent_z, height = fluid_mask.shape
    last = extent_x - 1
    count_x, count_z = lax.axis_size("gx"), lax.axis_size("gz")
    mx, mz = lax.axis_index("gx"), lax.axis_index("gz")

    def shifted_x(step):
        return lax.rem(mx + step + count_x, count_x)

    def shifted_z(step):
        return lax.rem(mz + step + count_z, count_z)

    inner = pl.ds(TOP, extent_z)

    def fetch(x):
        return pltpu.make_async_copy(populations.at[:, x], held.at[x], in_sem.at[x])

    mask_copy = pltpu.make_async_copy(fluid_mask, mask_i, in_sem.at[extent_x])
    mask_copy.start()
    for k in range(extent_x):
        fetch((extent_x - k) % extent_x).start()

    barrier = pltpu.get_barrier_semaphore()
    partners = [(shifted_x(dx), shifted_z(dz)) for dx, dz in SIDES + DIAGONALS]
    if spectral:
        partners += [(shifted_x(p), mz) for p in range(2, count_x - 1)]
        partners += [(mx, shifted_z(p)) for p in range(2, count_z - 1)]
    for partner in partners:
        pl.semaphore_signal(barrier, inc=1, device_id=partner, device_id_type=MESH)
    if spectral:
        table_copy = pltpu.make_async_copy(table, weights, table_sem.at[0])
        table_copy.start()

    wide = extent_z + 2
    lanes = lax.broadcasted_iota(jnp.int32, (wide, height), 1)

    def edge_rows(cz):
        if cz > 0:
            return pl.ds(TOP + extent_z - 1, 1), pl.ds(TOP + extent_z - 2, 1)
        return pl.ds(TOP, 1), pl.ds(TOP + 1, 1)

    def halo_rows(cz):
        if cz > 0:
            return pl.ds(TOP - 1, 1), pl.ds(TOP - 2, 1)
        return pl.ds(TOP + extent_z, 1), pl.ds(TOP + extent_z + 1, 1)

    def remote(source, target, send_sem, recv_sem, dx, dz):
        return pltpu.make_async_remote_copy(
            src_ref=source,
            dst_ref=target,
            send_sem=send_sem,
            recv_sem=recv_sem,
            device_id=(shifted_x(dx), shifted_z(dz)),
            device_id_type=MESH,
        )

    def send(*arguments):
        copy = remote(*arguments)
        copy.start()
        return copy

    x_sides = []
    for side, dx in enumerate((1, -1)):
        here, there = (extent_x, 0) if dx > 0 else (1, extent_x + 1)
        group = pl.ds(X_FIRST[dx], 6)
        x_sides.append(
            remote(rolled.at[group, here, inner], rolled.at[group, there, inner],
                   halo_send.at[0, side], halo_recv.at[0, side], dx, 0)
        )

    def send_along_x():
        odd = lax.rem(mx, 2)
        for up in (odd, 1 - odd):
            group = pl.ds(X_FIRST[-1] * (1 - up), 6)
            pltpu.make_async_remote_copy(
                src_ref=rolled.at[group, 1 + up * last, inner],
                dst_ref=rolled.at[group, (1 - up) * (extent_x + 1), inner],
                send_sem=halo_send.at[0, 1 - up],
                recv_sem=halo_recv.at[0, 1 - up],
                device_id=(shifted_x(2 * up - 1), mz),
                device_id_type=MESH,
            ).start()

    mask_copy.wait()
    for x in range(extent_x):
        solid = mask_i[x].astype(jnp.float32)
        walls[0, 1 + x, inner, :] = solid
        if x == last:
            rolled[SOLIDITY[1], 1 + x, inner, :] = solid
        if x == 0:
            rolled[SOLIDITY[-1], 1 + x, inner, :] = solid

    def first_collision(k, carry):
        x = lax.rem(extent_x - k, extent_x)
        fetch(x).wait()
        g = collide([held[x, number] for number in range(19)], walls[0, 1 + x, inner, :] > 0)
        for number in range(19):
            cy = VELOCITIES[number][1]
            value = g[number]
            if cy:
                plain[number, x, inner, :] = value
                value = pltpu.roll(value, cy % height, 1)
            rolled[SLOT[number], 1 + x, inner, :] = value

        @pl.when(k == 1)
        def _():
            pl.semaphore_wait(barrier, len(partners))
            send_along_x()

        return carry

    lax.fori_loop(0, extent_x, first_collision, 0)
    z_sides, corners = [], []

    def pack(x, carry):
        for side, cz in enumerate((1, -1)):
            edge, beside = edge_rows(cz)
            for number in range(19):
                if VELOCITIES[number][1]:
                    value = plain[number, x, edge, :]
                else:
                    value = rolled[SLOT[number], 1 + x, edge, :]
                edges_out[side, x, pl.ds(number, 1), :] = value
            for order in range(5):
                edges_out[side, x, pl.ds(19 + order, 1), :] = rolled[
                    SLOT[Z_GROUP[cz][order]], 1 + x, beside, :
                ]
            edges_out[side, x, pl.ds(24, 1), :] = walls[0, 1 + x, edge, :]
            edges_out[side, x, pl.ds(25, 1), :] = walls[0, 1 + x, beside, :]
        return carry

    lax.fori_loop(0, extent_x, pack, 0)
    for side, cz in enumerate((1, -1)):
        z_sides.append(
            send(edges_out.at[side], edges_in.at[side],
                 halo_send.at[0, 2 + side], halo_recv.at[0, 2 + side], 0, cz)
        )
    for diagonal, (dx, dz) in enumerate(DIAGONALS):
        edge, beside = edge_rows(dz)
        plane = extent_x if dx > 0 else 1
        for order in range(5):
            corners_out[diagonal, pl.ds(order, 1), :] = rolled[SLOT[X_GROUP[dx][order]], plane, edge, :]
        corners_out[diagonal, pl.ds(5, 1), :] = rolled[SLOT[DIAGONAL_MOVER[diagonal]], plane, beside, :]
        corners_out[diagonal, pl.ds(6, 1), :] = walls[0, plane, edge, :]
        corners_out[diagonal, pl.ds(7, 1), :] = walls[0, plane, beside, :]
        corners.append(
            send(corners_out.at[diagonal], corners_in.at[diagonal],
                 halo_send.at[0, 4 + diagonal], halo_recv.at[0, 4 + diagonal], dx, dz)
        )

    around = lax.broadcasted_iota(jnp.int32, (extent_z + 2 * TOP, height), 1)

    def shift_walls(plane):
        value = walls[0, plane]
        walls[1, plane] = jnp.where(around == 0, 0.0, pltpu.roll(value, 1, 1))
        walls[2, plane] = jnp.where(around == height - 1, 0.0, pltpu.roll(value, height - 1, 1))

    def wall_from(number, x):
        cx, cy, cz = VELOCITIES[number]
        return walls[(0, 1, 2)[cy], 1 + x - cx, pl.ds(TOP - 1 - cz, wide), :] > 0

    def second_collision(k, carry):
        x = lax.rem(k + 1, extent_x)

        @pl.when(k == extent_x - 2)
        def _():
            for copy in x_sides + corners:
                copy.wait_recv()
            for cx, plane in ((1, 0), (-1, extent_x + 1)):
                walls[0, plane, inner, :] = rolled[SOLIDITY[cx], plane, inner, :]
            for diagonal, (cx, cz) in enumerate(DIAGONALS):
                beside, further = halo_rows(cz)
                plane = 0 if cx > 0 else extent_x + 1
                for order in range(5):
                    rolled[SLOT[X_GROUP[cx][order]], plane, beside, :] = corners_in[diagonal, pl.ds(order, 1), :]
                rolled[SLOT[DIAGONAL_MOVER[diagonal]], plane, further, :] = corners_in[diagonal, pl.ds(5, 1), :]
                walls[0, plane, beside, :] = corners_in[diagonal, pl.ds(6, 1), :]
                walls[0, plane, further, :] = corners_in[diagonal, pl.ds(7, 1), :]
            for plane in (0, extent_x + 1):
                shift_walls(plane)

        region = pl.ds(TOP - 1, wide)
        fluid = walls[0, 1 + x, region, :] > 0
        owned = []
        for number in range(19):
            if VELOCITIES[number][1]:
                owned.append(plain[number, x, region, :])
            else:
                owned.append(rolled[SLOT[number], 1 + x, region, :])
        f = [owned[0]]
        for number in range(1, 19):
            cx, cy, cz = VELOCITIES[number]
            value = rolled[SLOT[number], 1 + x - cx, pl.ds(TOP - 1 - cz, wide), :]
            arrived = jnp.where(wall_from(number, x), value, owned[OPPOSITES[number]])
            f.append(jnp.where(fluid, arrived, owned[number]))
        g = collide(f, fluid)
        leaving = {}
        turned_back = {}
        for number in range(1, 19):
            cx, cy, cz = VELOCITIES[number]
            value = jnp.where(fluid, g[number], 0.0)
            if cy:
                value = pltpu.roll(value, cy % height, 1)
                value = jnp.where(lanes == (0 if cy > 0 else height - 1), 0.0, value)
            leaving[cx, cz] = leaving[cx, cz] + value if (cx, cz) in leaving else value
            value = jnp.where(wall_from(number, x), 0.0, g[OPPOSITES[number]])
            turned_back[cx] = turned_back[cx] + value if cx in turned_back else value
        stay = slice(1, 1 + extent_z)
        leaving[0, 0] = leaving[0, 0] + g[0] + (turned_back[0] + turned_back[1] + turned_back[-1])
        for cx, keep in ((1, ahead), (-1, behind), (0, density)):
            keep[x] = leaving[cx, 0][stay] + leaving[cx, 1][:extent_z] + leaving[cx, -1][2:]
        forward[x] = (turned_back[1] - turned_back[-1])[stay]
        return carry

    for copy in z_sides:
        copy.wait_recv()
    def unpack(x, carry):
        for side, cz in enumerate((1, -1)):
            beside, further = halo_rows(cz)
            for number in range(19):
                value = edges_in[side, x, pl.ds(number, 1), :]
                cy = VELOCITIES[number][1]
                if cy:
                    plain[number, x, beside, :] = value
                    value = pltpu.roll(value, cy % height, 1)
                rolled[SLOT[number], 1 + x, beside, :] = value
            for order in range(5):
                rolled[SLOT[Z_GROUP[cz][order]], 1 + x, further, :] = edges_in[
                    side, x, pl.ds(19 + order, 1), :
                ]
            walls[0, 1 + x, beside, :] = edges_in[side, x, pl.ds(24, 1), :]
            walls[0, 1 + x, further, :] = edges_in[side, x, pl.ds(25, 1), :]
        return carry

    lax.fori_loop(0, extent_x, unpack, 0)

    def shift_inner(plane, carry):
        shift_walls(plane)
        return carry

    lax.fori_loop(1, 1 + extent_x, shift_inner, 0)
    lax.fori_loop(0, extent_x, second_collision, 0)

    for x in range(extent_x):
        total, along = density[x], forward[x]
        if x > 0:
            total, along = total + ahead[x - 1], along + ahead[x - 1]
        if x < last:
            total, along = total + behind[x + 1], along - behind[x + 1]
        density[x] = total
        forward[x] = along

    halo_copies = x_sides + z_sides + corners

    def is_fluid(plane):
        return walls[0, plane, inner, :] > 0

    if not spectral:
        sums = []
        for side, (dx, x, keep) in enumerate(((1, last, ahead), (-1, 0, behind))):
            sums.append(
                send(keep.at[x], sums_in.at[side],
                     halo_send.at[1, 2 + side], halo_recv.at[1, 2 + side], dx, 0)
            )
        for copy in sums:
            copy.wait_recv()
        for x in range(extent_x):
            total, along = density[x], forward[x]
            if x == 0:
                total, along = total + sums_in[0], along + sums_in[0]
            if x == last:
                total, along = total + sums_in[1], along - sums_in[1]
            out_ref[x] = jnp.where(is_fluid(1 + x), along / total, 0.0)
        for copy in halo_copies + sums:
            copy.wait_send()

    if spectral:
        parts = []
        for x in range(extent_x):
            if x in (0, last):
                parts.append(jnp.where(is_fluid(1 + x), density[x], 1.0))
            else:
                parts.append(jnp.where(is_fluid(1 + x), forward[x] / density[x], 0.0))
        parts.append(jnp.where(is_fluid(1), forward[0], 0.0))
        parts.append(jnp.where(is_fluid(extent_x + 1), ahead[last], 0.0))
        parts.append(jnp.where(is_fluid(0), behind[0], 0.0))
        parts.append(jnp.where(is_fluid(extent_x), forward[last], 0.0))
        sent_x[...] = jnp.concatenate(parts, axis=0).T.reshape(8, 16, 128)
        x_copies = []
        for p in range(1, count_x):
            there = shifted_x(p)
            copy = pltpu.make_async_remote_copy(
                src_ref=sent_x.at[there],
                dst_ref=got_x.at[mx],
                send_sem=x_send.at[p],
                recv_sem=x_recv.at[p],
                device_id=(there, mz),
                device_id_type=MESH,
            )
            copy.start()
            x_copies.append(copy)
        got_x[mx] = sent_x[mx]
        table_copy.wait()
        first = weights[pl.ds(16, 128), :].astype(jnp.bfloat16)
        for copy in halo_copies:
            copy.wait_send()
        for copy in x_copies:
            copy.wait_recv()
        lane = lax.broadcasted_iota(jnp.int32, (16, 128), 1)
        head, tail = lane < 16, lane >= 48
        got = [got_x[s] for s in range(8)]
        speeds = []
        for s in range(8):
            forth = pltpu.roll(got[(s - 1) % 8], 128 - 80, 1)
            back = pltpu.roll(got[(s + 1) % 8], 128 - 48, 1)
            mine = pltpu.roll(got[s], 64, 1)
            total = got[s] + jnp.where(head, forth, back)
            along = mine + jnp.where(head, forth, -back)
            speeds.append(jnp.where(head | tail, along / total, got[s]))
        re, im = eight_point(speeds)
        low_lanes = lane < 64
        for k in range(8):
            c = weights[pl.ds(k, 1), :]
            s = weights[pl.ds(8 + k, 1), :]
            if im[k] is None:
                real, imag = re[k] * c, -re[k] * s
            else:
                real, imag = re[k] * c + im[k] * s, im[k] * c - re[k] * s
            left[pl.ds(k, 16, stride=8), :] = jnp.where(low_lanes, real, pltpu.roll(imag, 64, 1))
        high, low = halves(left[...])
        contract = (((1,), (1,)), ((), ()))
        along = lax.dot_general(
            jnp.concatenate([first, first], axis=1),
            jnp.concatenate([high, low], axis=1),
            contract,
            preferred_element_type=jnp.float32,
        )
        for b in range(count_z):
            sent_z[b] = along[32 * b : 32 * b + 32, :]
        z_copies = []
        for p in range(1, count_z):
            there = shifted_z(p)
            copy = pltpu.make_async_remote_copy(
                src_ref=sent_z.at[there],
                dst_ref=got_z.at[mz],
                send_sem=z_send.at[p],
                recv_sem=z_recv.at[p],
                device_id=(mx, there),
                device_id_type=MESH,
            )
            copy.start()
            z_copies.append(copy)
        got_z[mz] = sent_z[mz]
        second_high, second_low = halves(weights[pl.ds(144, 128), :])
        second_twice = jnp.concatenate([second_high, second_high], axis=0)
        for copy in x_copies:
            copy.wait_send()
        for copy in z_copies:
            copy.wait_recv()
        lines = got_z[...].reshape(128, 128).T
        high, low = halves(lines)
        result = jnp.dot(
            jnp.concatenate([high, low], axis=1), second_twice, preferred_element_type=jnp.float32
        ) + jnp.dot(high, second_low, preferred_element_type=jnp.float32)
        out_ref[0] = result[:, :64].reshape(16, 8, 64)
        out_ref[1] = result[:, 64:].reshape(16, 8, 64)
        for copy in z_copies:
            copy.wait_send()


def shards(populations, fluid_mask):
    number, extent_x, extent_z, height = populations.shape
    count_x, count_z = lax.axis_size("gx"), lax.axis_size("gz")
    full_x, full_z = count_x * extent_x, count_z * extent_z
    norm_scale = 1.0 / (math.sqrt(full_x * full_z) * SPEED_UNIT)
    spectral = (count_x, count_z, extent_x, extent_z, height) == (8, 4, 4, 16, 128)
    if spectral:
        table = jnp.asarray(tables(count_x, count_z, extent_x, extent_z, norm_scale))
    else:
        table = jnp.zeros((8, 128), jnp.float32)
    f32 = jnp.float32
    padded = (extent_x + 2, extent_z + 2 * TOP, height)
    dma = pltpu.SemaphoreType.DMA
    scratch = [
        pltpu.VMEM((extent_x, 19, extent_z, height), f32),
        pltpu.VMEM((extent_x, extent_z, height), jnp.int32),
        pltpu.VMEM((len(CHAIN),) + padded, f32),
        pltpu.VMEM((19, extent_x) + padded[1:], f32),
        pltpu.VMEM((3,) + padded, f32),
        pltpu.VMEM((2, extent_x, 26, height), f32),
        pltpu.VMEM((2, extent_x, 26, height), f32),
        pltpu.VMEM((4, 8, height), f32),
        pltpu.VMEM((4, 8, height), f32),
        pltpu.VMEM((2, extent_z, height), f32),
        pltpu.VMEM((extent_x, extent_z, height), f32),
        pltpu.VMEM((extent_x, extent_z, height), f32),
        pltpu.VMEM((extent_x, extent_z, height), f32),
        pltpu.VMEM((extent_x, extent_z, height), f32),
        dma((extent_x + 1,)),
        dma((2, 8)),
        dma((2, 8)),
    ]
    if spectral:
        scratch += [
            pltpu.VMEM((8, 16, 128), f32),
            pltpu.VMEM((8, 16, 128), f32),
            pltpu.VMEM((128, 128), f32),
            pltpu.VMEM((4, 32, 128), f32),
            pltpu.VMEM((4, 32, 128), f32),
            pltpu.VMEM(table.shape, f32),
            dma((1,)),
            dma((8,)),
            dma((8,)),
            dma((4,)),
            dma((4,)),
        ]
        out_shape = jax.ShapeDtypeStruct((2, 16, 8, 64), f32)
    else:
        out_shape = jax.ShapeDtypeStruct((extent_x, extent_z, height), f32)
    in_hbm = pl.BlockSpec(memory_space=pltpu.HBM)
    result = pl.pallas_call(
        functools.partial(kernel, spectral),
        out_shape=out_shape,
        in_specs=[in_hbm] * 3,
        out_specs=pl.BlockSpec(memory_space=pltpu.VMEM),
        scratch_shapes=scratch,
        compiler_params=pltpu.CompilerParams(
            collective_id=0, has_side_effects=True, vmem_limit_bytes=32 * 1024 * 1024
        ),
    )(*(pltpu.with_memory_space_constraint(array, pltpu.HBM) for array in (populations, fluid_mask, table)))
    if spectral:
        return result
    return spectrum(result, norm_scale)


def dft_tables(length, factor):
    index = jnp.arange(length, dtype=jnp.int32)
    products = index[:, None] * index[None, :] % length
    angles = products.astype(jnp.float32) * (2.0 * math.pi / length)
    return (jnp.cos(angles) * factor, jnp.sin(angles) * factor)


def spectrum(speed_x, norm_scale):
    columns = jnp.transpose(speed_x, (2, 1, 0))
    highest = lax.Precision.HIGHEST
    block = lax.all_to_all(columns, "gx", split_axis=0, concat_axis=2, tiled=True)
    cosine, sine = dft_tables(block.shape[2], norm_scale)
    real_part = jnp.einsum("yzx,xk->yzk", block, cosine, precision=highest)
    imag_part = -jnp.einsum("yzx,xk->yzk", block, sine, precision=highest)
    along_kx = jnp.stack([real_part, imag_part], axis=0)
    block = lax.all_to_all(along_kx, "gz", split_axis=3, concat_axis=2, tiled=True)
    cosine, sine = dft_tables(block.shape[2], 1.0)
    real_in = block[0]
    imag_in = block[1]
    real_part = jnp.einsum("ync,nk->yck", real_in, cosine, precision=highest) + jnp.einsum(
        "ync,nk->yck", imag_in, sine, precision=highest
    )
    imag_part = jnp.einsum("ync,nk->yck", imag_in, cosine, precision=highest) - jnp.einsum(
        "ync,nk->yck", real_in, sine, precision=highest
    )
    return jnp.stack([real_part, imag_part], axis=0)


def solution(mesh):
    placed = (P(None, "gx", "gz", None), P("gx", "gz", None))
    return jax.shard_map(
        shards, mesh=mesh, in_specs=placed, out_specs=P(None, "gx", "gz", None), check_vma=False
    )
```

```python
import functools
import math

import jax
import jax.numpy as jnp
import numpy as np
from jax import lax
from jax.experimental import pallas as pl
from jax.experimental.pallas import tpu as pltpu
from jax.sharding import PartitionSpec as P

VELOCITIES = (
    (0, 0, 0),
    (1, 0, 0),
    (-1, 0, 0),
    (0, 1, 0),
    (0, -1, 0),
    (0, 0, 1),
    (0, 0, -1),
    (1, 1, 0),
    (-1, -1, 0),
    (1, -1, 0),
    (-1, 1, 0),
    (1, 0, 1),
    (-1, 0, -1),
    (1, 0, -1),
    (-1, 0, 1),
    (0, 1, 1),
    (0, -1, -1),
    (0, 1, -1),
    (0, -1, 1),
)
LATTICE_WEIGHTS = (1.0 / 3.0,) + (1.0 / 18.0,) * 6 + (1.0 / 36.0,) * 12
OPPOSITES = (0, 2, 1, 4, 3, 6, 5, 8, 7, 10, 9, 12, 11, 14, 13, 16, 15, 18, 17)
RELAX_TIME = 0.6
BODY_FORCE = 0.0001
SPEED_UNIT = 0.05

X_GROUP = {1: (13, 1, 7, 9, 11), -1: (14, 2, 8, 10, 12)}
Z_GROUP = {1: (11, 5, 15, 18, 14), -1: (12, 6, 16, 17, 13)}
CHAIN = (-1,) + X_GROUP[1] + (5, 15, 18, 6, 16, 17, 0, 3, 4) + X_GROUP[-1] + (-1,)
SLOT = {number: CHAIN.index(number) for number in range(19)}
X_FIRST = {1: 0, -1: len(CHAIN) - 6}
SOLIDITY = {1: 0, -1: len(CHAIN) - 1}
SIDES = ((1, 0), (-1, 0), (0, 1), (0, -1))
DIAGONALS = ((1, 1), (1, -1), (-1, 1), (-1, -1))
DIAGONAL_MOVER = (11, 13, 14, 12)
TOP = 8
MESH = pl.DeviceIdType.MESH


def collide(f, fluid):
    omega = 1.0 / RELAX_TIME
    keep = 1.0 - omega
    plus = {}
    minus = {}
    for i in range(1, 19, 2):
        plus[i] = f[i] + f[i + 1]
        minus[i] = f[i] - f[i + 1]
    density = f[0]
    momentum = [None, None, None]
    for i in range(1, 19, 2):
        density = density + plus[i]
        for axis in range(3):
            c = VELOCITIES[i][axis]
            if c:
                term = minus[i] if c > 0 else -minus[i]
                momentum[axis] = term if momentum[axis] is None else momentum[axis] + term
    inverse = 1.0 / density
    jx, jy, jz = momentum
    square = (jx * jx + jy * jy + jz * jz) * inverse
    base = density - 1.5 * square
    force = density * BODY_FORCE
    out = [None] * 19
    w0 = LATTICE_WEIGHTS[0] * omega
    out[0] = jnp.where(fluid, keep * f[0] + w0 * base, f[0])
    for i in range(1, 19, 2):
        w = LATTICE_WEIGHTS[i]
        cj = None
        for axis in range(3):
            c = VELOCITIES[i][axis]
            if c:
                j = momentum[axis]
                if cj is None:
                    cj = j if c > 0 else -j
                else:
                    cj = cj + j if c > 0 else cj - j
        even = (w * omega) * (base + 4.5 * (cj * cj * inverse))
        odd = (3.0 * w * omega) * cj
        if VELOCITIES[i][0]:
            odd = odd + (3.0 * w * VELOCITIES[i][0]) * force
        out[i] = jnp.where(fluid, keep * f[i] + (even + odd), f[i])
        out[i + 1] = jnp.where(fluid, keep * f[i + 1] + (even - odd), f[i + 1])
    return out


def tables(count_x, count_z, extent_x, extent_z, norm):
    lane = np.arange(128)
    step = (lane // extent_z) % extent_x
    k0 = np.arange(8)[:, None]
    angle = 2.0 * np.pi * k0 * step[None, :] / (count_x * extent_x)
    twiddle = np.concatenate([np.cos(angle), np.sin(angle)], axis=0)
    quarter_cos = np.array([1.0, 0.0, -1.0, 0.0])
    quarter_sin = np.array([0.0, 1.0, 0.0, -1.0])
    k1 = np.arange(4)[:, None]
    xl = np.arange(4)[None, :]
    c = quarter_cos[(k1 * xl) % 4]
    s = quarter_sin[(k1 * xl) % 4]
    block = np.zeros((4, 2, 2, 4))
    block[:, 0, 0] = c
    block[:, 0, 1] = s
    block[:, 1, 1] = c
    block[:, 1, 0] = -s
    first = np.einsum("kpqx,zw->kpzqxw", block, np.eye(extent_z)).reshape(128, 128)
    full_z = count_z * extent_z
    z = np.arange(full_z)
    angle = 2.0 * np.pi * ((z[:, None] * z[None, :]) % full_z) / full_z
    c = np.cos(angle) * norm
    s = np.sin(angle) * norm
    second = np.zeros((2, full_z, 2, full_z))
    second[0, :, 0] = c
    second[1, :, 0] = s
    second[1, :, 1] = c
    second[0, :, 1] = -s
    second = second.reshape(2, count_z, extent_z, 2, full_z).transpose(1, 0, 2, 3, 4)
    second = second.reshape(128, 128)
    return np.concatenate([twiddle, first, second], axis=0).astype(np.float32)


def halves(value):
    high = value.astype(jnp.bfloat16)
    low = (value - high.astype(jnp.float32)).astype(jnp.bfloat16)
    return high, low


def eight_point(v):
    r = math.sqrt(0.5)
    a0, a1, a2, a3 = v[0] + v[4], v[1] + v[5], v[2] + v[6], v[3] + v[7]
    b0, b1, b2, b3 = v[0] - v[4], v[1] - v[5], v[2] - v[6], v[3] - v[7]
    e0, e1 = a0 + a2, a1 + a3
    d, t = r * (b1 - b3), r * (b1 + b3)
    re = [e0 + e1, b0 + d, a0 - a2, b0 - d, e0 - e1]
    im = [None, -b2 - t, a3 - a1, b2 - t, None]
    re = re + [re[3], re[2], re[1]]
    im = im + [-im[3], -im[2], -im[1]]
    return re, im


def kernel(spectral, populations, fluid_mask, table, *rest):
    (out_ref, held, mask_i, rolled, plain, walls, edges_out, edges_in, corners_out, corners_in,
     sums_in, density, forward, ahead, behind,
     in_sem, halo_send, halo_recv) = rest[:18]
    if spectral:
        (sent_x, got_x, left, sent_z, got_z, weights,
         table_sem, x_send, x_recv, z_send, z_recv) = rest[18:]
    extent_x, extent_z, height = fluid_mask.shape
    last = extent_x - 1
    count_x, count_z = lax.axis_size("gx"), lax.axis_size("gz")
    mx, mz = lax.axis_index("gx"), lax.axis_index("gz")

    def shifted_x(step):
        return lax.rem(mx + step + count_x, count_x)

    def shifted_z(step):
        return lax.rem(mz + step + count_z, count_z)

    inner = pl.ds(TOP, extent_z)

    def fetch(x):
        return pltpu.make_async_copy(populations.at[:, x], held.at[x], in_sem.at[x])

    mask_copy = pltpu.make_async_copy(fluid_mask, mask_i, in_sem.at[extent_x])
    mask_copy.start()
    for k in range(extent_x):
        fetch((extent_x - k) % extent_x).start()

    barrier = pltpu.get_barrier_semaphore()
    partners = [(shifted_x(dx), shifted_z(dz)) for dx, dz in SIDES + DIAGONALS]
    if spectral:
        partners += [(shifted_x(p), mz) for p in range(2, count_x - 1)]
        partners += [(mx, shifted_z(p)) for p in range(2, count_z - 1)]
    for partner in partners:
        pl.semaphore_signal(barrier, inc=1, device_id=partner, device_id_type=MESH)
    if spectral:
        table_copy = pltpu.make_async_copy(table, weights, table_sem.at[0])
        table_copy.start()

    wide = extent_z + 2
    lanes = lax.broadcasted_iota(jnp.int32, (wide, height), 1)

    def edge_rows(cz):
        if cz > 0:
            return pl.ds(TOP + extent_z - 1, 1), pl.ds(TOP + extent_z - 2, 1)
        return pl.ds(TOP, 1), pl.ds(TOP + 1, 1)

    def halo_rows(cz):
        if cz > 0:
            return pl.ds(TOP - 1, 1), pl.ds(TOP - 2, 1)
        return pl.ds(TOP + extent_z, 1), pl.ds(TOP + extent_z + 1, 1)

    def remote(source, target, send_sem, recv_sem, dx, dz):
        return pltpu.make_async_remote_copy(
            src_ref=source,
            dst_ref=target,
            send_sem=send_sem,
            recv_sem=recv_sem,
            device_id=(shifted_x(dx), shifted_z(dz)),
            device_id_type=MESH,
        )

    def send(*arguments):
        copy = remote(*arguments)
        copy.start()
        return copy

    x_sides = []
    for side, dx in enumerate((1, -1)):
        here, there = (extent_x, 0) if dx > 0 else (1, extent_x + 1)
        group = pl.ds(X_FIRST[dx], 6)
        x_sides.append(
            remote(rolled.at[group, here, inner], rolled.at[group, there, inner],
                   halo_send.at[0, side], halo_recv.at[0, side], dx, 0)
        )

    def send_along_x():
        odd = lax.rem(mx, 2)
        for up in (odd, 1 - odd):
            group = pl.ds(X_FIRST[-1] * (1 - up), 6)
            pltpu.make_async_remote_copy(
                src_ref=rolled.at[group, 1 + up * last, inner],
                dst_ref=rolled.at[group, (1 - up) * (extent_x + 1), inner],
                send_sem=halo_send.at[0, 1 - up],
                recv_sem=halo_recv.at[0, 1 - up],
                device_id=(shifted_x(2 * up - 1), mz),
                device_id_type=MESH,
            ).start()

    mask_copy.wait()
    for x in range(extent_x):
        solid = mask_i[x].astype(jnp.float32)
        walls[0, 1 + x, inner, :] = solid
        if x == last:
            rolled[SOLIDITY[1], 1 + x, inner, :] = solid
        if x == 0:
            rolled[SOLIDITY[-1], 1 + x, inner, :] = solid

    def first_collision(k, carry):
        x = lax.rem(extent_x - k, extent_x)
        fetch(x).wait()
        g = collide([held[x, number] for number in range(19)], walls[0, 1 + x, inner, :] > 0)
        for number in range(19):
            cy = VELOCITIES[number][1]
            value = g[number]
            if cy:
                plain[number, x, inner, :] = value
                value = pltpu.roll(value, cy % height, 1)
            rolled[SLOT[number], 1 + x, inner, :] = value
        return carry

    lax.fori_loop(0, extent_x, first_collision, 0)
    z_sides, corners = [], []

    def pack(x, carry):
        for side, cz in enumerate((1, -1)):
            edge, beside = edge_rows(cz)
            for number in range(19):
                if VELOCITIES[number][1]:
                    value = plain[number, x, edge, :]
                else:
                    value = rolled[SLOT[number], 1 + x, edge, :]
                edges_out[side, x, pl.ds(number, 1), :] = value
            for order in range(5):
                edges_out[side, x, pl.ds(19 + order, 1), :] = rolled[
                    SLOT[Z_GROUP[cz][order]], 1 + x, beside, :
                ]
            edges_out[side, x, pl.ds(24, 1), :] = walls[0, 1 + x, edge, :]
            edges_out[side, x, pl.ds(25, 1), :] = walls[0, 1 + x, beside, :]
        return carry

    for diagonal, (dx, dz) in enumerate(DIAGONALS):
        edge, beside = edge_rows(dz)
        plane = extent_x if dx > 0 else 1
        for order in range(5):
            corners_out[diagonal, pl.ds(order, 1), :] = rolled[SLOT[X_GROUP[dx][order]], plane, edge, :]
        corners_out[diagonal, pl.ds(5, 1), :] = rolled[SLOT[DIAGONAL_MOVER[diagonal]], plane, beside, :]
        corners_out[diagonal, pl.ds(6, 1), :] = walls[0, plane, edge, :]
        corners_out[diagonal, pl.ds(7, 1), :] = walls[0, plane, beside, :]
    lax.fori_loop(0, extent_x, pack, 0)
    pl.semaphore_wait(barrier, len(partners))
    send_along_x()
    for diagonal, (dx, dz) in enumerate(DIAGONALS):
        corners.append(
            send(corners_out.at[diagonal], corners_in.at[diagonal],
                 halo_send.at[0, 4 + diagonal], halo_recv.at[0, 4 + diagonal], dx, dz)
        )
    for side, cz in enumerate((1, -1)):
        z_sides.append(
            send(edges_out.at[side], edges_in.at[side],
                 halo_send.at[0, 2 + side], halo_recv.at[0, 2 + side], 0, cz)
        )

    around = lax.broadcasted_iota(jnp.int32, (extent_z + 2 * TOP, height), 1)

    def shift_walls(plane):
        value = walls[0, plane]
        walls[1, plane] = jnp.where(around == 0, 0.0, pltpu.roll(value, 1, 1))
        walls[2, plane] = jnp.where(around == height - 1, 0.0, pltpu.roll(value, height - 1, 1))

    def wall_from(number, x):
        cx, cy, cz = VELOCITIES[number]
        return walls[(0, 1, 2)[cy], 1 + x - cx, pl.ds(TOP - 1 - cz, wide), :] > 0

    def second_collision(k, carry):
        x = lax.rem(k + 1, extent_x)

        @pl.when(k == extent_x - 2)
        def _():
            for copy in x_sides + corners:
                copy.wait_recv()
            for cx, plane in ((1, 0), (-1, extent_x + 1)):
                walls[0, plane, inner, :] = rolled[SOLIDITY[cx], plane, inner, :]
            for diagonal, (cx, cz) in enumerate(DIAGONALS):
                beside, further = halo_rows(cz)
                plane = 0 if cx > 0 else extent_x + 1
                for order in range(5):
                    rolled[SLOT[X_GROUP[cx][order]], plane, beside, :] = corners_in[diagonal, pl.ds(order, 1), :]
                rolled[SLOT[DIAGONAL_MOVER[diagonal]], plane, further, :] = corners_in[diagonal, pl.ds(5, 1), :]
                walls[0, plane, beside, :] = corners_in[diagonal, pl.ds(6, 1), :]
                walls[0, plane, further, :] = corners_in[diagonal, pl.ds(7, 1), :]
            for plane in (0, extent_x + 1):
                shift_walls(plane)

        region = pl.ds(TOP - 1, wide)
        fluid = walls[0, 1 + x, region, :] > 0
        owned = []
        for number in range(19):
            if VELOCITIES[number][1]:
                owned.append(plain[number, x, region, :])
            else:
                owned.append(rolled[SLOT[number], 1 + x, region, :])
        f = [owned[0]]
        for number in range(1, 19):
            cx, cy, cz = VELOCITIES[number]
            value = rolled[SLOT[number], 1 + x - cx, pl.ds(TOP - 1 - cz, wide), :]
            arrived = jnp.where(wall_from(number, x), value, owned[OPPOSITES[number]])
            f.append(jnp.where(fluid, arrived, owned[number]))
        g = collide(f, fluid)
        leaving = {}
        turned_back = {}
        for number in range(1, 19):
            cx, cy, cz = VELOCITIES[number]
            value = jnp.where(fluid, g[number], 0.0)
            if cy:
                value = pltpu.roll(value, cy % height, 1)
                value = jnp.where(lanes == (0 if cy > 0 else height - 1), 0.0, value)
            leaving[cx, cz] = leaving[cx, cz] + value if (cx, cz) in leaving else value
            value = jnp.where(wall_from(number, x), 0.0, g[OPPOSITES[number]])
            turned_back[cx] = turned_back[cx] + value if cx in turned_back else value
        stay = slice(1, 1 + extent_z)
        leaving[0, 0] = leaving[0, 0] + g[0] + (turned_back[0] + turned_back[1] + turned_back[-1])
        for cx, keep in ((1, ahead), (-1, behind), (0, density)):
            keep[x] = leaving[cx, 0][stay] + leaving[cx, 1][:extent_z] + leaving[cx, -1][2:]
        forward[x] = (turned_back[1] - turned_back[-1])[stay]
        return carry

    for copy in z_sides:
        copy.wait_recv()
    def unpack(x, carry):
        for side, cz in enumerate((1, -1)):
            beside, further = halo_rows(cz)
            for number in range(19):
                value = edges_in[side, x, pl.ds(number, 1), :]
                cy = VELOCITIES[number][1]
                if cy:
                    plain[number, x, beside, :] = value
                    value = pltpu.roll(value, cy % height, 1)
                rolled[SLOT[number], 1 + x, beside, :] = value
            for order in range(5):
                rolled[SLOT[Z_GROUP[cz][order]], 1 + x, further, :] = edges_in[
                    side, x, pl.ds(19 + order, 1), :
                ]
            walls[0, 1 + x, beside, :] = edges_in[side, x, pl.ds(24, 1), :]
            walls[0, 1 + x, further, :] = edges_in[side, x, pl.ds(25, 1), :]
        return carry

    lax.fori_loop(0, extent_x, unpack, 0)

    def shift_inner(plane, carry):
        shift_walls(plane)
        return carry

    lax.fori_loop(1, 1 + extent_x, shift_inner, 0)
    lax.fori_loop(0, extent_x, second_collision, 0)

    for x in range(extent_x):
        total, along = density[x], forward[x]
        if x > 0:
            total, along = total + ahead[x - 1], along + ahead[x - 1]
        if x < last:
            total, along = total + behind[x + 1], along - behind[x + 1]
        density[x] = total
        forward[x] = along

    halo_copies = x_sides + z_sides + corners

    def is_fluid(plane):
        return walls[0, plane, inner, :] > 0

    if not spectral:
        sums = []
        for side, (dx, x, keep) in enumerate(((1, last, ahead), (-1, 0, behind))):
            sums.append(
                send(keep.at[x], sums_in.at[side],
                     halo_send.at[1, 2 + side], halo_recv.at[1, 2 + side], dx, 0)
            )
        for copy in sums:
            copy.wait_recv()
        for x in range(extent_x):
            total, along = density[x], forward[x]
            if x == 0:
                total, along = total + sums_in[0], along + sums_in[0]
            if x == last:
                total, along = total + sums_in[1], along - sums_in[1]
            out_ref[x] = jnp.where(is_fluid(1 + x), along / total, 0.0)
        for copy in halo_copies + sums:
            copy.wait_send()

    if spectral:
        parts = []
        for x in range(extent_x):
            if x in (0, last):
                parts.append(jnp.where(is_fluid(1 + x), density[x], 1.0))
            else:
                parts.append(jnp.where(is_fluid(1 + x), forward[x] / density[x], 0.0))
        parts.append(jnp.where(is_fluid(1), forward[0], 0.0))
        parts.append(jnp.where(is_fluid(extent_x + 1), ahead[last], 0.0))
        parts.append(jnp.where(is_fluid(0), behind[0], 0.0))
        parts.append(jnp.where(is_fluid(extent_x), forward[last], 0.0))
        sent_x[...] = jnp.concatenate(parts, axis=0).T.reshape(8, 16, 128)
        x_copies = []
        for p in range(1, count_x):
            there = shifted_x(p)
            copy = pltpu.make_async_remote_copy(
                src_ref=sent_x.at[there],
                dst_ref=got_x.at[mx],
                send_sem=x_send.at[p],
                recv_sem=x_recv.at[p],
                device_id=(there, mz),
                device_id_type=MESH,
            )
            copy.start()
            x_copies.append(copy)
        got_x[mx] = sent_x[mx]
        table_copy.wait()
        first = weights[pl.ds(16, 128), :].astype(jnp.bfloat16)
        for copy in halo_copies:
            copy.wait_send()
        for copy in x_copies:
            copy.wait_recv()
        lane = lax.broadcasted_iota(jnp.int32, (16, 128), 1)
        head, tail = lane < 16, lane >= 48
        got = [got_x[s] for s in range(8)]
        speeds = []
        for s in range(8):
            forth = pltpu.roll(got[(s - 1) % 8], 128 - 80, 1)
            back = pltpu.roll(got[(s + 1) % 8], 128 - 48, 1)
            mine = pltpu.roll(got[s], 64, 1)
            total = got[s] + jnp.where(head, forth, back)
            along = mine + jnp.where(head, forth, -back)
            speeds.append(jnp.where(head | tail, along / total, got[s]))
        re, im = eight_point(speeds)
        low_lanes = lane < 64
        for k in range(8):
            c = weights[pl.ds(k, 1), :]
            s = weights[pl.ds(8 + k, 1), :]
            if im[k] is None:
                real, imag = re[k] * c, -re[k] * s
            else:
                real, imag = re[k] * c + im[k] * s, im[k] * c - re[k] * s
            left[pl.ds(k, 16, stride=8), :] = jnp.where(low_lanes, real, pltpu.roll(imag, 64, 1))
        high, low = halves(left[...])
        contract = (((1,), (1,)), ((), ()))
        along = lax.dot_general(
            jnp.concatenate([first, first], axis=1),
            jnp.concatenate([high, low], axis=1),
            contract,
            preferred_element_type=jnp.float32,
        )
        for b in range(count_z):
            sent_z[b] = along[32 * b : 32 * b + 32, :]
        z_copies = []
        for p in range(1, count_z):
            there = shifted_z(p)
            copy = pltpu.make_async_remote_copy(
                src_ref=sent_z.at[there],
                dst_ref=got_z.at[mz],
                send_sem=z_send.at[p],
                recv_sem=z_recv.at[p],
                device_id=(mx, there),
                device_id_type=MESH,
            )
            copy.start()
            z_copies.append(copy)
        got_z[mz] = sent_z[mz]
        second_high, second_low = halves(weights[pl.ds(144, 128), :])
        second_twice = jnp.concatenate([second_high, second_high], axis=0)
        for copy in x_copies:
            copy.wait_send()
        for copy in z_copies:
            copy.wait_recv()
        lines = got_z[...].reshape(128, 128).T
        high, low = halves(lines)
        result = jnp.dot(
            jnp.concatenate([high, low], axis=1), second_twice, preferred_element_type=jnp.float32
        ) + jnp.dot(high, second_low, preferred_element_type=jnp.float32)
        out_ref[0] = result[:, :64].reshape(16, 8, 64)
        out_ref[1] = result[:, 64:].reshape(16, 8, 64)
        for copy in z_copies:
            copy.wait_send()


def shards(populations, fluid_mask):
    number, extent_x, extent_z, height = populations.shape
    count_x, count_z = lax.axis_size("gx"), lax.axis_size("gz")
    full_x, full_z = count_x * extent_x, count_z * extent_z
    norm_scale = 1.0 / (math.sqrt(full_x * full_z) * SPEED_UNIT)
    spectral = (count_x, count_z, extent_x, extent_z, height) == (8, 4, 4, 16, 128)
    if spectral:
        table = jnp.asarray(tables(count_x, count_z, extent_x, extent_z, norm_scale))
    else:
        table = jnp.zeros((8, 128), jnp.float32)
    f32 = jnp.float32
    padded = (extent_x + 2, extent_z + 2 * TOP, height)
    dma = pltpu.SemaphoreType.DMA
    scratch = [
        pltpu.VMEM((extent_x, 19, extent_z, height), f32),
        pltpu.VMEM((extent_x, extent_z, height), jnp.int32),
        pltpu.VMEM((len(CHAIN),) + padded, f32),
        pltpu.VMEM((19, extent_x) + padded[1:], f32),
        pltpu.VMEM((3,) + padded, f32),
        pltpu.VMEM((2, extent_x, 26, height), f32),
        pltpu.VMEM((2, extent_x, 26, height), f32),
        pltpu.VMEM((4, 8, height), f32),
        pltpu.VMEM((4, 8, height), f32),
        pltpu.VMEM((2, extent_z, height), f32),
        pltpu.VMEM((extent_x, extent_z, height), f32),
        pltpu.VMEM((extent_x, extent_z, height), f32),
        pltpu.VMEM((extent_x, extent_z, height), f32),
        pltpu.VMEM((extent_x, extent_z, height), f32),
        dma((extent_x + 1,)),
        dma((2, 8)),
        dma((2, 8)),
    ]
    if spectral:
        scratch += [
            pltpu.VMEM((8, 16, 128), f32),
            pltpu.VMEM((8, 16, 128), f32),
            pltpu.VMEM((128, 128), f32),
            pltpu.VMEM((4, 32, 128), f32),
            pltpu.VMEM((4, 32, 128), f32),
            pltpu.VMEM(table.shape, f32),
            dma((1,)),
            dma((8,)),
            dma((8,)),
            dma((4,)),
            dma((4,)),
        ]
        out_shape = jax.ShapeDtypeStruct((2, 16, 8, 64), f32)
    else:
        out_shape = jax.ShapeDtypeStruct((extent_x, extent_z, height), f32)
    in_hbm = pl.BlockSpec(memory_space=pltpu.HBM)
    result = pl.pallas_call(
        functools.partial(kernel, spectral),
        out_shape=out_shape,
        in_specs=[in_hbm] * 3,
        out_specs=pl.BlockSpec(memory_space=pltpu.VMEM),
        scratch_shapes=scratch,
        compiler_params=pltpu.CompilerParams(
            collective_id=0, has_side_effects=True, vmem_limit_bytes=32 * 1024 * 1024
        ),
    )(*(pltpu.with_memory_space_constraint(array, pltpu.HBM) for array in (populations, fluid_mask, table)))
    if spectral:
        return result
    return spectrum(result, norm_scale)


def dft_tables(length, factor):
    index = jnp.arange(length, dtype=jnp.int32)
    products = index[:, None] * index[None, :] % length
    angles = products.astype(jnp.float32) * (2.0 * math.pi / length)
    return (jnp.cos(angles) * factor, jnp.sin(angles) * factor)


def spectrum(speed_x, norm_scale):
    columns = jnp.transpose(speed_x, (2, 1, 0))
    highest = lax.Precision.HIGHEST
    block = lax.all_to_all(columns, "gx", split_axis=0, concat_axis=2, tiled=True)
    cosine, sine = dft_tables(block.shape[2], norm_scale)
    real_part = jnp.einsum("yzx,xk->yzk", block, cosine, precision=highest)
    imag_part = -jnp.einsum("yzx,xk->yzk", block, sine, precision=highest)
    along_kx = jnp.stack([real_part, imag_part], axis=0)
    block = lax.all_to_all(along_kx, "gz", split_axis=3, concat_axis=2, tiled=True)
    cosine, sine = dft_tables(block.shape[2], 1.0)
    real_in = block[0]
    imag_in = block[1]
    real_part = jnp.einsum("ync,nk->yck", real_in, cosine, precision=highest) + jnp.einsum(
        "ync,nk->yck", imag_in, sine, precision=highest
    )
    imag_part = jnp.einsum("ync,nk->yck", imag_in, cosine, precision=highest) - jnp.einsum(
        "ync,nk->yck", real_in, sine, precision=highest
    )
    return jnp.stack([real_part, imag_part], axis=0)


def solution(mesh):
    placed = (P(None, "gx", "gz", None), P("gx", "gz", None))
    return jax.shard_map(
        shards, mesh=mesh, in_specs=placed, out_specs=P(None, "gx", "gz", None), check_vma=False
    )
```
